128 devices in a mesh: dp: 2 (over x_lo), ctx: 64 (over x_hi, y, z, core).
Axes of the slice: x: 4 (x_hi: 2, x_lo: 2; x = x_hi * 2 + x_lo), y: 4, z: 4, core: 2. Of those that a mesh axis runs over, the one named last changes fastest.
Arguments:
- hidden: bfloat16 [2, 8192, 576], P('dp', 'ctx'), may hold values from -6 to 6
- positions: int32 [2, 8192], P('dp', 'ctx'), may hold values from 0 to 8191, as said below
- w_query: bfloat16 [1, 576, 576], P(None, 'dp'), may hold values from -0.25 to 0.25
- w_key: bfloat16 [1, 576, 192], P(None, 'dp'), may hold values from -0.25 to 0.25
- w_value: bfloat16 [1, 576, 192], P(None, 'dp'), may hold values from -0.25 to 0.25
- w_out: bfloat16 [1, 576, 576], P(None, 'dp'), may hold values from -3 to 3
- w_gate: bfloat16 [1, 576, 1536], P(None, 'dp'), may hold values from -0.25 to 0.25
- w_up: bfloat16 [1, 576, 1536], P(None, 'dp'), may hold values from -0.25 to 0.25
- w_down: bfloat16 [1, 1536, 576], P(None, 'dp'), may hold values from -0.15625 to 0.15625
- gain_attn: bfloat16 [1, 576], P(None, 'dp'), may hold values from 0.099609375 to 1.8984375
- gain_ffn: bfloat16 [1, 576], P(None, 'dp'), may hold values from 0.099609375 to 1.8984375
- grad_out: bfloat16 [2, 8192, 576], P('dp', 'ctx'), may hold values from -18 to 18
Outputs:
- output: bfloat16 [2, 8192, 576], P('dp', 'ctx')
- grad_hidden: float32 [2, 8192, 576], P('dp', 'ctx')
- grad_query: float32 [1, 576, 576], P(None, 'dp', 'ctx')
- grad_key: float32 [1, 576, 192], P(None, 'dp', 'ctx')
- grad_value: float32 [1, 576, 192], P(None, 'dp', 'ctx')
- grad_proj: float32 [1, 576, 576], P(None, 'dp', 'ctx')
- grad_gate: float32 [1, 576, 1536], P(None, 'dp', 'ctx')
- grad_up: float32 [1, 576, 1536], P(None, 'dp', 'ctx')
- grad_down: float32 [1, 1536, 576], P(None, 'dp', 'ctx')
- grad_gain_attn: float32 [1, 576], P(None, 'dp')
- grad_gain_ffn: float32 [1, 576], P(None, 'dp')
The draws below stay inside these ranges and needn't reach their ends.
Inputs may be any that keep to these rules, and one draw needn't show every extreme that they name: In each sequence the positions are a permutation of 0 to 8191 made of runs of 128 consecutive increasing positions, one run on each device's block.
All inputs are finite; a program needn't handle non-finite values.
Results may differ from the reference program's by a relative error of at most 0.02.
Values may be sent and summed in bfloat16 or wider, within the bound.
A program may use at most 128 MiB of HBM per device.

```python
import jax
import jax.numpy as jnp
from jax import lax

D = 576
HEADS = 9
KV_HEADS = 3
HEAD = 64
FF = 1536
LAYERS = 1
BLK = 128
SEQ_LEN = 8192
SEQS = 2
HQ = 576
KV = 192


def draw_positions(key, part):
    key = jax.random.fold_in(key, 11)
    keys = jax.random.split(key, SEQS)
    orders = jax.vmap(lambda each: jax.random.permutation(each, SEQ_LEN // BLK))(keys)
    offsets = jnp.arange(BLK, dtype=jnp.int32)
    places = orders[:, :, None].astype(jnp.int32) * BLK + offsets[None, None, :]
    return places.reshape(SEQS, SEQ_LEN)


def draw_grad_out(key, part):
    key = jax.random.fold_in(key, 23)
    count = SEQS * SEQ_LEN
    ramp = 1.0 + 2.0 * jnp.arange(count, dtype=jnp.float32) / count
    ramp = ramp.reshape(SEQS, SEQ_LEN, 1)
    noise = jnp.clip(jax.random.normal(key, (SEQS, SEQ_LEN, D), jnp.float32), -6.0, 6.0)
    return (noise * ramp).astype(jnp.bfloat16)


def shard_levels(rng, dims, cuts, smallest, high):
    def one(axis_at, blocks):
        heights = jax.random.uniform(jax.random.fold_in(jax.random.fold_in(rng, 6), axis_at), (blocks,), jnp.float32, smallest / len(cuts), high / len(cuts))
        return jnp.repeat(jnp.exp(heights), dims[axis_at] // blocks).reshape((-1,) + (1,) * (len(dims) - axis_at - 1))

    level = one(*cuts[0])
    for cut in cuts[1:]:
        level = level * one(*cut)
    return level


def scatter_about(key, shape, deviation, limit, cuts=(), kind=jnp.bfloat16):
    level = shard_levels(key, shape, cuts, -0.22, 0.18) if cuts else 1.0
    array = jax.random.normal(key, shape, jnp.float32) * deviation * level
    return jnp.minimum(jnp.maximum(array, -limit), limit).astype(kind)


def setup_inputs(seed: int = 0) -> dict:
    streams_of = jax.random.split(jax.random.key(seed), 13)
    hidden = scatter_about(streams_of[0], (SEQS, SEQ_LEN, D), 1.0, 6.0, ((0, 2), (1, 64)))
    positions = draw_positions(jax.random.fold_in(streams_of[12], 71), 0)
    w_query = scatter_about(streams_of[2], (LAYERS, D, HQ), D ** -0.5, 0.25, ((1, 2),))
    w_key = scatter_about(streams_of[3], (LAYERS, D, KV), D ** -0.5, 0.25, ((1, 2),))
    w_value = scatter_about(streams_of[4], (LAYERS, D, KV), D ** -0.5, 0.25, ((1, 2),))
    w_out = scatter_about(streams_of[5], (LAYERS, HQ, D), (HEAD // 16) ** -0.5, 3.0, ((1, 2),))
    w_gate = scatter_about(streams_of[6], (LAYERS, D, FF), D ** -0.5, 0.25, ((1, 2),))
    w_up = scatter_about(streams_of[7], (LAYERS, D, FF), D ** -0.5, 0.25, ((1, 2),))
    w_down = scatter_about(streams_of[8], (LAYERS, FF, D), FF ** -0.5, 0.15625, ((1, 2),))
    gain_attn = jnp.clip(1.0 + 0.18 * jax.random.normal(streams_of[9], (LAYERS, D), jnp.float32), 0.099609375, 1.8984375).astype(jnp.bfloat16)
    gain_ffn = jnp.clip(1.0 + 0.18 * jax.random.normal(streams_of[10], (LAYERS, D), jnp.float32), 0.099609375, 1.8984375).astype(jnp.bfloat16)
    grad_out = draw_grad_out(jax.random.fold_in(streams_of[12], 71), 0)
    return {"hidden": hidden, "positions": positions, "w_query": w_query, "w_key": w_key, "w_value": w_value, "w_out": w_out, "w_gate": w_gate, "w_up": w_up, "w_down": w_down, "gain_attn": gain_attn, "gain_ffn": gain_ffn, "grad_out": grad_out}


eps = 1e-05
rope_base = 100000.0

@jax.custom_vjp
def low(v):
    return lax.optimization_barrier(v.astype(jnp.bfloat16)).astype(jnp.float32)

@jax.custom_vjp
def low_back(v):
    return v

def low_keep(v):
    return (low(v), None)

def low_pass(kept, grad):
    return (grad,)

def back_keep(v):
    return (v, None)

def back_low(kept, grad):
    return (low(grad),)
low.defvjp(low_keep, low_pass)
low_back.defvjp(back_keep, back_low)

def precise(left, right):
    return jnp.dot(left, right, precision=lax.Precision.HIGHEST, preferred_element_type=jnp.float32)

def rope_tables(places, width):
    half = width // 2
    freqs = rope_base ** (-(jnp.arange(half, dtype=jnp.float32) * 2.0 / width))
    angles = places.astype(jnp.float32)[:, None] * freqs[None, :]
    angles = jnp.concatenate([angles, angles], axis=1)
    return (jnp.cos(angles), jnp.sin(angles))

def turned(values, cosine, sine):
    half = values.shape[-1] // 2
    swapped = jnp.concatenate([-values[..., half:], values[..., :half]], axis=-1)
    return values * cosine[:, None, :] + swapped * sine[:, None, :]

def normed(hidden, gain):
    scale = lax.rsqrt(lax.optimization_barrier(jnp.mean(hidden * hidden, axis=-1, keepdims=True)) + eps)
    return hidden * scale * gain

def layer(hidden, places, wq, wk, wv, wo, wg, wu, wd, gain_one, gain_two):
    length = hidden.shape[0]
    group = HEADS // KV_HEADS
    scale = HEAD ** (-0.5)
    normal_one = low(normed(hidden, gain_one))
    cosine, sine = rope_tables(places, HEAD)
    query = low(turned(low_back(precise(normal_one, wq)).reshape(length, HEADS, HEAD), cosine, sine))
    keys = low(turned(low_back(precise(normal_one, wk)).reshape(length, KV_HEADS, HEAD), cosine, sine))
    values = low(low_back(precise(normal_one, wv))).reshape(length, KV_HEADS, HEAD)
    block = min(512, length)
    query_blocks = query.reshape(length // block, block, KV_HEADS, group, HEAD)
    place_blocks = places.reshape(length // block, block)

    def attend(item):
        query_part, query_places = item
        scores = jnp.einsum('qgrd,kgd->grqk', query_part, keys, precision=lax.Precision.HIGHEST) * scale
        scores = low_back(scores)
        allowed = places[None, :] <= query_places[:, None]
        scores = jnp.where(allowed[None, None], scores, -1e+30)
        top = lax.optimization_barrier(jnp.max(scores, axis=-1, keepdims=True))
        weights = jnp.exp(scores - top)
        probs = low(weights / lax.optimization_barrier(jnp.sum(weights, axis=-1, keepdims=True)))
        return jnp.einsum('grqk,kgd->qgrd', probs, values, precision=lax.Precision.HIGHEST)
    attended = lax.map(jax.checkpoint(attend), (query_blocks, place_blocks))
    attended = low(low_back(attended.reshape(length, HEADS * HEAD)))
    middle = hidden + low_back(precise(attended, wo))
    normal_two = low(normed(middle, gain_two))
    gate = low_back(precise(normal_two, wg))
    upper = low_back(precise(normal_two, wu))
    inner = low(jax.nn.silu(gate) * upper)
    return middle + low_back(precise(inner, wd))

def forward(hidden, places, weights):

    def one(item):
        state, where = item
        for index in range(LAYERS):
            state = layer(state, where, *[w[index] for w in weights])
        return state
    return lax.map(one, (hidden, places))

def reference(hidden, positions, w_query, w_key, w_value, w_out, w_gate, w_up, w_down, gain_attn, gain_ffn, grad_out):
    weights = tuple((w.astype(jnp.float32) for w in (w_query, w_key, w_value, w_out, w_gate, w_up, w_down, gain_attn, gain_ffn)))

    def whole(state, *params):
        return forward(state, positions, params)
    result, pullback = jax.vjp(whole, hidden.astype(jnp.float32), *weights)
    grads = pullback(grad_out.astype(jnp.float32))
    return (result.astype(jnp.bfloat16), grads[0], grads[1], grads[2], grads[3], grads[4], grads[5], grads[6], grads[7], grads[8], grads[9])
```

```python
import functools

import jax
import jax.numpy as jnp
from jax import lax
from jax.experimental import pallas as pl
from jax.experimental.pallas import tpu as pltpu
from jax.sharding import PartitionSpec as P

HEADS = 9
KV_HEADS = 3
HEAD = 64
TOK = 128
D = 576
FF = 1536
QG = 4
KG = 16
eps = 1e-05
rope_base = 100000.0
MESH = pl.DeviceIdType.MESH
BF = jnp.bfloat16
F32 = jnp.float32
LIMIT = 56 * 1024 * 1024
VM = pl.BlockSpec(memory_space=pltpu.VMEM)
ANY = pl.BlockSpec(memory_space=pl.ANY)


def params(ident):
    return pltpu.CompilerParams(
        collective_id=ident, has_side_effects=True, vmem_limit_bytes=LIMIT
    )


def place():
    dp = lax.axis_index("dp")
    ctx = lax.axis_index("ctx")
    x_hi = ctx // 32
    plane = (ctx // 2) % 16
    core = ctx % 2
    return dp, x_hi, plane, core


def ctx_of(x_hi, plane, core):
    return x_hi * 32 + plane * 2 + core


def remote(src, dst, send, recv, device):
    return pltpu.make_async_remote_copy(
        src_ref=src,
        dst_ref=dst,
        send_sem=send,
        recv_sem=recv,
        device_id=device,
        device_id_type=MESH,
    )


def greet(devices):
    barrier = pltpu.get_barrier_semaphore()
    for device in devices:
        pl.semaphore_signal(barrier, inc=1, device_id=device, device_id_type=MESH)
    pl.semaphore_wait(barrier, len(devices))


def plane_peer(plane, offset):
    y, z = plane // 4, plane % 4
    return ((y + offset // 4) % 4) * 4 + (z + offset % 4) % 4


def plane_source(plane, offset):
    y, z = plane // 4, plane % 4
    return ((y + 4 - offset // 4) % 4) * 4 + (z + 4 - offset % 4) % 4


def weight_pieces(rows):
    if rows == 288:
        return ((0, 80), (80, 64), (144, 80), (224, 64))
    quarter = rows // 4
    return tuple((quarter * i, quarter) for i in range(4))


def weights_kernel(count, *refs):
    shards = refs[:count]
    gains = refs[count]
    fulls = refs[count + 1 : 2 * count + 1]
    gains_full = refs[2 * count + 1]
    own_sem, send, recv, send_core, recv_core = refs[2 * count + 2 :]
    dp, x_hi, plane, core = place()
    other = 1 - dp
    near = (other, ctx_of(x_hi, plane, core))
    far = (other, ctx_of(1 - x_hi, plane, core))
    sibling = (dp, ctx_of(x_hi, plane, 1 - core))
    greet([near, far, sibling])
    started = []
    locals_ = []
    for which in range(count):
        shard, full = shards[which], fulls[which]
        rows = shard.shape[0]
        pieces = weight_pieces(rows)

        def views(piece):
            off, size = pieces[piece]
            return shard.at[pl.ds(off, size)], full.at[
                pl.ds(pl.multiple_of(dp * rows, 16) + off, size)
            ]

        for role, target in ((0, near), (1, far)):
            for c in range(2):
                src, dst = views(2 * c + role)

                @pl.when(core == c)
                def _():
                    remote(src, dst, send.at[which, role], recv.at[which, role], target).start()

        own = pltpu.make_async_copy(
            shard, full.at[pl.ds(pl.multiple_of(dp * rows, 16), rows)], own_sem.at[which]
        )
        own.start()
        locals_.append(own)
    gain_copy = remote(
        gains, gains_full.at[dp], send.at[count, 0], recv.at[count, 0], near
    )
    gain_copy.start()
    own = pltpu.make_async_copy(gains, gains_full.at[dp], own_sem.at[count])
    own.start()
    locals_.append(own)
    for which in range(count):
        shard, full = shards[which], fulls[which]
        rows = shard.shape[0]
        pieces = weight_pieces(rows)
        for role, target in ((0, near), (1, far)):
            for c in range(2):
                off, size = pieces[2 * c + role]
                got = full.at[pl.ds(pl.multiple_of(other * rows, 16) + off, size)]
                src = shard.at[pl.ds(off, size)]

                @pl.when(core == c)
                def _():
                    remote(src, got, send.at[which, role], recv.at[which, role], target).wait_recv()
                    remote(
                        got, got, send_core.at[which, role], recv_core.at[which, role], sibling
                    ).start()

    for which in range(count):
        shard, full = shards[which], fulls[which]
        rows = shard.shape[0]
        pieces = weight_pieces(rows)
        for role, target in ((0, near), (1, far)):
            for c in range(2):
                off, size = pieces[2 * c + role]
                got = full.at[pl.ds(pl.multiple_of(other * rows, 16) + off, size)]
                src = shard.at[pl.ds(off, size)]
                off2, size2 = pieces[2 * (1 - c) + role]
                got2 = full.at[pl.ds(pl.multiple_of(other * rows, 16) + off2, size2)]

                @pl.when(core == c)
                def _():
                    remote(src, got, send.at[which, role], recv.at[which, role], target).wait_send()
                    remote(
                        got, got, send_core.at[which, role], recv_core.at[which, role], sibling
                    ).wait_send()
                    remote(
                        got2, got2, send_core.at[which, role], recv_core.at[which, role], sibling
                    ).wait_recv()

    gain_copy.wait()
    for own in locals_:
        own.wait()


def gather_weights(shards, gains):
    count = len(shards)
    outs = [jax.ShapeDtypeStruct((2 * s.shape[0], s.shape[1]), s.dtype) for s in shards]
    outs.append(jax.ShapeDtypeStruct((2,) + gains.shape, gains.dtype))
    return pl.pallas_call(
        functools.partial(weights_kernel, count),
        out_shape=outs,
        in_specs=[ANY] * (count + 1),
        out_specs=[ANY] * (count + 1),
        scratch_shapes=[
            pltpu.SemaphoreType.DMA((count + 1,)),
            pltpu.SemaphoreType.DMA((count + 1, 2)),
            pltpu.SemaphoreType.DMA((count + 1, 2)),
            pltpu.SemaphoreType.DMA((count, 2)),
            pltpu.SemaphoreType.DMA((count, 2)),
        ],
        compiler_params=params(0),
    )(*shards, gains)


QROWS = D + 16
KROWS = 384 + 16
CHUNK = 4


def groups():
    dp, x_hi, plane, core = place()
    mine = x_hi * 2 + core
    query_peers = []
    for o in range(1, QG):
        a = (mine + o) % QG
        query_peers.append((a, (dp, ctx_of(a // 2, plane, a % 2))))
    key_peers = []
    for o in range(1, KG):
        j = plane_peer(plane, o)
        key_peers.append((j, (dp, ctx_of(x_hi, j, core))))
    return mine, plane, query_peers, key_peers


def flip_keys(kv_all, kv_tok, j):
    for g in range(KV_HEADS):
        block = kv_all[j, pl.ds(g * 128, 128), :].astype(F32)
        kv_tok[g, pl.ds(pl.multiple_of(j * TOK, TOK), TOK), :] = block.T.astype(BF)


def masks_of(q_all, kv_all, chunk):
    lane = lax.broadcasted_iota(jnp.int32, (1, TOK), 1).astype(F32)
    q_pos = jnp.concatenate(
        [q_all[a, pl.ds(D, 16), :].astype(F32)[0:1] * TOK + lane for a in range(QG)], axis=1
    )
    rows = lax.broadcasted_iota(jnp.int32, (TOK, QG * TOK), 0).astype(F32)
    parts = []
    for b in range(CHUNK):
        start = kv_all[chunk * CHUNK + b, pl.ds(384, 16), :].astype(F32)[0:1] * TOK
        start = jnp.concatenate([start] * QG, axis=1)
        parts.append(rows <= (q_pos - start))
    return jnp.concatenate(parts, axis=0)


def head_rows(ref, h):
    first = pl.multiple_of(h * HEAD, HEAD)
    return jnp.concatenate([ref[a, pl.ds(first, HEAD), :] for a in range(QG)], axis=1)


def scores_of(q_all, kv_all, kv_tok, g, chunk, queries, zeros):
    keys = kv_tok[g, pl.ds(chunk * CHUNK * TOK, CHUNK * TOK), :]
    scores = jnp.dot(keys, jnp.concatenate([queries, zeros], axis=0), preferred_element_type=F32)
    return keys, jnp.where(masks_of(q_all, kv_all, chunk), scores, -1e30)


def forward_kernel(
    q_ref, kv_ref, o_ref, lse_ref, q_all, kv_all, kv_tok, o_buf, st_buf, o_got, st_got,
    q_send, q_recv, kv_send, kv_recv, o_send, o_recv, st_send, st_recv, own_sem,
):
    mine, plane, query_peers, key_peers = groups()
    greet([d for _, d in query_peers] + [d for _, d in key_peers])
    copies = []
    for o in range(1, QG):
        copies.append(
            remote(q_ref, q_all.at[mine], q_send.at[o], q_recv.at[o], query_peers[o - 1][1])
        )
    for o in range(1, KG):
        copies.append(
            remote(kv_ref, kv_all.at[plane], kv_send.at[o], kv_recv.at[o], key_peers[o - 1][1])
        )
    for c in copies:
        c.start()
    own_q = pltpu.make_async_copy(q_ref, q_all.at[mine], own_sem.at[0])
    own_kv = pltpu.make_async_copy(kv_ref, kv_all.at[plane], own_sem.at[1])
    own_q.start()
    own_kv.start()
    own_q.wait()
    own_kv.wait()
    for c in copies:
        c.wait_recv()

    def flip(j, unused):
        flip_keys(kv_all, kv_tok, j)
        return unused

    lax.fori_loop(0, KG, flip, 0)
    zeros = jnp.zeros((HEAD, QG * TOK), BF)
    o_copies = []
    for g in range(KV_HEADS):

        def one(r, unused, g=g):
            h = g * 3 + r
            queries = head_rows(q_all, h)
            top = jnp.full((1, QG * TOK), -1e30, F32)
            total = jnp.zeros((1, QG * TOK), F32)
            accum = jnp.zeros((HEAD, QG * TOK), F32)
            for chunk in range(KG // CHUNK):
                keys, scores = scores_of(q_all, kv_all, kv_tok, g, chunk, queries, zeros)
                new_top = jnp.maximum(top, jnp.max(scores, axis=0, keepdims=True))
                probs = jnp.exp(scores - new_top)
                fade = jnp.exp(top - new_top)
                total = total * fade + jnp.sum(probs, axis=0, keepdims=True)
                values = jnp.concatenate(
                    [
                        kv_all[chunk * CHUNK + b, pl.ds(g * 128 + HEAD, HEAD), :]
                        for b in range(CHUNK)
                    ],
                    axis=1,
                )
                accum = accum * fade + jnp.dot(
                    values, probs.astype(BF), preferred_element_type=F32
                )
                top = new_top
            part = (accum / total).astype(BF)
            first = pl.multiple_of(h * HEAD, HEAD)
            for a in range(QG):
                lanes = slice(a * TOK, (a + 1) * TOK)
                o_buf[a, pl.ds(first, HEAD), :] = part[:, lanes]
                st_buf[a, pl.ds(h, 1), :] = top[:, lanes]
                st_buf[a, pl.ds(h + 16, 1), :] = total[:, lanes]
            return unused

        lax.fori_loop(0, 3, one, 0)
        rows = pl.ds(g * 192, 192)
        for o in range(1, QG):
            a, device = query_peers[o - 1]
            c = remote(
                o_buf.at[a, rows], o_got.at[mine, rows], o_send.at[o, g], o_recv.at[o, g], device
            )
            c.start()
            o_copies.append(c)
    for o in range(1, QG):
        a, device = query_peers[o - 1]
        c = remote(st_buf.at[a], st_got.at[mine], st_send.at[o], st_recv.at[o], device)
        c.start()
        o_copies.append(c)
    o_got[mine] = o_buf[mine]
    st_got[mine] = st_buf[mine]
    for c in o_copies:
        c.wait_recv()
    lse_ref[...] = jnp.zeros_like(lse_ref)
    for h in range(HEADS):
        tops = [st_got[a, pl.ds(h, 1), :] for a in range(QG)]
        best = jnp.maximum(jnp.maximum(tops[0], tops[1]), jnp.maximum(tops[2], tops[3]))
        shares = [st_got[a, pl.ds(h + 16, 1), :] * jnp.exp(tops[a] - best) for a in range(QG)]
        whole = shares[0] + shares[1] + shares[2] + shares[3]
        lse_ref[pl.ds(h, 1), :] = best + jnp.log(whole)
        result = jnp.zeros((HEAD, TOK), F32)
        for a in range(QG):
            result = result + o_got[a, pl.ds(h * HEAD, HEAD), :].astype(F32) * (shares[a] / whole)
        o_ref[pl.ds(h * HEAD, HEAD), :] = result
    for c in copies + o_copies:
        c.wait_send()


def attention_forward(q_block, kv_block):
    return pl.pallas_call(
        forward_kernel,
        out_shape=[
            jax.ShapeDtypeStruct((D, TOK), F32),
            jax.ShapeDtypeStruct((16, TOK), F32),
            jax.ShapeDtypeStruct((QG, QROWS, TOK), BF),
            jax.ShapeDtypeStruct((KG, KROWS, TOK), BF),
            jax.ShapeDtypeStruct((KV_HEADS, KG * TOK, 128), BF),
        ],
        in_specs=[VM, VM],
        out_specs=[VM] * 5,
        scratch_shapes=[
            pltpu.VMEM((QG, D, TOK), BF),
            pltpu.VMEM((QG, 32, TOK), F32),
            pltpu.VMEM((QG, D, TOK), BF),
            pltpu.VMEM((QG, 32, TOK), F32),
            pltpu.SemaphoreType.DMA((QG,)),
            pltpu.SemaphoreType.DMA((QG,)),
            pltpu.SemaphoreType.DMA((KG,)),
            pltpu.SemaphoreType.DMA((KG,)),
            pltpu.SemaphoreType.DMA((QG, KV_HEADS)),
            pltpu.SemaphoreType.DMA((QG, KV_HEADS)),
            pltpu.SemaphoreType.DMA((QG,)),
            pltpu.SemaphoreType.DMA((QG,)),
            pltpu.SemaphoreType.DMA((2,)),
        ],
        compiler_params=params(1),
    )(q_block, kv_block)


def across(left, right):
    return lax.dot_general(left, right, (((1,), (1,)), ((), ())), preferred_element_type=F32)


def backward_kernel(
    do_ref, st_ref, q_all, kv_all, kv_tok, dq_ref, dkv_ref,
    do_all, st_all, dq_buf, dkv_acc, dkv_buf, dq_got, dkv_got,
    do_send, do_recv, st_send, st_recv, dq_send, dq_recv, dkv_send, dkv_recv, own_sem,
):
    mine, plane, query_peers, key_peers = groups()
    greet([d for _, d in query_peers] + [d for _, d in key_peers])
    copies = []
    for o in range(1, QG):
        device = query_peers[o - 1][1]
        copies.append(remote(do_ref, do_all.at[mine], do_send.at[o], do_recv.at[o], device))
        copies.append(remote(st_ref, st_all.at[mine], st_send.at[o], st_recv.at[o], device))
    for c in copies:
        c.start()
    own_do = pltpu.make_async_copy(do_ref, do_all.at[mine], own_sem.at[0])
    own_st = pltpu.make_async_copy(st_ref, st_all.at[mine], own_sem.at[1])
    own_do.start()
    own_st.start()
    own_do.wait()
    own_st.wait()
    for c in copies:
        c.wait_recv()
    zeros = jnp.zeros((HEAD, QG * TOK), BF)
    sends = []
    for g in range(KV_HEADS):
        dkv_acc[...] = jnp.zeros_like(dkv_acc)

        def one(r, unused, g=g):
            h = g * 3 + r
            queries = head_rows(q_all, h)
            grads = head_rows(do_all, h)
            grads_low = jnp.concatenate([zeros, grads], axis=0)
            lse = jnp.concatenate([st_all[a, pl.ds(h, 1), :] for a in range(QG)], axis=1)
            delta = jnp.concatenate([st_all[a, pl.ds(h + 16, 1), :] for a in range(QG)], axis=1)
            accum = jnp.zeros((HEAD, QG * TOK), F32)
            for chunk in range(KG // CHUNK):
                keys, scores = scores_of(q_all, kv_all, kv_tok, g, chunk, queries, zeros)
                probs = jnp.exp(scores - lse)
                grad_probs = jnp.dot(keys, grads_low, preferred_element_type=F32)
                grad_scores = (probs * (grad_probs - delta)).astype(BF)
                keys_flat = jnp.concatenate(
                    [kv_all[chunk * CHUNK + b, pl.ds(g * 128, HEAD), :] for b in range(CHUNK)],
                    axis=1,
                )
                accum = accum + jnp.dot(keys_flat, grad_scores, preferred_element_type=F32)
                lanes = pl.ds(chunk * CHUNK * TOK, CHUNK * TOK)
                dkv_acc[0:HEAD, lanes] += across(queries, grad_scores)
                dkv_acc[HEAD : 2 * HEAD, lanes] += across(grads, probs.astype(BF))
            part = accum.astype(BF)
            first = pl.multiple_of(h * HEAD, HEAD)
            for a in range(QG):
                dq_buf[a, pl.ds(first, HEAD), :] = part[:, a * TOK : (a + 1) * TOK]
            return unused

        lax.fori_loop(0, 3, one, 0)
        for j in range(KG):
            dkv_buf[j, pl.ds(g * 128, 128), :] = dkv_acc[:, j * TOK : (j + 1) * TOK].astype(BF)
        rows = pl.ds(g * 128, 128)
        for o in range(1, KG):
            j, device = key_peers[o - 1]
            c = remote(
                dkv_buf.at[j, rows], dkv_got.at[plane, rows], dkv_send.at[o, g], dkv_recv.at[o, g], device
            )
            c.start()
            sends.append(c)
        rows = pl.ds(g * 192, 192)
        for o in range(1, QG):
            a, device = query_peers[o - 1]
            c = remote(
                dq_buf.at[a, rows], dq_got.at[mine, rows], dq_send.at[o, g], dq_recv.at[o, g], device
            )
            c.start()
            sends.append(c)
    dq_got[mine] = dq_buf[mine]
    dkv_got[plane] = dkv_buf[plane]
    for c in sends:
        c.wait_recv()
    total = dq_got[0].astype(F32)
    for a in range(1, QG):
        total = total + dq_got[a].astype(F32)
    dq_ref[...] = total
    total = dkv_got[0].astype(F32)
    for j in range(1, KG):
        total = total + dkv_got[j].astype(F32)
    dkv_ref[...] = total
    for c in copies + sends:
        c.wait_send()


def attention_backward(do_block, st_block, q_all, kv_all, kv_tok):
    return pl.pallas_call(
        backward_kernel,
        out_shape=[
            jax.ShapeDtypeStruct((D, TOK), F32),
            jax.ShapeDtypeStruct((384, TOK), F32),
        ],
        in_specs=[VM] * 5,
        out_specs=[VM] * 2,
        scratch_shapes=[
            pltpu.VMEM((QG, D, TOK), BF),
            pltpu.VMEM((QG, 32, TOK), F32),
            pltpu.VMEM((QG, D, TOK), BF),
            pltpu.VMEM((128, KG * TOK), F32),
            pltpu.VMEM((KG, 384, TOK), BF),
            pltpu.VMEM((QG, D, TOK), BF),
            pltpu.VMEM((KG, 384, TOK), BF),
            pltpu.SemaphoreType.DMA((QG,)),
            pltpu.SemaphoreType.DMA((QG,)),
            pltpu.SemaphoreType.DMA((QG,)),
            pltpu.SemaphoreType.DMA((QG,)),
            pltpu.SemaphoreType.DMA((QG, KV_HEADS)),
            pltpu.SemaphoreType.DMA((QG, KV_HEADS)),
            pltpu.SemaphoreType.DMA((KG, KV_HEADS)),
            pltpu.SemaphoreType.DMA((KG, KV_HEADS)),
            pltpu.SemaphoreType.DMA((2,)),
        ],
        compiler_params=params(2),
    )(do_block, st_block, q_all, kv_all, kv_tok)


WIDE = 640
XCOLS = 3 * WIDE + FF
YROWS = 3072
AROWS = 160
DROWS = 32


def reduce_kernel(
    x_ref, y_ref, gn_ref, fa_ref, fd_ref,
    x_all, y_all, gn_all, ga, gd, ra, rd, sa, sd, wa, wd,
    own_sem, sib_send, sib_recv, a_send, a_recv, d_send, d_recv,
    wa_send, wa_recv, wd_send, wd_recv, f_send, f_recv,
):
    dp, x_hi, plane, core = place()
    sibling = (dp, ctx_of(x_hi, plane, 1 - core))
    line = []
    for flip_dp in range(2):
        for flip_x in range(2):
            for flip_core in range(2):
                if flip_dp + flip_x + flip_core:
                    line.append(
                        (
                            (dp + flip_dp) % 2,
                            ctx_of((x_hi + flip_x) % 2, plane, (core + flip_core) % 2),
                        )
                    )
    peers = []
    for o in range(1, KG):
        j = plane_peer(plane, o)
        peers.append((j, (dp, ctx_of(x_hi, j, core))))
    greet(line + [d for _, d in peers])
    to_sibling = [
        remote(x_ref, x_all.at[pl.ds(TOK, TOK)], sib_send.at[0], sib_recv.at[0], sibling),
        remote(
            y_ref.at[1 - core], y_all.at[:, pl.ds(TOK, TOK)], sib_send.at[1], sib_recv.at[1], sibling
        ),
        remote(gn_ref, gn_all, sib_send.at[2], sib_recv.at[2], sibling),
    ]
    own = [
        pltpu.make_async_copy(x_ref, x_all.at[pl.ds(0, TOK)], own_sem.at[0]),
        pltpu.make_async_copy(y_ref.at[core], y_all.at[:, pl.ds(0, TOK)], own_sem.at[1]),
    ]
    for c in to_sibling + own:
        c.start()
    for c in own:
        c.wait()
    for c in to_sibling:
        c.wait_recv()

    def product(first, rows, x_first, x_cols):
        return jnp.dot(
            y_all[pl.ds(first, rows), :],
            x_all[:, pl.ds(x_first, x_cols)],
            preferred_element_type=F32,
        )

    row = lax.broadcasted_iota(jnp.int32, (KG, 32, WIDE), 1)
    sums = gn_ref[...] + gn_all[...]
    part = product(0, 512, 0, WIDE).reshape(KG, 32, WIDE)
    part = jnp.where(row == 30, sums[0:1][None], part)
    ga[:, 0:32, :] = part.astype(BF)
    part = product(512, 512, WIDE, WIDE).reshape(KG, 32, WIDE)
    part = jnp.where(row == 18, sums[1:2][None], part)
    ga[:, 32:64, :] = part.astype(BF)
    ga[:, 64:112, :] = product(1024, 768, 2 * WIDE, WIDE).reshape(KG, 48, WIDE).astype(BF)
    ga[:, 112:160, :] = product(1792, 768, 2 * WIDE, WIDE).reshape(KG, 48, WIDE).astype(BF)
    gd[...] = product(2560, 512, 3 * WIDE, FF).reshape(KG, DROWS, FF).astype(BF)
    sends = []
    for o in range(1, KG):
        j, device = peers[o - 1]
        sends.append(remote(ga.at[j], ra.at[plane], a_send.at[o], a_recv.at[o], device))
        sends.append(remote(gd.at[j], rd.at[plane], d_send.at[o], d_recv.at[o], device))
    for c in sends:
        c.start()
    ra[plane] = ga[plane]
    rd[plane] = gd[plane]
    for c in sends:
        c.wait_recv()

    def add_a(i, unused):
        rows = pl.ds(pl.multiple_of(i * 16, 16), 16)
        total = ra[0, rows, :].astype(F32)
        for s in range(1, KG):
            total = total + ra[s, rows, :].astype(F32)
        sa[rows, :] = total.astype(BF)
        return unused

    lax.fori_loop(0, AROWS // 16, add_a, 0)

    def add_d(i, unused):
        rows = pl.ds(pl.multiple_of(i * 16, 16), 16)
        total = rd[0, rows, :].astype(F32)
        for s in range(1, KG):
            total = total + rd[s, rows, :].astype(F32)
        sd[rows, :] = total.astype(BF)
        return unused

    lax.fori_loop(0, DROWS // 16, add_d, 0)
    slot = dp * 2 + x_hi

    def toward(target_dp):
        device = (target_dp, ctx_of(core, plane, core))
        lanes_a = pl.ds(pl.multiple_of(target_dp * 256, 128), 384)
        lanes_d = pl.ds(pl.multiple_of(target_dp * 768, 128), 768)
        return (
            remote(
                sa.at[:, lanes_a], wa.at[slot], wa_send.at[target_dp], wa_recv.at[slot], device
            ),
            remote(
                sd.at[:, lanes_d], wd.at[slot], wd_send.at[target_dp], wd_recv.at[slot], device
            ),
        )

    collector = core == x_hi
    for target_dp in range(2):

        @pl.when(jnp.logical_not(jnp.logical_and(collector, dp == target_dp)))
        def _():
            for c in toward(target_dp):
                c.start()

        @pl.when(jnp.logical_and(collector, dp == target_dp))
        def _():
            wa[slot] = sa[:, target_dp * 256 : target_dp * 256 + 384]
            wd[slot] = sd[:, target_dp * 768 : target_dp * 768 + 768]

    final = (
        remote(fa_ref, fa_ref, f_send.at[0], f_recv.at[0], sibling),
        remote(fd_ref, fd_ref, f_send.at[1], f_recv.at[1], sibling),
    )

    @pl.when(collector)
    def _():
        for source in range(4):

            @pl.when(slot != source)
            def _():
                remote(
                    sa.at[:, pl.ds(0, 384)], wa.at[source], wa_send.at[0], wa_recv.at[source], sibling
                ).wait_recv()
                remote(
                    sd.at[:, pl.ds(0, 768)], wd.at[source], wd_send.at[0], wd_recv.at[source], sibling
                ).wait_recv()

        fa_ref[...] = (
            wa[0].astype(F32) + wa[1].astype(F32) + wa[2].astype(F32) + wa[3].astype(F32)
        )
        fd_ref[...] = (
            wd[0].astype(F32) + wd[1].astype(F32) + wd[2].astype(F32) + wd[3].astype(F32)
        )
        for c in final:
            c.start()
        for c in final:
            c.wait_send()

    @pl.when(jnp.logical_not(collector))
    def _():
        for c in final:
            c.wait_recv()

    for target_dp in range(2):

        @pl.when(jnp.logical_not(jnp.logical_and(collector, dp == target_dp)))
        def _():
            for c in toward(target_dp):
                c.wait_send()

    for c in to_sibling + sends:
        c.wait_send()


def reduce_weights(x, y, gain_terms):
    dma = pltpu.SemaphoreType.DMA
    return pl.pallas_call(
        reduce_kernel,
        out_shape=[
            jax.ShapeDtypeStruct((AROWS, 384), F32),
            jax.ShapeDtypeStruct((DROWS, 768), F32),
        ],
        in_specs=[VM] * 3,
        out_specs=[VM] * 2,
        scratch_shapes=[
            pltpu.VMEM((2 * TOK, XCOLS), BF),
            pltpu.VMEM((YROWS, 2 * TOK), BF),
            pltpu.VMEM((8, WIDE), F32),
            pltpu.VMEM((KG, AROWS, WIDE), BF),
            pltpu.VMEM((KG, DROWS, FF), BF),
            pltpu.VMEM((KG, AROWS, WIDE), BF),
            pltpu.VMEM((KG, DROWS, FF), BF),
            pltpu.VMEM((AROWS, WIDE), BF),
            pltpu.VMEM((DROWS, FF), BF),
            pltpu.VMEM((4, AROWS, 384), BF),
            pltpu.VMEM((4, DROWS, 768), BF),
            dma((2,)),
            dma((3,)),
            dma((3,)),
            dma((KG,)),
            dma((KG,)),
            dma((KG,)),
            dma((KG,)),
            dma((2,)),
            dma((4,)),
            dma((2,)),
            dma((4,)),
            dma((2,)),
            dma((2,)),
        ],
        compiler_params=params(3),
    )(x, y, gain_terms)


def times_back(left, right):
    return lax.dot_general(left, right, (((1,), (1,)), ((), ())), preferred_element_type=F32)


def flat(weight, tokens):
    return lax.dot_general(weight, tokens, (((0,), (1,)), ((), ())), preferred_element_type=F32)


def unflat(rows, weight):
    return lax.dot_general(rows, weight, (((0,), (1,)), ((), ())), preferred_element_type=F32)


def rope_flat(rows, heads, cosine, sine, sign):
    parts = rows.reshape(heads, 2, HEAD // 2, TOK)
    one, two = parts[:, 0], parts[:, 1]
    first = one * cosine - sign * two * sine
    second = two * cosine + sign * one * sine
    return jnp.stack([first, second], axis=1)


def by_chip(rows):
    return rows.reshape(32, rows.shape[0] // 32, TOK)


def local(
    hidden, positions, w_query, w_key, w_value, w_out, w_gate, w_up, w_down,
    gain_attn, gain_ffn, grad_out,
):
    dp, x_hi, plane, core = place()
    gains = jnp.pad(jnp.concatenate([gain_attn, gain_ffn], axis=0), ((0, 14), (0, 96)))
    wq, wk, wv, wo, wg, wu, wd, gains = gather_weights(
        [w[0] for w in (w_query, w_key, w_value, w_out, w_gate, w_up, w_down)], gains
    )
    gains = jnp.concatenate([gains[0, :2, :288], gains[1, :2, :288]], axis=1).astype(F32)
    gain_one, gain_two = gains[0:1], gains[1:2]
    state = hidden[0].astype(F32)
    scale_one = lax.rsqrt(jnp.mean(state * state, axis=-1, keepdims=True) + eps)
    unit_one = state * scale_one
    normal_one = (unit_one * gain_one).astype(BF)
    places = positions[0]
    freqs = rope_base ** (-(jnp.arange(HEAD // 2, dtype=F32) * 2.0 / HEAD))
    angles = freqs[:, None] * places.astype(F32)[None, :]
    cosine, sine = jnp.cos(angles), jnp.sin(angles)
    run = (places[0] // TOK).astype(BF)
    run_rows = jnp.full((16, TOK), run, BF)
    query = rope_flat(flat(wq, normal_one), HEADS, cosine, sine, 1.0).astype(BF)
    query = query.reshape(D, TOK) * jnp.asarray(0.125, BF)
    keys = rope_flat(flat(wk, normal_one), KV_HEADS, cosine, sine, 1.0).astype(BF)
    keys = keys.reshape(KV_HEADS, HEAD, TOK)
    values = flat(wv, normal_one).astype(BF).reshape(KV_HEADS, HEAD, TOK)
    kv_block = jnp.concatenate([keys, values], axis=1).reshape(384, TOK)
    o_rows, lse, q_all, kv_all, kv_tok = attention_forward(
        jnp.concatenate([query, run_rows], axis=0), jnp.concatenate([kv_block, run_rows], axis=0)
    )
    attended = o_rows.T.astype(BF)
    middle = state + jnp.dot(attended, wo, preferred_element_type=F32)
    scale_two = lax.rsqrt(jnp.mean(middle * middle, axis=-1, keepdims=True) + eps)
    unit_two = middle * scale_two
    normal_two = (unit_two * gain_two).astype(BF)
    gate = jnp.dot(normal_two, wg, preferred_element_type=F32)
    upper = jnp.dot(normal_two, wu, preferred_element_type=F32)
    inner = (jax.nn.silu(gate) * upper).astype(BF)
    output = (middle + jnp.dot(inner, wd, preferred_element_type=F32)).astype(BF)

    grad_low = grad_out[0]
    grad = grad_low.astype(F32)
    grad_inner = times_back(grad_low, wd)
    sigma = jax.nn.sigmoid(gate)
    grad_gate_low = (grad_inner * upper * sigma * (1.0 + gate * (1.0 - sigma))).astype(BF)
    grad_up_low = (grad_inner * gate * sigma).astype(BF)
    grad_normal = times_back(grad_gate_low, wg) + times_back(grad_up_low, wu)
    gain_ffn_term = jnp.sum(grad_normal * unit_two, axis=0)
    grad_unit = grad_normal * gain_two
    grad_middle = (
        scale_two * (grad_unit - unit_two * jnp.mean(grad_unit * unit_two, axis=-1, keepdims=True))
        + grad
    )
    branch_low = grad_middle.astype(BF)
    do_block = times_back(wo, branch_low).astype(BF)
    delta = jnp.sum((do_block.astype(F32) * o_rows).reshape(HEADS, HEAD, TOK), axis=1)
    st_block = jnp.concatenate([lse, jnp.pad(delta, ((0, 7), (0, 0)))], axis=0)
    dq_rows, dkv_rows = attention_backward(do_block, st_block, q_all, kv_all, kv_tok)
    dq_rows = rope_flat(dq_rows * 0.125, HEADS, cosine, sine, -1.0).astype(BF).reshape(D, TOK)
    dkv_rows = dkv_rows.reshape(KV_HEADS, 2, HEAD, TOK)
    dk_rows = rope_flat(dkv_rows[:, 0].reshape(192, TOK), KV_HEADS, cosine, sine, -1.0)
    dk_rows = dk_rows.astype(BF).reshape(192, TOK)
    dv_rows = dkv_rows[:, 1].reshape(192, TOK).astype(BF)
    grad_first = unflat(dq_rows, wq) + unflat(dk_rows, wk) + unflat(dv_rows, wv)
    gain_attn_term = jnp.sum(grad_first * unit_one, axis=0)
    grad_unit_one = grad_first * gain_one
    grad_input = (
        scale_one
        * (grad_unit_one - unit_one * jnp.mean(grad_unit_one * unit_one, axis=-1, keepdims=True))
        + grad_middle
    )

    wide = ((0, 0), (0, WIDE - D))
    x = jnp.concatenate(
        [jnp.pad(normal_one, wide), jnp.pad(attended, wide), jnp.pad(normal_two, wide), inner],
        axis=1,
    )
    blank = lambda rows: jnp.zeros((32, rows, TOK), BF)
    qkv_rows = jnp.concatenate(
        [by_chip(dq_rows), by_chip(dk_rows), by_chip(dv_rows), blank(2)], axis=1
    ).reshape(2, 512, TOK)
    o_part = jnp.concatenate([by_chip(branch_low.T), blank(14)], axis=1).reshape(2, 512, TOK)
    down_part = jnp.concatenate([by_chip(grad_low.T), blank(14)], axis=1).reshape(2, 512, TOK)
    y = jnp.concatenate(
        [
            qkv_rows,
            o_part,
            grad_gate_low.T.reshape(2, 768, TOK),
            grad_up_low.T.reshape(2, 768, TOK),
            down_part,
        ],
        axis=1,
    )
    gain_terms = jnp.pad(jnp.stack([gain_attn_term, gain_ffn_term]), ((0, 6), (0, WIDE - D)))
    fa, fd = reduce_weights(x, y, gain_terms)
    fa = lax.dynamic_slice(fa, (0, dp * 32), (AROWS, 288))

    def mine_of(rows, first, count):
        part = lax.dynamic_slice_in_dim(rows, first + core * count, count, 0)
        return part.T[None]

    return (
        output[None],
        grad_input[None],
        mine_of(fa, 0, 9),
        mine_of(fa, 18, 3),
        mine_of(fa, 24, 3),
        mine_of(fa, 32, 9),
        mine_of(fa, 64, 24),
        mine_of(fa, 112, 24),
        mine_of(fd, 0, 9),
        fa[30][None],
        fa[32 + 18][None],
    )


def solution(mesh):
    in_specs = (
        P("dp", "ctx", None),
        P("dp", "ctx"),
    ) + (P(None, "dp", None),) * 7 + (
        P(None, "dp"),
        P(None, "dp"),
        P("dp", "ctx", None),
    )
    out_specs = (
        P("dp", "ctx", None),
        P("dp", "ctx", None),
    ) + (P(None, "dp", "ctx"),) * 7 + (
        P(None, "dp"),
        P(None, "dp"),
    )
    return jax.shard_map(local, mesh=mesh, in_specs=in_specs, out_specs=out_specs, check_vma=False)
```

```python
import functools

import jax
import jax.numpy as jnp
from jax import lax
from jax.experimental import pallas as pl
from jax.experimental.pallas import tpu as pltpu
from jax.sharding import PartitionSpec as P

HEADS = 9
KV_HEADS = 3
HEAD = 64
TOK = 128
D = 576
FF = 1536
QG = 4
KG = 16
eps = 1e-05
rope_base = 100000.0
MESH = pl.DeviceIdType.MESH
BF = jnp.bfloat16
F32 = jnp.float32
LIMIT = 56 * 1024 * 1024
VM = pl.BlockSpec(memory_space=pltpu.VMEM)
ANY = pl.BlockSpec(memory_space=pl.ANY)


def params(ident):
    return pltpu.CompilerParams(
        collective_id=ident, has_side_effects=True, vmem_limit_bytes=LIMIT
    )


def place():
    dp = lax.axis_index("dp")
    ctx = lax.axis_index("ctx")
    x_hi = ctx // 32
    plane = (ctx // 2) % 16
    core = ctx % 2
    return dp, x_hi, plane, core


def ctx_of(x_hi, plane, core):
    return x_hi * 32 + plane * 2 + core


def remote(src, dst, send, recv, device):
    return pltpu.make_async_remote_copy(
        src_ref=src,
        dst_ref=dst,
        send_sem=send,
        recv_sem=recv,
        device_id=device,
        device_id_type=MESH,
    )


def greet(devices):
    barrier = pltpu.get_barrier_semaphore()
    for device in devices:
        pl.semaphore_signal(barrier, inc=1, device_id=device, device_id_type=MESH)
    pl.semaphore_wait(barrier, len(devices))


def plane_peer(plane, offset):
    y, z = plane // 4, plane % 4
    return ((y + offset // 4) % 4) * 4 + (z + offset % 4) % 4


def plane_source(plane, offset):
    y, z = plane // 4, plane % 4
    return ((y + 4 - offset // 4) % 4) * 4 + (z + 4 - offset % 4) % 4


def weight_copies(shards, fulls, own_sem, send, recv, core_send, core_recv):
    dp, x_hi, plane, core = place()
    near = (1 - dp, ctx_of(x_hi, plane, core))
    far = (1 - dp, ctx_of(1 - x_hi, plane, core))
    sibling = (dp, ctx_of(x_hi, plane, 1 - core))
    own, first, second = [], [], []
    for which, (shard, full) in enumerate(zip(shards, fulls)):
        rows = shard.shape[0]
        half = rows // 2
        cut = 80 if rows == 288 else half // 2
        mine = pl.multiple_of(dp * rows, 16)
        theirs = pl.multiple_of((1 - dp) * rows, 16)
        own.append(
            pltpu.make_async_copy(shard, full.at[pl.ds(mine, rows)], own_sem.at[which])
        )
        for role, target in ((0, near), (1, far)):
            off = pl.multiple_of(role * cut + core * half, 16)
            size = half - cut if role else cut
            first.append(
                remote(
                    shard.at[pl.ds(off, size)],
                    full.at[pl.ds(pl.multiple_of(mine + off, 16), size)],
                    send.at[which, role],
                    recv.at[which, role],
                    target,
                )
            )
            got = full.at[pl.ds(pl.multiple_of(theirs + off, 16), size)]
            second.append(
                remote(got, got, core_send.at[which, role], core_recv.at[which, role], sibling)
            )
    return own, first, second


def weight_sems(count):
    return [pltpu.SemaphoreType.DMA((count,))] + [pltpu.SemaphoreType.DMA((count, 2))] * 4


def weights_kernel(count, *refs):
    shards = refs[:count]
    gains = refs[count]
    fulls = refs[count + 1 : 2 * count + 1]
    gains_full = refs[2 * count + 1]
    gain_send, gain_recv = refs[2 * count + 2 : 2 * count + 4]
    dp, x_hi, plane, core = place()
    near = (1 - dp, ctx_of(x_hi, plane, core))
    far = (1 - dp, ctx_of(1 - x_hi, plane, core))
    sibling = (dp, ctx_of(x_hi, plane, 1 - core))
    greet([near, far, sibling])
    own, first, second = weight_copies(shards, fulls, *refs[2 * count + 4 :])
    gain_copy = remote(gains, gains_full.at[dp], gain_send, gain_recv, near)
    for c in first + [gain_copy] + own:
        c.start()
    gains_full[dp] = gains[...]
    for c, d in zip(first, second):
        c.wait_recv()
        d.start()
    for c in second:
        c.wait_recv()
    gain_copy.wait_recv()
    for c in own:
        c.wait()
    for c in first + second + [gain_copy]:
        c.wait_send()


def gather_weights(shards, gains):
    count = len(shards)
    outs = [jax.ShapeDtypeStruct((2 * s.shape[0], s.shape[1]), s.dtype) for s in shards]
    outs.append(jax.ShapeDtypeStruct((2,) + gains.shape, gains.dtype))
    return pl.pallas_call(
        functools.partial(weights_kernel, count),
        out_shape=outs,
        in_specs=[VM] * (count + 1),
        out_specs=[VM] * (count + 1),
        scratch_shapes=[pltpu.SemaphoreType.DMA, pltpu.SemaphoreType.DMA] + weight_sems(count),
        compiler_params=params(0),
    )(*shards, gains)


QROWS = D + 16
KROWS = 384 + 16
CHUNK = 4


def groups():
    dp, x_hi, plane, core = place()
    mine = x_hi * 2 + core
    query_peers = []
    for o in range(1, QG):
        a = (mine + o) % QG
        query_peers.append((a, (dp, ctx_of(a // 2, plane, a % 2))))
    key_peers = []
    for o in range(1, KG):
        j = plane_peer(plane, o)
        key_peers.append((j, (dp, ctx_of(x_hi, j, core))))
    return mine, plane, query_peers, key_peers


def flip_keys(kv_all, kv_tok, j):
    for g in range(KV_HEADS):
        block = kv_all[j, pl.ds(g * 128, 128), :].astype(F32)
        kv_tok[g, pl.ds(pl.multiple_of(j * TOK, TOK), TOK), :] = block.T.astype(BF)


def masks_of(q_all, kv_all, base):
    lane = lax.broadcasted_iota(jnp.int32, (1, TOK), 1).astype(F32)
    q_pos = jnp.concatenate(
        [q_all[a, pl.ds(D, 16), :].astype(F32)[0:1] * TOK + lane for a in range(QG)], axis=1
    )
    rows = lax.broadcasted_iota(jnp.int32, (TOK, QG * TOK), 0).astype(F32)
    parts = []
    for b in range(CHUNK):
        start = kv_all[base + b, pl.ds(384, 16), :].astype(F32)[0:1] * TOK
        start = jnp.concatenate([start] * QG, axis=1)
        parts.append(rows <= (q_pos - start))
    return jnp.concatenate(parts, axis=0)


def head_rows(ref, h):
    first = pl.multiple_of(h * HEAD, HEAD)
    return jnp.concatenate([ref[a, pl.ds(first, HEAD), :] for a in range(QG)], axis=1)


def scores_of(q_all, kv_all, kv_tok, g, base, queries, zeros):
    keys = kv_tok[g, pl.ds(pl.multiple_of(base * TOK, TOK), CHUNK * TOK), :]
    scores = jnp.dot(keys, jnp.concatenate([queries, zeros], axis=0), preferred_element_type=F32)
    return keys, jnp.where(masks_of(q_all, kv_all, base), scores, -1e30)


def forward_kernel(count, *refs):
    q_ref, kv_ref = refs[:2]
    shards = refs[2 : 2 + count]
    o_ref, lse_ref, q_all, kv_all, kv_tok = refs[2 + count : 7 + count]
    fulls = refs[7 + count : 7 + 2 * count]
    (
        accum_all, top_all, total_all, o_buf, st_buf, o_got, st_got,
        q_send, q_recv, kv_send, kv_recv, o_send, o_recv, st_send, st_recv, own_sem,
    ) = refs[7 + 2 * count : 23 + 2 * count]
    mine, plane, query_peers, key_peers = groups()
    dp, x_hi, plane, core = place()
    greet(
        [d for _, d in query_peers]
        + [d for _, d in key_peers]
        + [(1 - dp, ctx_of(x_hi, plane, core)), (1 - dp, ctx_of(1 - x_hi, plane, core))]
    )
    copies, q_copies, kv_copies = [], [], [None]
    for o in range(1, QG):
        q_copies.append(
            remote(q_ref, q_all.at[mine], q_send.at[o], q_recv.at[o], query_peers[o - 1][1])
        )
    for o in range(1, KG):
        kv_copies.append(
            remote(kv_ref, kv_all.at[plane], kv_send.at[o], kv_recv.at[o], key_peers[o - 1][1])
        )
    copies = q_copies + kv_copies[1:]
    for c in copies:
        c.start()
    own_w, first_w, second_w = weight_copies(shards, fulls, *refs[23 + 2 * count :])
    for c in first_w + own_w:
        c.start()
    q_all[mine] = q_ref[...]
    kv_all[plane] = kv_ref[...]
    for c in q_copies:
        c.wait_recv()
    zeros = jnp.zeros((HEAD, QG * TOK), BF)
    o_copies = []
    for step in range(4):
        base = ((plane // 4 + 4 - step) % 4) * 4
        for dz in range(4):
            if step * 4 + dz:
                kv_copies[step * 4 + dz].wait_recv()

        def flip(b, unused, base=base):
            flip_keys(kv_all, kv_tok, base + b)
            return unused

        lax.fori_loop(0, 4, flip, 0)

        def one(h, unused, step=step, base=base):
            g = h // 3
            first = pl.multiple_of(h * HEAD, HEAD)
            queries = head_rows(q_all, h)
            keys, scores = scores_of(q_all, kv_all, kv_tok, g, base, queries, zeros)
            new_top = jnp.max(scores, axis=0, keepdims=True)
            if step:
                top = top_all[pl.ds(h, 1), :]
                new_top = jnp.maximum(top, new_top)
            probs = jnp.exp(scores - new_top)
            total = jnp.sum(probs, axis=0, keepdims=True)
            value_rows = pl.ds(pl.multiple_of(g * 128 + HEAD, HEAD), HEAD)
            values = jnp.concatenate(
                [kv_all[base + b, value_rows, :] for b in range(CHUNK)], axis=1
            )
            accum = jnp.dot(values, probs.astype(BF), preferred_element_type=F32)
            if step:
                fade = jnp.exp(top - new_top)
                total = total + total_all[pl.ds(h, 1), :] * fade
                accum = accum + accum_all[pl.ds(first, HEAD), :] * fade
            if step < 3:
                top_all[pl.ds(h, 1), :] = new_top
                total_all[pl.ds(h, 1), :] = total
                accum_all[pl.ds(first, HEAD), :] = accum
                return unused
            part = (accum / total).astype(BF)
            for a in range(QG):
                lanes = slice(a * TOK, (a + 1) * TOK)
                o_buf[a, pl.ds(first, HEAD), :] = part[:, lanes]
                st_buf[a, pl.ds(h, 1), :] = new_top[:, lanes]
                st_buf[a, pl.ds(h + 16, 1), :] = total[:, lanes]
            return unused

        if step < 3:
            lax.fori_loop(0, HEADS, one, 0)
            if step == 1:
                for c, d in zip(first_w, second_w):
                    c.wait_recv()
                    d.start()
            continue
        for g in range(KV_HEADS):
            lax.fori_loop(3 * g, 3 * g + 3, one, 0)
            rows = pl.ds(g * 192, 192)
            for o in range(1, QG):
                a, device = query_peers[o - 1]
                c = remote(
                    o_buf.at[a, rows], o_got.at[mine, rows], o_send.at[o, g], o_recv.at[o, g], device
                )
                c.start()
                o_copies.append(c)
    for o in range(1, QG):
        a, device = query_peers[o - 1]
        c = remote(st_buf.at[a], st_got.at[mine], st_send.at[o], st_recv.at[o], device)
        c.start()
        o_copies.append(c)
    o_got[mine] = o_buf[mine]
    st_got[mine] = st_buf[mine]
    for c in own_w:
        c.wait()
    for c in second_w:
        c.wait_recv()
    for c in first_w + second_w:
        c.wait_send()
    for c in o_copies:
        c.wait_recv()
    lse_ref[...] = jnp.zeros_like(lse_ref)
    for h in range(HEADS):
        tops = [st_got[a, pl.ds(h, 1), :] for a in range(QG)]
        best = jnp.maximum(jnp.maximum(tops[0], tops[1]), jnp.maximum(tops[2], tops[3]))
        shares = [st_got[a, pl.ds(h + 16, 1), :] * jnp.exp(tops[a] - best) for a in range(QG)]
        whole = shares[0] + shares[1] + shares[2] + shares[3]
        lse_ref[pl.ds(h, 1), :] = best + jnp.log(whole)
        result = jnp.zeros((HEAD, TOK), F32)
        for a in range(QG):
            result = result + o_got[a, pl.ds(h * HEAD, HEAD), :].astype(F32) * (shares[a] / whole)
        o_ref[pl.ds(h * HEAD, HEAD), :] = result
    for c in copies + o_copies:
        c.wait_send()


def attention_forward(q_block, kv_block, shards):
    count = len(shards)
    dma = pltpu.SemaphoreType.DMA
    fulls = [jax.ShapeDtypeStruct((2 * s.shape[0], s.shape[1]), s.dtype) for s in shards]
    return pl.pallas_call(
        functools.partial(forward_kernel, count),
        out_shape=[
            jax.ShapeDtypeStruct((D, TOK), F32),
            jax.ShapeDtypeStruct((16, TOK), F32),
            jax.ShapeDtypeStruct((QG, QROWS, TOK), BF),
            jax.ShapeDtypeStruct((KG, KROWS, TOK), BF),
            jax.ShapeDtypeStruct((KV_HEADS, KG * TOK, 128), BF),
        ]
        + fulls,
        in_specs=[VM] * (2 + count),
        out_specs=[VM] * (5 + count),
        scratch_shapes=[
            pltpu.VMEM((D, QG * TOK), F32),
            pltpu.VMEM((16, QG * TOK), F32),
            pltpu.VMEM((16, QG * TOK), F32),
            pltpu.VMEM((QG, D, TOK), BF),
            pltpu.VMEM((QG, 32, TOK), F32),
            pltpu.VMEM((QG, D, TOK), BF),
            pltpu.VMEM((QG, 32, TOK), F32),
            dma((QG,)),
            dma((QG,)),
            dma((KG,)),
            dma((KG,)),
            dma((QG, KV_HEADS)),
            dma((QG, KV_HEADS)),
            dma((QG,)),
            dma((QG,)),
            dma((2,)),
        ]
        + weight_sems(count),
        compiler_params=params(1),
    )(q_block, kv_block, *shards)


def across(left, right):
    return lax.dot_general(left, right, (((1,), (1,)), ((), ())), preferred_element_type=F32)


WIDE = 640
GROWS = 128
GYROWS = 2048
QUARTER = 384


def line_peers():
    dp, x_hi, plane, core = place()
    return [
        ((dp + d) % 2, (x_hi + x) % 2, ((dp + d) % 2, ctx_of((x_hi + x) % 2, plane, core)))
        for d, x in ((1, 0), (0, 1), (1, 1))
    ]


def sum_pieces(pieces, count, rows):
    total = pieces[0, rows, :].astype(F32)
    for i in range(1, count):
        total = total + pieces[i, rows, :].astype(F32)
    return total


def backward_kernel(
    do_ref, st_ref, q_all, kv_all, kv_tok, x_ref, in_ref, y_ref, yd_ref,
    dq_ref, dkv_ref, sa_ref, fd_ref,
    do_all, st_all, dq_buf, dkv_acc, dkv_buf, dq_got, dkv_got,
    x_all, in_all, y_all, yd_all, ga, ra, gd, rd, gp, rp,
    do_send, do_recv, st_send, st_recv, dq_send, dq_recv, dkv_send, dkv_recv,
    sib_send, sib_recv, a_send, a_recv, d_send, d_recv, p_send, p_recv, f_send, f_recv,
):
    dp, x_hi, plane, core = place()
    mine, plane, query_peers, key_peers = groups()
    line = line_peers()
    sibling = (dp, ctx_of(x_hi, plane, 1 - core))
    greet(
        [d for _, d in query_peers] + [d for _, d in key_peers] + [line[0][2], line[2][2]]
    )
    own, late = pl.ds(0, TOK), pl.ds(TOK, TOK)
    to_sibling = [
        remote(x_ref, x_all.at[late], sib_send.at[0], sib_recv.at[0], sibling),
        remote(in_ref.at[1 - core], in_all.at[late], sib_send.at[1], sib_recv.at[1], sibling),
        remote(y_ref.at[1 - core], y_all.at[:, late], sib_send.at[2], sib_recv.at[2], sibling),
        remote(yd_ref, yd_all.at[:, late], sib_send.at[3], sib_recv.at[3], sibling),
    ]
    copies = []
    for o in range(1, QG):
        device = query_peers[o - 1][1]
        copies.append(remote(do_ref, do_all.at[mine], do_send.at[o], do_recv.at[o], device))
        copies.append(remote(st_ref, st_all.at[mine], st_send.at[o], st_recv.at[o], device))
    for c in to_sibling + copies:
        c.start()
    x_all[own, :] = x_ref[...]
    in_all[own, :] = in_ref[core]
    y_all[:, own] = y_ref[core]
    yd_all[:, own] = yd_ref[...]
    do_all[mine] = do_ref[...]
    st_all[mine] = st_ref[...]
    for c in to_sibling:
        c.wait_recv()

    part = jnp.dot(yd_all[...], in_all[...], preferred_element_type=F32).astype(BF)
    for x in range(2):
        for d in range(2):
            gd[x, d] = part[512 * x : 512 * (x + 1), QUARTER * d : QUARTER * (d + 1)].reshape(
                KG, 32, QUARTER
            )
    slot = dp * 2 + x_hi
    sends = []
    d_sends = []
    for i, (d, x, device) in enumerate(line):
        d_sends.append(remote(gd.at[x, d], rd.at[slot], d_send.at[i], d_recv.at[i], device))
    for c in d_sends:
        c.start()
    rd[slot] = gd[x_hi, dp]

    def product(first, rows, x_first):
        return jnp.dot(
            y_all[pl.ds(first, rows), :], x_all[:, pl.ds(x_first, WIDE)], preferred_element_type=F32
        ).astype(BF)

    ga[:, 0:32, :] = product(0, 512, 0).reshape(KG, 32, WIDE)
    ga[:, 32:80, :] = product(512, 768, WIDE).reshape(KG, 48, WIDE)
    ga[:, 80:128, :] = product(1280, 768, WIDE).reshape(KG, 48, WIDE)
    a_sends = []
    for o in range(1, KG):
        j, device = key_peers[o - 1]
        a_sends.append(remote(ga.at[j], ra.at[plane], a_send.at[o], a_recv.at[o], device))
    for c in a_sends:
        c.start()
    ra[plane] = ga[plane]
    p_sends = []
    for c in copies:
        c.wait_recv()
    zeros = jnp.zeros((HEAD, QG * TOK), BF)
    for g in range(KV_HEADS):
        dkv_acc[...] = jnp.zeros_like(dkv_acc)

        def one(r, unused, g=g):
            h = g * 3 + r
            queries = head_rows(q_all, h)
            grads = head_rows(do_all, h)
            grads_low = jnp.concatenate([zeros, grads], axis=0)
            lse = jnp.concatenate([st_all[a, pl.ds(h, 1), :] for a in range(QG)], axis=1)
            delta = jnp.concatenate([st_all[a, pl.ds(h + 16, 1), :] for a in range(QG)], axis=1)
            accum = jnp.zeros((HEAD, QG * TOK), F32)
            for chunk in range(KG // CHUNK):
                base = chunk * CHUNK
                keys, scores = scores_of(q_all, kv_all, kv_tok, g, base, queries, zeros)
                probs = jnp.exp(scores - lse)
                grad_probs = jnp.dot(keys, grads_low, preferred_element_type=F32)
                grad_scores = (probs * (grad_probs - delta)).astype(BF)
                keys_flat = jnp.concatenate(
                    [kv_all[base + b, pl.ds(g * 128, HEAD), :] for b in range(CHUNK)], axis=1
                )
                accum = accum + jnp.dot(keys_flat, grad_scores, preferred_element_type=F32)
                lanes = pl.ds(base * TOK, CHUNK * TOK)
                dkv_acc[0:HEAD, lanes] += across(queries, grad_scores)
                dkv_acc[HEAD : 2 * HEAD, lanes] += across(grads, probs.astype(BF))
            part = accum.astype(BF)
            first = pl.multiple_of(h * HEAD, HEAD)
            for a in range(QG):
                dq_buf[a, pl.ds(first, HEAD), :] = part[:, a * TOK : (a + 1) * TOK]
            return unused

        lax.fori_loop(0, 3, one, 0)
        for j in range(KG):
            dkv_buf[j, pl.ds(g * 128, 128), :] = dkv_acc[:, j * TOK : (j + 1) * TOK].astype(BF)
        rows = pl.ds(g * 128, 128)
        for o in range(1, KG):
            j, device = key_peers[o - 1]
            c = remote(
                dkv_buf.at[j, rows], dkv_got.at[plane, rows], dkv_send.at[o, g], dkv_recv.at[o, g], device
            )
            c.start()
            sends.append(c)
        rows = pl.ds(g * 192, 192)
        for o in range(1, QG):
            a, device = query_peers[o - 1]
            c = remote(
                dq_buf.at[a, rows], dq_got.at[mine, rows], dq_send.at[o, g], dq_recv.at[o, g], device
            )
            c.start()
            sends.append(c)
        if g == 1:
            for c in d_sends:
                c.wait_recv()
            for j in range(KG):
                total = rd[0, j].astype(F32)
                for s in range(1, 4):
                    total = total + rd[s, j].astype(F32)
                gp[j] = total.astype(BF)
            for o in range(1, KG):
                j, device = key_peers[o - 1]
                p_sends.append(remote(gp.at[j], rp.at[plane], p_send.at[o], p_recv.at[o], device))
            for c in p_sends:
                c.start()
            rp[plane] = gp[plane]
    dq_got[mine] = dq_buf[mine]
    dkv_got[plane] = dkv_buf[plane]
    for c in p_sends:
        c.wait_recv()
    fd_ref[core] = sum_pieces(rp, KG, slice(0, 32))
    final = remote(fd_ref.at[core], fd_ref.at[core], f_send, f_recv, sibling)
    final.start()
    for c in a_sends:
        c.wait_recv()

    def add(i, unused):
        rows = pl.ds(pl.multiple_of(i * 16, 16), 16)
        sa_ref[rows, :] = sum_pieces(ra, KG, rows).astype(BF)
        return unused

    lax.fori_loop(0, GROWS // 16, add, 0)
    for c in sends:
        c.wait_recv()
    total = dq_got[0].astype(F32)
    for a in range(1, QG):
        total = total + dq_got[a].astype(F32)
    dq_ref[...] = total
    total = dkv_got[0].astype(F32)
    for j in range(1, KG):
        total = total + dkv_got[j].astype(F32)
    dkv_ref[...] = total
    final.wait_recv()
    final.wait_send()
    for c in copies + sends + to_sibling + d_sends + a_sends + p_sends:
        c.wait_send()


def attention_backward(do_block, st_block, q_all, kv_all, kv_tok, x, inner, y, yd):
    dma = pltpu.SemaphoreType.DMA
    return pl.pallas_call(
        backward_kernel,
        out_shape=[
            jax.ShapeDtypeStruct((D, TOK), F32),
            jax.ShapeDtypeStruct((384, TOK), F32),
            jax.ShapeDtypeStruct((GROWS, WIDE), BF),
            jax.ShapeDtypeStruct((2, 32, QUARTER), F32),
        ],
        in_specs=[VM] * 9,
        out_specs=[VM] * 4,
        scratch_shapes=[
            pltpu.VMEM((QG, D, TOK), BF),
            pltpu.VMEM((QG, 32, TOK), F32),
            pltpu.VMEM((QG, D, TOK), BF),
            pltpu.VMEM((128, KG * TOK), F32),
            pltpu.VMEM((KG, 384, TOK), BF),
            pltpu.VMEM((QG, D, TOK), BF),
            pltpu.VMEM((KG, 384, TOK), BF),
            pltpu.VMEM((2 * TOK, 2 * WIDE), BF),
            pltpu.VMEM((2 * TOK, 2 * QUARTER), BF),
            pltpu.VMEM((GYROWS, 2 * TOK), BF),
            pltpu.VMEM((1024, 2 * TOK), BF),
            pltpu.VMEM((KG, GROWS, WIDE), BF),
            pltpu.VMEM((KG, GROWS, WIDE), BF),
            pltpu.VMEM((2, 2, KG, 32, QUARTER), BF),
            pltpu.VMEM((4, KG, 32, QUARTER), BF),
            pltpu.VMEM((KG, 32, QUARTER), BF),
            pltpu.VMEM((KG, 32, QUARTER), BF),
            dma((QG,)),
            dma((QG,)),
            dma((QG,)),
            dma((QG,)),
            dma((QG, KV_HEADS)),
            dma((QG, KV_HEADS)),
            dma((KG, KV_HEADS)),
            dma((KG, KV_HEADS)),
            dma((4,)),
            dma((4,)),
            dma((KG,)),
            dma((KG,)),
            dma((3,)),
            dma((3,)),
            dma((KG,)),
            dma((KG,)),
            dma,
            dma,
        ],
        compiler_params=params(2),
    )(do_block, st_block, q_all, kv_all, kv_tok, x, inner, y, yd)


AROWS = 32 + GROWS


def reduce_kernel(
    x_ref, y_ref, gn_ref, sa_ref, fa_ref,
    x_all, y_all, gn_all, gq, rq, sq, wa, wq,
    sib_send, sib_recv, q_send, q_recv, wa_send, wa_recv, wq_send, wq_recv, f_send, f_recv,
):
    dp, x_hi, plane, core = place()
    sibling = (dp, ctx_of(x_hi, plane, 1 - core))
    line = []
    for flip_dp in range(2):
        for flip_x in range(2):
            for flip_core in range(2):
                if flip_dp + flip_x + flip_core:
                    line.append(
                        (
                            (dp + flip_dp) % 2,
                            ctx_of((x_hi + flip_x) % 2, plane, (core + flip_core) % 2),
                        )
                    )
    peers = []
    for o in range(1, KG):
        j = plane_peer(plane, o)
        peers.append((j, (dp, ctx_of(x_hi, j, core))))
    greet(line + [d for _, d in peers])
    own, late = pl.ds(0, TOK), pl.ds(TOK, TOK)
    to_sibling = [
        remote(x_ref, x_all.at[late], sib_send.at[0], sib_recv.at[0], sibling),
        remote(y_ref.at[1 - core], y_all.at[:, late], sib_send.at[1], sib_recv.at[1], sibling),
        remote(gn_ref, gn_all, sib_send.at[2], sib_recv.at[2], sibling),
    ]
    for c in to_sibling:
        c.start()
    slot = dp * 2 + x_hi
    collector = core == x_hi

    def toward(target_dp, src, dst, send, recv):
        device = (target_dp, ctx_of(core, plane, core))
        lanes = pl.ds(pl.multiple_of(target_dp * 256, 128), QUARTER)
        return remote(src.at[:, lanes], dst.at[slot], send.at[target_dp], recv.at[slot], device)

    def pass_on(src, dst, send, recv):
        for target_dp in range(2):
            here = jnp.logical_and(collector, dp == target_dp)

            @pl.when(jnp.logical_not(here))
            def _():
                toward(target_dp, src, dst, send, recv).start()

            @pl.when(here)
            def _():
                dst[slot] = src[:, target_dp * 256 : target_dp * 256 + QUARTER]

    pass_on(sa_ref, wa, wa_send, wa_recv)
    x_all[own, :] = x_ref[...]
    y_all[:, own] = y_ref[core]
    for c in to_sibling:
        c.wait_recv()
    row = lax.broadcasted_iota(jnp.int32, (KG, 32, WIDE), 1)
    sums = gn_ref[...] + gn_all[...]
    part = jnp.dot(y_all[...], x_all[...], preferred_element_type=F32).reshape(KG, 32, WIDE)
    part = jnp.where(row == 30, sums[0:1][None], part)
    part = jnp.where(row == 31, sums[1:2][None], part)
    gq[...] = part.astype(BF)
    sends = []
    for o in range(1, KG):
        j, device = peers[o - 1]
        sends.append(remote(gq.at[j], rq.at[plane], q_send.at[o], q_recv.at[o], device))
    for c in sends:
        c.start()
    rq[plane] = gq[plane]
    for c in sends:
        c.wait_recv()
    sq[...] = sum_pieces(rq, KG, slice(0, 32)).astype(BF)
    pass_on(sq, wq, wq_send, wq_recv)
    final = remote(fa_ref, fa_ref, f_send, f_recv, sibling)

    @pl.when(collector)
    def _():
        for source in range(4):

            @pl.when(slot != source)
            def _():
                for src, dst, send, recv in (
                    (sa_ref, wa, wa_send, wa_recv),
                    (sq, wq, wq_send, wq_recv),
                ):
                    remote(
                        src.at[:, pl.ds(0, QUARTER)], dst.at[source], send.at[0], recv.at[source], sibling
                    ).wait_recv()

        fa_ref[pl.ds(0, 32), :] = sum_pieces(wq, 4, slice(0, 32))
        fa_ref[pl.ds(32, GROWS), :] = sum_pieces(wa, 4, slice(0, GROWS))
        final.start()
        final.wait_send()

    @pl.when(jnp.logical_not(collector))
    def _():
        final.wait_recv()

    for target_dp in range(2):

        @pl.when(jnp.logical_not(jnp.logical_and(collector, dp == target_dp)))
        def _():
            toward(target_dp, sa_ref, wa, wa_send, wa_recv).wait_send()
            toward(target_dp, sq, wq, wq_send, wq_recv).wait_send()

    for c in to_sibling + sends:
        c.wait_send()


def reduce_weights(x, y, gain_terms, sums):
    dma = pltpu.SemaphoreType.DMA
    return pl.pallas_call(
        reduce_kernel,
        out_shape=jax.ShapeDtypeStruct((AROWS, QUARTER), F32),
        in_specs=[VM] * 4,
        out_specs=VM,
        scratch_shapes=[
            pltpu.VMEM((2 * TOK, WIDE), BF),
            pltpu.VMEM((512, 2 * TOK), BF),
            pltpu.VMEM((8, WIDE), F32),
            pltpu.VMEM((KG, 32, WIDE), BF),
            pltpu.VMEM((KG, 32, WIDE), BF),
            pltpu.VMEM((32, WIDE), BF),
            pltpu.VMEM((4, GROWS, QUARTER), BF),
            pltpu.VMEM((4, 32, QUARTER), BF),
            dma((3,)),
            dma((3,)),
            dma((KG,)),
            dma((KG,)),
            dma((2,)),
            dma((4,)),
            dma((2,)),
            dma((4,)),
            dma,
            dma,
        ],
        compiler_params=params(3),
    )(x, y, gain_terms, sums)


def times_back(left, right):
    return lax.dot_general(left, right, (((1,), (1,)), ((), ())), preferred_element_type=F32)


def flat(weight, tokens):
    return lax.dot_general(weight, tokens, (((0,), (1,)), ((), ())), preferred_element_type=F32)


def unflat(rows, weight):
    return lax.dot_general(rows, weight, (((0,), (1,)), ((), ())), preferred_element_type=F32)


def rope_flat(rows, heads, cosine, sine, sign):
    parts = rows.reshape(heads, 2, HEAD // 2, TOK)
    one, two = parts[:, 0], parts[:, 1]
    first = one * cosine - sign * two * sine
    second = two * cosine + sign * one * sine
    return jnp.stack([first, second], axis=1)


def by_chip(rows):
    return rows.reshape(32, rows.shape[0] // 32, TOK)


def local(
    hidden, positions, w_query, w_key, w_value, w_out, w_gate, w_up, w_down,
    gain_attn, gain_ffn, grad_out,
):
    dp, x_hi, plane, core = place()
    gains = jnp.pad(jnp.concatenate([gain_attn, gain_ffn], axis=0), ((0, 14), (0, 96)))
    wq, wk, wv, gains = gather_weights([w[0] for w in (w_query, w_key, w_value)], gains)
    gains = jnp.concatenate([gains[0, :2, :288], gains[1, :2, :288]], axis=1).astype(F32)
    gain_one, gain_two = gains[0:1], gains[1:2]
    state = hidden[0].astype(F32)
    scale_one = lax.rsqrt(jnp.mean(state * state, axis=-1, keepdims=True) + eps)
    unit_one = state * scale_one
    normal_one = (unit_one * gain_one).astype(BF)
    places = positions[0]
    freqs = rope_base ** (-(jnp.arange(HEAD // 2, dtype=F32) * 2.0 / HEAD))
    angles = freqs[:, None] * places.astype(F32)[None, :]
    cosine, sine = jnp.cos(angles), jnp.sin(angles)
    run = (places[0] // TOK).astype(BF)
    run_rows = jnp.full((16, TOK), run, BF)
    query = rope_flat(flat(wq, normal_one), HEADS, cosine, sine, 1.0).astype(BF)
    query = query.reshape(D, TOK) * jnp.asarray(0.125, BF)
    keys = rope_flat(flat(wk, normal_one), KV_HEADS, cosine, sine, 1.0).astype(BF)
    keys = keys.reshape(KV_HEADS, HEAD, TOK)
    values = flat(wv, normal_one).astype(BF).reshape(KV_HEADS, HEAD, TOK)
    kv_block = jnp.concatenate([keys, values], axis=1).reshape(384, TOK)
    o_rows, lse, q_all, kv_all, kv_tok, wo, wg, wu, wd = attention_forward(
        jnp.concatenate([query, run_rows], axis=0),
        jnp.concatenate([kv_block, run_rows], axis=0),
        [w[0] for w in (w_out, w_gate, w_up, w_down)],
    )
    attended = o_rows.T.astype(BF)
    middle = state + jnp.dot(attended, wo, preferred_element_type=F32)
    scale_two = lax.rsqrt(jnp.mean(middle * middle, axis=-1, keepdims=True) + eps)
    unit_two = middle * scale_two
    normal_two = (unit_two * gain_two).astype(BF)
    gate = jnp.dot(normal_two, wg, preferred_element_type=F32)
    upper = jnp.dot(normal_two, wu, preferred_element_type=F32)
    inner = (jax.nn.silu(gate) * upper).astype(BF)
    output = (middle + jnp.dot(inner, wd, preferred_element_type=F32)).astype(BF)

    grad_low = grad_out[0]
    grad = grad_low.astype(F32)
    grad_inner = times_back(grad_low, wd)
    sigma = jax.nn.sigmoid(gate)
    grad_gate_low = (grad_inner * upper * sigma * (1.0 + gate * (1.0 - sigma))).astype(BF)
    grad_up_low = (grad_inner * gate * sigma).astype(BF)
    grad_normal = times_back(grad_gate_low, wg) + times_back(grad_up_low, wu)
    gain_ffn_term = jnp.sum(grad_normal * unit_two, axis=0)
    grad_unit = grad_normal * gain_two
    grad_middle = (
        scale_two * (grad_unit - unit_two * jnp.mean(grad_unit * unit_two, axis=-1, keepdims=True))
        + grad
    )
    branch_low = grad_middle.astype(BF)
    do_block = times_back(wo, branch_low).astype(BF)
    delta = jnp.sum((do_block.astype(F32) * o_rows).reshape(HEADS, HEAD, TOK), axis=1)
    st_block = jnp.concatenate([lse, jnp.pad(delta, ((0, 7), (0, 0)))], axis=0)
    wide = ((0, 0), (0, WIDE - D))
    blank = lambda rows: jnp.zeros((32, rows, TOK), BF)
    x = jnp.concatenate([jnp.pad(attended, wide), jnp.pad(normal_two, wide)], axis=1)
    inner_parts = jnp.stack(
        [
            jnp.concatenate([inner[:, q : q + QUARTER], inner[:, 768 + q : 768 + q + QUARTER]], axis=1)
            for q in (0, QUARTER)
        ]
    )
    o_part = jnp.concatenate([by_chip(branch_low.T), blank(14)], axis=1).reshape(2, 512, TOK)
    down_part = jnp.concatenate([by_chip(grad_low.T), blank(14)], axis=1).reshape(1024, TOK)
    y = jnp.concatenate(
        [o_part, grad_gate_low.T.reshape(2, 768, TOK), grad_up_low.T.reshape(2, 768, TOK)], axis=1
    )
    dq_rows, dkv_rows, sums, fd = attention_backward(
        do_block, st_block, q_all, kv_all, kv_tok, x, inner_parts, y, down_part
    )
    dq_rows = rope_flat(dq_rows * 0.125, HEADS, cosine, sine, -1.0).astype(BF).reshape(D, TOK)
    dkv_rows = dkv_rows.reshape(KV_HEADS, 2, HEAD, TOK)
    dk_rows = rope_flat(dkv_rows[:, 0].reshape(192, TOK), KV_HEADS, cosine, sine, -1.0)
    dk_rows = dk_rows.astype(BF).reshape(192, TOK)
    dv_rows = dkv_rows[:, 1].reshape(192, TOK).astype(BF)
    grad_first = unflat(dq_rows, wq) + unflat(dk_rows, wk) + unflat(dv_rows, wv)
    gain_attn_term = jnp.sum(grad_first * unit_one, axis=0)
    grad_unit_one = grad_first * gain_one
    grad_input = (
        scale_one
        * (grad_unit_one - unit_one * jnp.mean(grad_unit_one * unit_one, axis=-1, keepdims=True))
        + grad_middle
    )

    qkv_rows = jnp.concatenate(
        [by_chip(dq_rows), by_chip(dk_rows), by_chip(dv_rows), blank(2)], axis=1
    ).reshape(2, 512, TOK)
    gain_terms = jnp.pad(jnp.stack([gain_attn_term, gain_ffn_term]), ((0, 6), (0, WIDE - D)))
    fa = reduce_weights(jnp.pad(normal_one, wide), qkv_rows, gain_terms, sums)
    fd = jnp.concatenate([fd[0], fd[1]], axis=1)
    fa = lax.dynamic_slice(fa, (0, dp * 32), (AROWS, 288))

    def mine_of(rows, first, count):
        part = lax.dynamic_slice_in_dim(rows, first + core * count, count, 0)
        return part.T[None]

    return (
        output[None],
        grad_input[None],
        mine_of(fa, 0, 9),
        mine_of(fa, 18, 3),
        mine_of(fa, 24, 3),
        mine_of(fa, 32, 9),
        mine_of(fa, 64, 24),
        mine_of(fa, 112, 24),
        mine_of(fd, 0, 9),
        fa[30][None],
        fa[31][None],
    )


def solution(mesh):
    in_specs = (
        P("dp", "ctx", None),
        P("dp", "ctx"),
    ) + (P(None, "dp", None),) * 7 + (
        P(None, "dp"),
        P(None, "dp"),
        P("dp", "ctx", None),
    )
    out_specs = (
        P("dp", "ctx", None),
        P("dp", "ctx", None),
    ) + (P(None, "dp", "ctx"),) * 7 + (
        P(None, "dp"),
        P(None, "dp"),
    )
    return jax.shard_map(local, mesh=mesh, in_specs=in_specs, out_specs=out_specs, check_vma=False)
```

```python
import functools

import jax
import jax.numpy as jnp
import numpy as np
from jax import lax
from jax.experimental import pallas as pl
from jax.experimental.pallas import tpu as pltpu
from jax.sharding import PartitionSpec as P

HEADS = 9
KV_HEADS = 3
HEAD = 64
TOK = 128
D = 576
FF = 1536
QG = 4
KG = 16
WIDE = 640
eps = 1e-05
rope_base = 100000.0
MESH = pl.DeviceIdType.MESH
BF = jnp.bfloat16
F32 = jnp.float32
LIMIT = 56 * 1024 * 1024
VM = pl.BlockSpec(memory_space=pltpu.VMEM)
ANY = pl.BlockSpec(memory_space=pl.ANY)


def params(ident):
    return pltpu.CompilerParams(
        collective_id=ident, has_side_effects=True, vmem_limit_bytes=LIMIT
    )


def place():
    dp = lax.axis_index("dp")
    ctx = lax.axis_index("ctx")
    x_hi = ctx // 32
    plane = (ctx // 2) % 16
    core = ctx % 2
    return dp, x_hi, plane, core


def ctx_of(x_hi, plane, core):
    return x_hi * 32 + plane * 2 + core


def remote(src, dst, send, recv, device):
    return pltpu.make_async_remote_copy(
        src_ref=src,
        dst_ref=dst,
        send_sem=send,
        recv_sem=recv,
        device_id=device,
        device_id_type=MESH,
    )


def greet(devices):
    barrier = pltpu.get_barrier_semaphore()
    for device in devices:
        pl.semaphore_signal(barrier, inc=1, device_id=device, device_id_type=MESH)
    pl.semaphore_wait(barrier, len(devices))


def plane_peer(plane, offset):
    y, z = plane // 4, plane % 4
    return ((y + offset // 4) % 4) * 4 + (z + offset % 4) % 4


def plane_source(plane, offset):
    y, z = plane // 4, plane % 4
    return ((y + 4 - offset // 4) % 4) * 4 + (z + 4 - offset % 4) % 4


def weight_copies(shards, fulls, own_sem, send, recv, core_send, core_recv):
    dp, x_hi, plane, core = place()
    near = (1 - dp, ctx_of(x_hi, plane, core))
    far = (1 - dp, ctx_of(1 - x_hi, plane, core))
    sibling = (dp, ctx_of(x_hi, plane, 1 - core))
    own, first, second = [], [], []
    for which, (shard, full) in enumerate(zip(shards, fulls)):
        rows = shard.shape[0]
        half = rows // 2
        cut = 80 if rows == 288 else half // 2
        by_rows = full.shape[0] != rows

        def part(dp_of, off, size):
            if by_rows:
                return full.at[pl.ds(pl.multiple_of(dp_of * rows + off, 16), size)]
            width = shard.shape[1]
            return full.at[
                pl.ds(pl.multiple_of(off, 16), size), pl.ds(pl.multiple_of(dp_of * width, 128), width)
            ]

        own.append(pltpu.make_async_copy(shard, part(dp, 0, rows), own_sem.at[which]))
        for role, target in ((0, near), (1, far)):
            off = pl.multiple_of(role * cut + core * half, 16)
            size = half - cut if role else cut
            first.append(
                remote(
                    shard.at[pl.ds(off, size)],
                    part(dp, off, size),
                    send.at[which, role],
                    recv.at[which, role],
                    target,
                )
            )
            got = part(1 - dp, off, size)
            second.append(
                remote(got, got, core_send.at[which, role], core_recv.at[which, role], sibling)
            )
    return own, first, second


def weight_sems(count):
    return [pltpu.SemaphoreType.DMA((count,))] + [pltpu.SemaphoreType.DMA((count, 2))] * 4


QROWS = D + 16
KROWS = 384 + 16
CHUNK = 4


def groups():
    dp, x_hi, plane, core = place()
    mine = x_hi * 2 + core
    query_peers = []
    for o in range(1, QG):
        a = (mine + o) % QG
        query_peers.append((a, (dp, ctx_of(a // 2, plane, a % 2))))
    key_peers = []
    for o in range(1, KG):
        j = plane_peer(plane, o)
        key_peers.append((j, (dp, ctx_of(x_hi, j, core))))
    return mine, plane, query_peers, key_peers


def flip_keys(kv_all, kv_tok, j):
    for g in range(KV_HEADS):
        block = kv_all[j, pl.ds(g * 128, 128), :].astype(F32)
        kv_tok[g, pl.ds(pl.multiple_of(j * TOK, TOK), TOK), :] = block.T.astype(BF)


def masks_of(q_all, kv_all, base):
    lane = lax.broadcasted_iota(jnp.int32, (1, TOK), 1).astype(F32)
    q_pos = jnp.concatenate(
        [q_all[a, pl.ds(D, 16), :].astype(F32)[0:1] * TOK + lane for a in range(QG)], axis=1
    )
    rows = lax.broadcasted_iota(jnp.int32, (TOK, QG * TOK), 0).astype(F32)
    parts = []
    for b in range(CHUNK):
        start = kv_all[base + b, pl.ds(384, 16), :].astype(F32)[0:1] * TOK
        start = jnp.concatenate([start] * QG, axis=1)
        parts.append(rows <= (q_pos - start))
    return jnp.concatenate(parts, axis=0)


def head_rows(ref, h):
    first = pl.multiple_of(h * HEAD, HEAD)
    return jnp.concatenate([ref[a, pl.ds(first, HEAD), :] for a in range(QG)], axis=1)


def scores_of(q_all, kv_all, kv_tok, g, base, queries, zeros):
    keys = kv_tok[g, pl.ds(pl.multiple_of(base * TOK, TOK), CHUNK * TOK), :]
    scores = jnp.dot(keys, jnp.concatenate([queries, zeros], axis=0), preferred_element_type=F32)
    return keys, jnp.where(masks_of(q_all, kv_all, base), scores, -1e30)


def turn(rows, heads, cosine, sine, sign):
    parts = rows.reshape(heads, 2, HEAD // 2, TOK)
    one, two = parts[:, 0], parts[:, 1]
    first = one * cosine - sign * two * sine
    second = two * cosine + sign * one * sine
    return jnp.concatenate([first[:, None], second[:, None]], axis=1)


def flipped(rows):
    wide = (rows.shape[1] + 127) // 128 * 128
    if wide != rows.shape[1]:
        rows = jnp.concatenate(
            [rows, jnp.zeros((rows.shape[0], wide - rows.shape[1]), rows.dtype)], axis=1
        )
    return rows.T


def gain_rows(row):
    return jnp.broadcast_to(row, (TOK, WIDE)).T[0:D]


def forward_kernel(count, *refs):
    h_ref, pos_ref, run_cos, run_sin, in_cos, in_sin, gain_a, gain_f = refs[:8]
    shards = refs[8 : 8 + count]
    refs = refs[8 + count :]
    o_ref, lse_ref, q_all, kv_all, kv_tok, x_one, gains, tables = refs[:8]
    fulls = refs[8 : 8 + count]
    refs = refs[8 + count :]
    (
        accum_all, top_all, total_all, o_buf, st_buf, o_got, st_got, gain_own, gain_got,
        gain_send, gain_recv,
        q_send, q_recv, kv_send, kv_recv, o_send, o_recv, st_send, st_recv,
    ) = refs[:19]
    mine, plane, query_peers, key_peers = groups()
    dp, x_hi, plane, core = place()
    near = (1 - dp, ctx_of(x_hi, plane, core))
    greet(
        [d for _, d in query_peers]
        + [d for _, d in key_peers]
        + [near, (1 - dp, ctx_of(1 - x_hi, plane, core))]
    )
    own_w, first_w, second_w = weight_copies(shards, fulls, *refs[19:])
    gain_own[...] = jnp.zeros_like(gain_own)
    gain_own[0:1, 0:288] = gain_a[...].astype(F32)
    gain_own[1:2, 0:288] = gain_f[...].astype(F32)
    placed = gain_own[...]
    gain_own[...] = jnp.where(dp == 0, placed, pltpu.roll(placed, 288, 1))
    gain_copy = remote(gain_own, gain_got, gain_send, gain_recv, near)
    gain_copy.start()
    for c in first_w[:6] + own_w:
        c.start()
    state = h_ref[...].astype(F32)
    scale = lax.rsqrt(jnp.mean(state * state, axis=0, keepdims=True) + eps)
    unit = state * scale
    run = pos_ref[0:1, 0:1].astype(F32) * (1.0 / TOK)
    lane = lax.broadcasted_iota(jnp.int32, (HEAD // 2, 64), 1).astype(F32)
    at_run = lane == run
    cos_a = jnp.sum(jnp.where(at_run, run_cos[...], 0.0), axis=1, keepdims=True)
    sin_a = jnp.sum(jnp.where(at_run, run_sin[...], 0.0), axis=1, keepdims=True)
    cosine = cos_a * in_cos[...] - sin_a * in_sin[...]
    sine = sin_a * in_cos[...] + cos_a * in_sin[...]
    tables[0] = cosine
    tables[1] = sine
    gain_copy.wait_recv()
    gains[...] = gain_own[...] + gain_got[...]
    normal = flipped((unit * gain_rows(gains[0:1, :])).astype(BF).astype(F32)).astype(BF)
    x_one[...] = jnp.zeros_like(x_one)
    x_one[:, 0:D] = normal
    for c, d in zip(first_w[:6], second_w[:6]):
        c.wait_recv()
        d.start()
    for c in own_w[:3]:
        c.wait()
    for c in second_w[:6]:
        c.wait_recv()
    wq, wk, wv = fulls[:3]
    run_rows = jnp.broadcast_to(run, (16, TOK)).astype(BF)
    keys = flipped(jnp.dot(normal, wk[...], preferred_element_type=F32))[0:192]
    keys = turn(keys, KV_HEADS, cosine, sine, 1.0).astype(BF).reshape(192, TOK)
    values = flipped(jnp.dot(normal, wv[...], preferred_element_type=F32))[0:192].astype(BF)
    for g in range(KV_HEADS):
        kv_all[plane, g * 128 : g * 128 + HEAD, :] = keys[g * HEAD : (g + 1) * HEAD]
        kv_all[plane, g * 128 + HEAD : (g + 1) * 128, :] = values[g * HEAD : (g + 1) * HEAD]
    kv_all[plane, 384:400, :] = run_rows
    q_copies, kv_copies = [], [None]
    own_kv, own_q = kv_all.at[plane], q_all.at[mine]
    for o in range(1, KG):
        kv_copies.append(remote(own_kv, own_kv, kv_send.at[o], kv_recv.at[o], key_peers[o - 1][1]))
    for c in kv_copies[1:]:
        c.start()
    query = flipped(jnp.dot(normal, wq[...], preferred_element_type=F32))[0:D]
    query = turn(query, HEADS, cosine, sine, 1.0).astype(BF).reshape(D, TOK)
    q_all[mine, 0:D, :] = query * jnp.asarray(0.125, BF)
    q_all[mine, D:QROWS, :] = run_rows
    for o in range(1, QG):
        q_copies.append(remote(own_q, own_q, q_send.at[o], q_recv.at[o], query_peers[o - 1][1]))
    for c in q_copies + first_w[6:]:
        c.start()
    copies = q_copies + kv_copies[1:]
    for c in q_copies:
        c.wait_recv()
    zeros = jnp.zeros((HEAD, QG * TOK), BF)
    o_copies = []
    for step in range(4):
        base = ((plane // 4 + 4 - step) % 4) * 4
        for dz in range(4):
            if step * 4 + dz:
                kv_copies[step * 4 + dz].wait_recv()

        def flip(b, unused, base=base):
            flip_keys(kv_all, kv_tok, base + b)
            return unused

        lax.fori_loop(0, 4, flip, 0)

        def one(h, unused, step=step, base=base):
            g = h // 3
            first = pl.multiple_of(h * HEAD, HEAD)
            queries = head_rows(q_all, h)
            keys, scores = scores_of(q_all, kv_all, kv_tok, g, base, queries, zeros)
            new_top = jnp.max(scores, axis=0, keepdims=True)
            if step:
                top = top_all[pl.ds(h, 1), :]
                new_top = jnp.maximum(top, new_top)
            probs = jnp.exp(scores - new_top)
            total = jnp.sum(probs, axis=0, keepdims=True)
            value_rows = pl.ds(pl.multiple_of(g * 128 + HEAD, HEAD), HEAD)
            values = jnp.concatenate(
                [kv_all[base + b, value_rows, :] for b in range(CHUNK)], axis=1
            )
            accum = jnp.dot(values, probs.astype(BF), preferred_element_type=F32)
            if step:
                fade = jnp.exp(top - new_top)
                total = total + total_all[pl.ds(h, 1), :] * fade
                accum = accum + accum_all[pl.ds(first, HEAD), :] * fade
            if step < 3:
                top_all[pl.ds(h, 1), :] = new_top
                total_all[pl.ds(h, 1), :] = total
                accum_all[pl.ds(first, HEAD), :] = accum
                return unused
            part = (accum / total).astype(BF)
            for a in range(QG):
                lanes = slice(a * TOK, (a + 1) * TOK)
                o_buf[a, pl.ds(first, HEAD), :] = part[:, lanes]
                st_buf[a, pl.ds(h, 1), :] = new_top[:, lanes]
                st_buf[a, pl.ds(h + 16, 1), :] = total[:, lanes]
            return unused

        if step < 3:
            lax.fori_loop(0, HEADS, one, 0)
            if step == 1:
                for c, d in zip(first_w[6:], second_w[6:]):
                    c.wait_recv()
                    d.start()
            continue
        for g in range(KV_HEADS):
            lax.fori_loop(3 * g, 3 * g + 3, one, 0)
            rows = pl.ds(g * 192, 192)
            for o in range(1, QG):
                a, device = query_peers[o - 1]
                c = remote(
                    o_buf.at[a, rows], o_got.at[mine, rows], o_send.at[o, g], o_recv.at[o, g], device
                )
                c.start()
                o_copies.append(c)
    for o in range(1, QG):
        a, device = query_peers[o - 1]
        c = remote(st_buf.at[a], st_got.at[mine], st_send.at[o], st_recv.at[o], device)
        c.start()
        o_copies.append(c)
    o_got[mine] = o_buf[mine]
    st_got[mine] = st_buf[mine]
    for c in own_w[3:]:
        c.wait()
    for c in second_w[6:]:
        c.wait_recv()
    for c in first_w + second_w:
        c.wait_send()
    for c in o_copies:
        c.wait_recv()
    lse_ref[...] = jnp.zeros_like(lse_ref)
    for h in range(HEADS):
        tops = [st_got[a, pl.ds(h, 1), :] for a in range(QG)]
        best = jnp.maximum(jnp.maximum(tops[0], tops[1]), jnp.maximum(tops[2], tops[3]))
        shares = [st_got[a, pl.ds(h + 16, 1), :] * jnp.exp(tops[a] - best) for a in range(QG)]
        whole = shares[0] + shares[1] + shares[2] + shares[3]
        lse_ref[pl.ds(h, 1), :] = best + jnp.log(whole)
        result = jnp.zeros((HEAD, TOK), F32)
        for a in range(QG):
            result = result + o_got[a, pl.ds(h * HEAD, HEAD), :].astype(F32) * (shares[a] / whole)
        o_ref[pl.ds(h * HEAD, HEAD), :] = result
    for c in copies + o_copies + [gain_copy]:
        c.wait_send()


def attention_forward(hidden, positions, gain_attn, gain_ffn, shards):
    count = len(shards)
    dma = pltpu.SemaphoreType.DMA
    shape = jax.ShapeDtypeStruct
    fulls = [
        shape((2 * s.shape[0], s.shape[1]) if s.shape[0] == 288 else (D, FF), s.dtype)
        for s in shards
    ]
    freqs = rope_base ** (-(np.arange(HEAD // 2, dtype=np.float64) * 2.0 / HEAD))[:, None]
    runs = freqs * (np.arange(64, dtype=np.float64) * TOK)[None]
    inside = freqs * np.arange(TOK, dtype=np.float64)[None]
    tables = [f(a).astype(np.float32) for a in (runs, inside) for f in (np.cos, np.sin)]
    return pl.pallas_call(
        functools.partial(forward_kernel, count),
        out_shape=[
            shape((D, TOK), F32),
            shape((16, TOK), F32),
            shape((QG, QROWS, TOK), BF),
            shape((KG, KROWS, TOK), BF),
            shape((KV_HEADS, KG * TOK, 128), BF),
            shape((TOK, WIDE), BF),
            shape((8, WIDE), F32),
            shape((2, HEAD // 2, TOK), F32),
        ]
        + fulls,
        in_specs=[VM] * (8 + count),
        out_specs=[VM] * (8 + count),
        scratch_shapes=[
            pltpu.VMEM((D, QG * TOK), F32),
            pltpu.VMEM((16, QG * TOK), F32),
            pltpu.VMEM((16, QG * TOK), F32),
            pltpu.VMEM((QG, D, TOK), BF),
            pltpu.VMEM((QG, 32, TOK), F32),
            pltpu.VMEM((QG, D, TOK), BF),
            pltpu.VMEM((QG, 32, TOK), F32),
            pltpu.VMEM((8, WIDE), F32),
            pltpu.VMEM((8, WIDE), F32),
            dma,
            dma,
            dma((QG,)),
            dma((QG,)),
            dma((KG,)),
            dma((KG,)),
            dma((QG, KV_HEADS)),
            dma((QG, KV_HEADS)),
            dma((QG,)),
            dma((QG,)),
        ]
        + weight_sems(count),
        compiler_params=params(1),
    )(hidden, positions, *[jnp.asarray(t) for t in tables], gain_attn, gain_ffn, *shards)


def across(left, right):
    return lax.dot_general(left, right, (((1,), (1,)), ((), ())), preferred_element_type=F32)


GROWS = 128
GYROWS = 2048
AROWS = 32 + GROWS
QUARTER = 384


def line_peers():
    dp, x_hi, plane, core = place()
    return [
        ((dp + d) % 2, (x_hi + x) % 2, ((dp + d) % 2, ctx_of((x_hi + x) % 2, plane, core)))
        for d, x in ((1, 0), (0, 1), (1, 1))
    ]


def sum_pieces(pieces, count, rows):
    total = pieces[0, rows, :].astype(F32)
    for i in range(1, count):
        total = total + pieces[i, rows, :].astype(F32)
    return total


def backward_kernel(
    do_ref, st_ref, q_all, kv_all, kv_tok, x_ref, in_ref, y_ref, yd_ref,
    h_ref, back_ref, wq_ref, wk_ref, wv_ref, x_one, gains, tables, gain_term,
    grad_ref, fa_ref, fd_ref,
    do_all, st_all, dq_buf, dkv_acc, dkv_buf, dq_got, dkv_got,
    x_all, in_all, y_all, yd_all, g1, g2, r1, r2, s1, s2, t1, t2, gd, rd, gp, rp,
    one_all, yq_own, yq_all, gn_own, gn_all, gq, rq, sq, sa_ref, wa, wb, spread,
    do_send, do_recv, st_send, st_recv, dq_send, dq_recv, dkv_send, dkv_recv,
    sib_send, sib_recv, a_send, a_recv, b_send, b_recv, d_send, d_recv, p_send, p_recv,
    f_send, f_recv, tail_send, tail_recv, q_send, q_recv,
    wa_send, wa_recv, wb_send, wb_recv, last_send, last_recv,
):
    dp, x_hi, plane, core = place()
    mine, plane, query_peers, key_peers = groups()
    line = line_peers()
    sibling = (dp, ctx_of(x_hi, plane, 1 - core))
    others = [(1 - dp, ctx_of((x_hi + x) % 2, plane, (core + c) % 2)) for x in range(2) for c in range(2)]
    greet([d for _, d in query_peers] + [d for _, d in key_peers] + others)
    own, late = pl.ds(0, TOK), pl.ds(TOK, TOK)
    to_sibling = [
        remote(x_ref, x_all.at[late], sib_send.at[0], sib_recv.at[0], sibling),
        remote(in_ref.at[1 - core], in_all.at[late], sib_send.at[1], sib_recv.at[1], sibling),
        remote(y_ref.at[1 - core], y_all.at[:, late], sib_send.at[2], sib_recv.at[2], sibling),
        remote(yd_ref, yd_all.at[:, late], sib_send.at[3], sib_recv.at[3], sibling),
        remote(x_one, one_all.at[late], sib_send.at[4], sib_recv.at[4], sibling),
    ]
    copies = []
    for o in range(1, QG):
        device = query_peers[o - 1][1]
        copies.append(remote(do_ref, do_all.at[mine], do_send.at[o], do_recv.at[o], device))
        copies.append(remote(st_ref, st_all.at[mine], st_send.at[o], st_recv.at[o], device))
    for c in to_sibling + copies:
        c.start()
    one_all[own, :] = x_one[...]
    x_all[own, :] = x_ref[...]
    in_all[own, :] = in_ref[core]
    y_all[:, own] = y_ref[core]
    yd_all[:, own] = yd_ref[...]
    do_all[mine] = do_ref[...]
    st_all[mine] = st_ref[...]
    for c in to_sibling:
        c.wait_recv()

    part = jnp.dot(yd_all[...], in_all[...], preferred_element_type=F32).astype(BF)
    for x in range(2):
        for d in range(2):
            gd[x, d] = part[512 * x : 512 * (x + 1), QUARTER * d : QUARTER * (d + 1)].reshape(
                KG, 32, QUARTER
            )
    slot = dp * 2 + x_hi
    sends = []
    d_sends = []
    for i, (d, x, device) in enumerate(line):
        d_sends.append(remote(gd.at[x, d], rd.at[slot], d_send.at[i], d_recv.at[i], device))
    for c in d_sends:
        c.start()
    rd[slot] = gd[x_hi, dp]

    def product(first, rows, x_first):
        return jnp.dot(
            y_all[pl.ds(first, rows), :], x_all[:, pl.ds(x_first, WIDE)], preferred_element_type=F32
        ).astype(BF)

    out_part = product(0, 512, 0).reshape(KG, 32, WIDE)
    gate_part = product(512, 768, WIDE).reshape(KG, 48, WIDE)
    up_part = product(1280, 768, WIDE).reshape(KG, 48, WIDE)
    for j in range(KG):
        g1[j // 4, j % 4, 0:32, :] = out_part[j]
        g1[j // 4, j % 4, 32:64, :] = gate_part[j, 0:32]
        g2[j % 4, j // 4, 0:16, :] = gate_part[j, 32:48]
        g2[j % 4, j // 4, 16:64, :] = up_part[j]
    y, z = plane // 4, plane % 4
    a_sends, b_sends = [], []
    for i in range(1, 4):
        y_to, z_to = (y + i) % 4, (z + i) % 4
        along_y = (dp, ctx_of(x_hi, y_to * 4 + z, core))
        along_z = (dp, ctx_of(x_hi, y * 4 + z_to, core))
        a_sends.append(remote(g1.at[y_to], r1.at[y], a_send.at[0, i], a_recv.at[0, i], along_y))
        a_sends.append(remote(g2.at[z_to], r2.at[z], a_send.at[1, i], a_recv.at[1, i], along_z))
        b_sends.append(remote(s1.at[z_to], t1.at[z], b_send.at[0, i], b_recv.at[0, i], along_z))
        b_sends.append(remote(s2.at[y_to], t2.at[y], b_send.at[1, i], b_recv.at[1, i], along_y))
    for c in a_sends:
        c.start()
    r1[y] = g1[y]
    r2[z] = g2[z]
    p_sends = []
    row = lax.broadcasted_iota(jnp.int32, (1024, 1), 0)
    chip, inside = row >> 5, row & 31
    target = jnp.where(
        inside < 18,
        chip * 18 + inside,
        jnp.where(
            inside < 24,
            D + chip * 6 + inside - 18,
            jnp.where(inside < 30, D + 192 + chip * 6 + inside - 24, -1),
        ),
    )
    column = lax.broadcasted_iota(jnp.int32, (1024, 960), 1)
    spread[...] = jnp.where(column == target, 1.0, 0.0).astype(BF)
    for c in copies:
        c.wait_recv()
    zeros = jnp.zeros((HEAD, QG * TOK), BF)
    for g in range(KV_HEADS):
        dkv_acc[...] = jnp.zeros_like(dkv_acc)

        def one(r, unused, g=g):
            h = g * 3 + r
            queries = head_rows(q_all, h)
            grads = head_rows(do_all, h)
            grads_low = jnp.concatenate([zeros, grads], axis=0)
            lse = jnp.concatenate([st_all[a, pl.ds(h, 1), :] for a in range(QG)], axis=1)
            delta = jnp.concatenate([st_all[a, pl.ds(h + 16, 1), :] for a in range(QG)], axis=1)
            accum = jnp.zeros((HEAD, QG * TOK), F32)
            for chunk in range(KG // CHUNK):
                base = chunk * CHUNK
                keys, scores = scores_of(q_all, kv_all, kv_tok, g, base, queries, zeros)
                probs = jnp.exp(scores - lse)
                grad_probs = jnp.dot(keys, grads_low, preferred_element_type=F32)
                grad_scores = (probs * (grad_probs - delta)).astype(BF)
                keys_flat = jnp.concatenate(
                    [kv_all[base + b, pl.ds(g * 128, HEAD), :] for b in range(CHUNK)], axis=1
                )
                accum = accum + jnp.dot(keys_flat, grad_scores, preferred_element_type=F32)
                lanes = pl.ds(base * TOK, CHUNK * TOK)
                dkv_acc[0:HEAD, lanes] += across(queries, grad_scores)
                dkv_acc[HEAD : 2 * HEAD, lanes] += across(grads, probs.astype(BF))
            part = accum.astype(BF)
            first = pl.multiple_of(h * HEAD, HEAD)
            for a in range(QG):
                dq_buf[a, pl.ds(first, HEAD), :] = part[:, a * TOK : (a + 1) * TOK]
            return unused

        lax.fori_loop(0, 3, one, 0)
        for j in range(KG):
            dkv_buf[j, pl.ds(g * 128, 128), :] = dkv_acc[:, j * TOK : (j + 1) * TOK].astype(BF)
        rows = pl.ds(g * 128, 128)
        for o in range(1, KG):
            j, device = key_peers[o - 1]
            c = remote(
                dkv_buf.at[j, rows], dkv_got.at[plane, rows], dkv_send.at[o, g], dkv_recv.at[o, g], device
            )
            c.start()
            sends.append(c)
        rows = pl.ds(g * 192, 192)
        for o in range(1, QG):
            a, device = query_peers[o - 1]
            c = remote(
                dq_buf.at[a, rows], dq_got.at[mine, rows], dq_send.at[o, g], dq_recv.at[o, g], device
            )
            c.start()
            sends.append(c)
        if g == 1:
            for c in d_sends:
                c.wait_recv()
            for j in range(KG):
                total = rd[0, j].astype(F32)
                for s in range(1, 4):
                    total = total + rd[s, j].astype(F32)
                gp[j] = total.astype(BF)
            for o in range(1, KG):
                j, device = key_peers[o - 1]
                p_sends.append(remote(gp.at[j], rp.at[plane], p_send.at[o], p_recv.at[o], device))
            for c in p_sends:
                c.start()
            rp[plane] = gp[plane]
            for c in a_sends:
                c.wait_recv()
            for i in range(4):
                for pieces, sums in ((r1, s1), (r2, s2)):
                    total = pieces[0, i].astype(F32)
                    for j in range(1, 4):
                        total = total + pieces[j, i].astype(F32)
                    sums[i] = total.astype(BF)
            for c in b_sends:
                c.start()
            t1[z] = s1[z]
            t2[y] = s2[y]
    dq_got[mine] = dq_buf[mine]
    dkv_got[plane] = dkv_buf[plane]
    for c in p_sends:
        c.wait_recv()
    fd_ref[core] = sum_pieces(rp, KG, slice(0, 32))
    final = remote(fd_ref.at[core], fd_ref.at[core], f_send, f_recv, sibling)
    final.start()
    for c in b_sends:
        c.wait_recv()
    sa_ref[0:64, :] = sum_pieces(t1, 4, slice(0, 64)).astype(BF)
    sa_ref[64:128, :] = sum_pieces(t2, 4, slice(0, 64)).astype(BF)
    collector = core == x_hi

    def toward(target_dp, src, dst, send, recv):
        device = (target_dp, ctx_of(core, plane, core))
        lanes = pl.ds(pl.multiple_of(target_dp * 256, 128), QUARTER)
        return remote(src.at[:, lanes], dst.at[slot], send.at[target_dp], recv.at[slot], device)

    def pass_on(src, dst, send, recv):
        for target_dp in range(2):
            here = jnp.logical_and(collector, dp == target_dp)

            @pl.when(jnp.logical_not(here))
            def _():
                toward(target_dp, src, dst, send, recv).start()

            @pl.when(here)
            def _():
                dst[slot] = src[:, target_dp * 256 : target_dp * 256 + QUARTER]

    pass_on(sa_ref, wa, wa_send, wa_recv)
    for c in sends:
        c.wait_recv()
    cosine, sine = tables[0], tables[1]
    total = dq_got[0].astype(F32)
    for a in range(1, QG):
        total = total + dq_got[a].astype(F32)
    dq = turn(total * 0.125, HEADS, cosine, sine, -1.0).astype(BF).reshape(D, TOK)
    total = dkv_got[0].astype(F32)
    for j in range(1, KG):
        total = total + dkv_got[j].astype(F32)
    total = total.reshape(KV_HEADS, 2, HEAD, TOK)
    dk = turn(total[:, 0], KV_HEADS, cosine, sine, -1.0).astype(BF).reshape(192, TOK)
    dv = total[:, 1].astype(BF).reshape(192, TOK)
    placed = jnp.dot(
        spread[...], jnp.concatenate([dq, dk, dv], axis=0), preferred_element_type=F32
    ).astype(BF)
    yq_own[0] = placed[0:512]
    yq_own[1] = placed[512:1024]
    tail = [
        remote(
            yq_own.at[1 - core], yq_all.at[:, late], tail_send.at[0], tail_recv.at[0], sibling
        ),
        remote(gn_own, gn_all, tail_send.at[1], tail_recv.at[1], sibling),
    ]
    tail[0].start()
    yq_all[:, own] = yq_own[core]
    first = (
        jnp.dot(wq_ref[...], dq, preferred_element_type=F32)
        + jnp.dot(wk_ref[...], dk, preferred_element_type=F32)
        + jnp.dot(wv_ref[...], dv, preferred_element_type=F32)
    )
    state = h_ref[...].astype(F32)
    scale = lax.rsqrt(jnp.mean(state * state, axis=0, keepdims=True) + eps)
    unit = state * scale
    gn_own[...] = jnp.zeros_like(gn_own)
    terms = jnp.concatenate([first * unit, jnp.zeros((WIDE - D, TOK), F32)], axis=0).T
    gn_own[0:1, :] = jnp.sum(terms, axis=0, keepdims=True)
    gn_own[1:2, 0:D] = gain_term[...]
    tail[1].start()
    grad_unit = first * gain_rows(gains[0:1, :])
    grad_ref[...] = (
        scale * (grad_unit - unit * jnp.mean(grad_unit * unit, axis=0, keepdims=True))
        + back_ref[...]
    )
    for c in tail:
        c.wait_recv()
    part = jnp.dot(yq_all[...], one_all[...], preferred_element_type=F32).reshape(KG, 32, WIDE)
    sums = gn_own[...] + gn_all[...]
    line_of = lax.broadcasted_iota(jnp.int32, (KG, 32, WIDE), 1)
    part = jnp.where(line_of == 30, sums[0:1][None], part)
    part = jnp.where(line_of == 31, sums[1:2][None], part)
    gq[...] = part.astype(BF)
    q_sends = []
    for o in range(1, KG):
        j, device = key_peers[o - 1]
        q_sends.append(remote(gq.at[j], rq.at[plane], q_send.at[o], q_recv.at[o], device))
    for c in q_sends:
        c.start()
    rq[plane] = gq[plane]
    final.wait_recv()
    for c in q_sends:
        c.wait_recv()
    sq[...] = sum_pieces(rq, KG, slice(0, 32)).astype(BF)
    pass_on(sq, wb, wb_send, wb_recv)
    last = remote(fa_ref, fa_ref, last_send, last_recv, sibling)
    moves = ((sa_ref, wa, wa_send, wa_recv), (sq, wb, wb_send, wb_recv))

    @pl.when(collector)
    def _():
        for src, dst, send, recv in moves:
            for source in range(4):

                @pl.when(slot != source)
                def _():
                    remote(
                        src.at[:, pl.ds(0, QUARTER)], dst.at[source], send.at[0], recv.at[source], sibling
                    ).wait_recv()

        fa_ref[pl.ds(0, 32), :] = sum_pieces(wb, 4, slice(0, 32))
        fa_ref[pl.ds(32, GROWS), :] = sum_pieces(wa, 4, slice(0, GROWS))
        last.start()
        last.wait_send()

    @pl.when(jnp.logical_not(collector))
    def _():
        last.wait_recv()

    for target_dp in range(2):

        @pl.when(jnp.logical_not(jnp.logical_and(collector, dp == target_dp)))
        def _():
            for move in moves:
                toward(target_dp, *move).wait_send()

    final.wait_send()
    for c in copies + sends + to_sibling + d_sends + a_sends + b_sends + p_sends + tail + q_sends:
        c.wait_send()


def attention_backward(*args):
    dma = pltpu.SemaphoreType.DMA
    return pl.pallas_call(
        backward_kernel,
        out_shape=[
            jax.ShapeDtypeStruct((D, TOK), F32),
            jax.ShapeDtypeStruct((AROWS, QUARTER), F32),
            jax.ShapeDtypeStruct((2, 32, QUARTER), F32),
        ],
        in_specs=[VM] * len(args),
        out_specs=[VM] * 3,
        scratch_shapes=[
            pltpu.VMEM((QG, D, TOK), BF),
            pltpu.VMEM((QG, 32, TOK), F32),
            pltpu.VMEM((QG, D, TOK), BF),
            pltpu.VMEM((128, KG * TOK), F32),
            pltpu.VMEM((KG, 384, TOK), BF),
            pltpu.VMEM((QG, D, TOK), BF),
            pltpu.VMEM((KG, 384, TOK), BF),
            pltpu.VMEM((2 * TOK, 2 * WIDE), BF),
            pltpu.VMEM((2 * TOK, 2 * QUARTER), BF),
            pltpu.VMEM((GYROWS, 2 * TOK), BF),
            pltpu.VMEM((1024, 2 * TOK), BF),
            pltpu.VMEM((4, 4, 64, WIDE), BF),
            pltpu.VMEM((4, 4, 64, WIDE), BF),
            pltpu.VMEM((4, 4, 64, WIDE), BF),
            pltpu.VMEM((4, 4, 64, WIDE), BF),
            pltpu.VMEM((4, 64, WIDE), BF),
            pltpu.VMEM((4, 64, WIDE), BF),
            pltpu.VMEM((4, 64, WIDE), BF),
            pltpu.VMEM((4, 64, WIDE), BF),
            pltpu.VMEM((2, 2, KG, 32, QUARTER), BF),
            pltpu.VMEM((4, KG, 32, QUARTER), BF),
            pltpu.VMEM((KG, 32, QUARTER), BF),
            pltpu.VMEM((KG, 32, QUARTER), BF),
            pltpu.VMEM((2 * TOK, WIDE), BF),
            pltpu.VMEM((2, 512, TOK), BF),
            pltpu.VMEM((512, 2 * TOK), BF),
            pltpu.VMEM((8, WIDE), F32),
            pltpu.VMEM((8, WIDE), F32),
            pltpu.VMEM((KG, 32, WIDE), BF),
            pltpu.VMEM((KG, 32, WIDE), BF),
            pltpu.VMEM((32, WIDE), BF),
            pltpu.VMEM((GROWS, WIDE), BF),
            pltpu.VMEM((4, GROWS, QUARTER), BF),
            pltpu.VMEM((4, 32, QUARTER), BF),
            pltpu.VMEM((1024, 960), BF),
            dma((QG,)),
            dma((QG,)),
            dma((QG,)),
            dma((QG,)),
            dma((QG, KV_HEADS)),
            dma((QG, KV_HEADS)),
            dma((KG, KV_HEADS)),
            dma((KG, KV_HEADS)),
            dma((5,)),
            dma((5,)),
            dma((2, 4)),
            dma((2, 4)),
            dma((2, 4)),
            dma((2, 4)),
            dma((3,)),
            dma((3,)),
            dma((KG,)),
            dma((KG,)),
            dma,
            dma,
            dma((2,)),
            dma((2,)),
            dma((KG,)),
            dma((KG,)),
            dma((2,)),
            dma((4,)),
            dma((2,)),
            dma((4,)),
            dma,
            dma,
        ],
        compiler_params=params(2),
    )(*args)


def times_back(left, right):
    return lax.dot_general(left, right, (((1,), (1,)), ((), ())), preferred_element_type=F32)


def times(left, right):
    return jnp.dot(left, right, preferred_element_type=F32)


def middle_kernel(
    hidden, o_rows, lse, gains, grad_out, wo, wg, wu, wd,
    output, grad_middle, do_block, st_block, x, inner_parts, y, yd, gain_term,
):
    attended = o_rows[...].T.astype(BF)
    gain = gains[1:2, 0:D]
    grad_flat = grad_out[...]
    grad_low = grad_flat.astype(F32).T.astype(BF)
    middle = hidden[...].astype(F32).T + times(attended, wo[...])
    scale = lax.rsqrt(jnp.mean(middle * middle, axis=-1, keepdims=True) + eps)
    unit = middle * scale
    normal = (unit * gain).astype(BF)
    gate = times(normal, wg[...])
    upper = times(normal, wu[...])
    sigma = 1.0 / (1.0 + jnp.exp(-gate))
    silu = gate * sigma
    inner = (silu * upper).astype(BF)
    output[...] = flipped(middle + times_back(inner, wd[...]))[0:D].astype(BF)
    grad_inner = times(grad_low, wd[...])
    grad_gate = (grad_inner * upper * sigma * (1.0 + gate * (1.0 - sigma))).astype(BF)
    grad_up = (grad_inner * silu).astype(BF)
    grad_normal = times_back(grad_gate, wg[...]) + times_back(grad_up, wu[...])
    gain_term[...] = jnp.sum(grad_normal * unit, axis=0, keepdims=True)
    grad_unit = grad_normal * gain
    back = (
        scale * (grad_unit - unit * jnp.mean(grad_unit * unit, axis=-1, keepdims=True))
        + grad_low.astype(F32)
    )
    grad_middle[...] = flipped(back)[0:D]
    branch = back.astype(BF)
    grads = times_back(wo[...], branch).astype(BF)
    do_block[...] = grads
    st_block[...] = jnp.zeros_like(st_block)
    st_block[0:16, :] = lse[...]
    for h in range(HEADS):
        rows = slice(h * HEAD, (h + 1) * HEAD)
        st_block[16 + h : 17 + h, :] = jnp.sum(
            grads[rows].astype(F32) * o_rows[rows, :], axis=0, keepdims=True
        )
    x[...] = jnp.zeros_like(x)
    x[:, 0:D] = attended
    x[:, WIDE : WIDE + D] = normal
    for core in range(2):
        for d in range(2):
            first = 768 * d + QUARTER * core
            inner_parts[core, :, QUARTER * d : QUARTER * (d + 1)] = inner[:, first : first + QUARTER]
    row = lax.broadcasted_iota(jnp.int32, (1024, D), 0)
    column = lax.broadcasted_iota(jnp.int32, (1024, D), 1)
    inside = row & 31
    chosen = jnp.logical_and(inside < 18, column == (row >> 5) * 18 + inside)
    spread = jnp.where(chosen, 1.0, 0.0).astype(BF)
    yd[...] = times(spread, grad_flat).astype(BF)
    o_part = times_back(spread, branch).astype(BF)
    gate_flat = grad_gate.astype(F32).T.astype(BF)
    up_flat = grad_up.astype(F32).T.astype(BF)
    for core in range(2):
        y[core, 0:512, :] = o_part[512 * core : 512 * (core + 1)]
        y[core, 512:1280, :] = gate_flat[768 * core : 768 * (core + 1)]
        y[core, 1280:2048, :] = up_flat[768 * core : 768 * (core + 1)]


def feed_forward(hidden, o_rows, lse, gain, grad_out, wo, wg, wu, wd):
    shape = jax.ShapeDtypeStruct
    return pl.pallas_call(
        middle_kernel,
        out_shape=[
            shape((D, TOK), BF),
            shape((D, TOK), F32),
            shape((D, TOK), BF),
            shape((32, TOK), F32),
            shape((TOK, 2 * WIDE), BF),
            shape((2, TOK, 2 * QUARTER), BF),
            shape((2, GYROWS, TOK), BF),
            shape((1024, TOK), BF),
            shape((1, D), F32),
        ],
        in_specs=[VM] * 9,
        out_specs=[VM] * 9,
        compiler_params=pltpu.CompilerParams(vmem_limit_bytes=LIMIT),
    )(hidden, o_rows, lse, gain, grad_out, wo, wg, wu, wd)


def finish_kernel(fa, fd, grad, *outs):
    core = lax.axis_index("ctx") % 2
    dp = lax.axis_index("dp")
    rows = jnp.where(dp == 0, fa[...], pltpu.roll(fa[...], QUARTER - 32, 1))[:, 0:288]
    down = jnp.concatenate([fd[0], fd[1]], axis=1)
    for out, count, block, at in zip(
        outs[:7], (9, 3, 3, 9, 24, 24, 9), (rows,) * 6 + (down,), (0, 18, 24, 32, 64, 112, 0)
    ):
        part = jnp.where(core == 0, block[at : at + count], block[at + count : at + 2 * count])
        if count == 24:
            out[0] = part
        else:
            for i in range(count):
                out[i] = part[i : i + 1]
    outs[7][...] = rows[30:31]
    outs[8][...] = rows[31:32]
    outs[9][...] = grad[...]


def finish(fa, fd, grad):
    shape = jax.ShapeDtypeStruct
    return pl.pallas_call(
        finish_kernel,
        out_shape=[
            shape((9, 1, 288), F32),
            shape((3, 1, 288), F32),
            shape((3, 1, 288), F32),
            shape((9, 1, 288), F32),
            shape((1, 24, 288), F32),
            shape((1, 24, 288), F32),
            shape((9, 1, 768), F32),
            shape((1, 288), F32),
            shape((1, 288), F32),
            shape((D, TOK), F32),
        ],
        in_specs=[VM] * 3,
        out_specs=[VM] * 10,
    )(fa, fd, grad)


def local(
    hidden, positions, w_query, w_key, w_value, w_out, w_gate, w_up, w_down,
    gain_attn, gain_ffn, grad_out,
):
    state = hidden[0].T
    (
        o_rows, lse, q_all, kv_all, kv_tok, x_one, gains, tables, wq, wk, wv, wo, wg, wu, wd,
    ) = attention_forward(
        state,
        positions,
        gain_attn,
        gain_ffn,
        [w[0] for w in (w_query, w_key, w_value, w_out, w_gate, w_up)] + [w_down[0].T],
    )
    (
        output, grad_middle, do_block, st_block, x, inner_parts, y, down_part, gain_term,
    ) = feed_forward(state, o_rows, lse, gains, grad_out[0].T, wo, wg, wu, wd)
    grad_input, fa, fd = attention_backward(
        do_block, st_block, q_all, kv_all, kv_tok, x, inner_parts, y, down_part,
        state, grad_middle, wq, wk, wv, x_one, gains, tables, gain_term,
    )
    *grads, gain_one, gain_two, grad_input = finish(fa, fd, grad_input)
    columns = [
        g.transpose(0, 2, 1) if g.shape[0] == 1 else g.transpose(1, 2, 0) for g in grads
    ]
    return (output.T[None], grad_input.T[None]) + tuple(columns) + (gain_one, gain_two)


def solution(mesh):
    in_specs = (
        P("dp", "ctx", None),
        P("dp", "ctx"),
    ) + (P(None, "dp", None),) * 7 + (
        P(None, "dp"),
        P(None, "dp"),
        P("dp", "ctx", None),
    )
    out_specs = (
        P("dp", "ctx", None),
        P("dp", "ctx", None),
    ) + (P(None, "dp", "ctx"),) * 7 + (
        P(None, "dp"),
        P(None, "dp"),
    )
    return jax.shard_map(local, mesh=mesh, in_specs=in_specs, out_specs=out_specs, check_vma=False)
```

```python
from types import SimpleNamespace

import jax
import jax.numpy as jnp
import numpy as np
from jax import lax
from jax.experimental import pallas as pl
from jax.experimental.pallas import tpu as pltpu
from jax.sharding import PartitionSpec as P

HEADS = 9
KV_HEADS = 3
HEAD = 64
TOK = 128
D = 576
FF = 1536
QG = 4
KG = 16
WIDE = 640
eps = 1e-05
rope_base = 100000.0
MESH = pl.DeviceIdType.MESH
BF = jnp.bfloat16
F32 = jnp.float32
LIMIT = 56 * 1024 * 1024
VM = pl.BlockSpec(memory_space=pltpu.VMEM)
ANY = pl.BlockSpec(memory_space=pl.ANY)


def params(ident):
    return pltpu.CompilerParams(
        collective_id=ident, has_side_effects=True, vmem_limit_bytes=LIMIT
    )


def place():
    dp = lax.axis_index("dp")
    ctx = lax.axis_index("ctx")
    x_hi = ctx // 32
    plane = (ctx // 2) % 16
    core = ctx % 2
    return dp, x_hi, plane, core


def ctx_of(x_hi, plane, core):
    return x_hi * 32 + plane * 2 + core


def remote(src, dst, send, recv, device):
    return pltpu.make_async_remote_copy(
        src_ref=src,
        dst_ref=dst,
        send_sem=send,
        recv_sem=recv,
        device_id=device,
        device_id_type=MESH,
    )


def greet(devices):
    barrier = pltpu.get_barrier_semaphore()
    for device in devices:
        pl.semaphore_signal(barrier, inc=1, device_id=device, device_id_type=MESH)


def met(devices):
    pl.semaphore_wait(pltpu.get_barrier_semaphore(), len(devices))


def plane_peer(plane, offset):
    y, z = plane // 4, plane % 4
    return ((y + offset // 4) % 4) * 4 + (z + offset % 4) % 4


def plane_source(plane, offset):
    y, z = plane // 4, plane % 4
    return ((y + 4 - offset // 4) % 4) * 4 + (z + 4 - offset % 4) % 4


def weight_copies(shards, fulls, own_sem, send, recv, core_send, core_recv):
    dp, x_hi, plane, core = place()
    near = (1 - dp, ctx_of(x_hi, plane, core))
    far = (1 - dp, ctx_of(1 - x_hi, plane, core))
    sibling = (dp, ctx_of(x_hi, plane, 1 - core))
    own, first, second = [], [], []
    for which, (shard, full) in enumerate(zip(shards, fulls)):
        rows = shard.shape[0]
        half = rows // 2
        cut = 80 if rows == 288 else half // 2
        by_rows = full.shape[0] != rows

        def part(dp_of, off, size):
            if by_rows:
                return full.at[pl.ds(pl.multiple_of(dp_of * rows + off, 16), size)]
            width = shard.shape[1]
            return full.at[
                pl.ds(pl.multiple_of(off, 16), size), pl.ds(pl.multiple_of(dp_of * width, 128), width)
            ]

        own.append(pltpu.make_async_copy(shard, part(dp, 0, rows), own_sem.at[which]))
        for role, target in ((0, near), (1, far)):
            off = pl.multiple_of(role * cut + core * half, 16)
            size = half - cut if role else cut
            first.append(
                remote(
                    shard.at[pl.ds(off, size)],
                    part(dp, off, size),
                    send.at[which, role],
                    recv.at[which, role],
                    target,
                )
            )
            got = part(1 - dp, off, size)
            second.append(
                remote(got, got, core_send.at[which, role], core_recv.at[which, role], sibling)
            )
    return own, first, second


QROWS = D + 16
KROWS = 384 + 16
CHUNK = 4


def groups():
    dp, x_hi, plane, core = place()
    mine = x_hi * 2 + core
    query_peers = []
    for o in range(1, QG):
        a = (mine + o) % QG
        query_peers.append((a, (dp, ctx_of(a // 2, plane, a % 2))))
    key_peers = []
    for o in range(1, KG):
        j = plane_peer(plane, o)
        key_peers.append((j, (dp, ctx_of(x_hi, j, core))))
    return mine, plane, query_peers, key_peers


def flip_keys(kv_all, kv_tok, j):
    for g in range(KV_HEADS):
        block = kv_all[j, pl.ds(g * 128, 128), :].astype(F32)
        kv_tok[g, pl.ds(pl.multiple_of(j * TOK, TOK), TOK), :] = block.T.astype(BF)


def masks_of(q_all, kv_all, base):
    lane = lax.broadcasted_iota(jnp.int32, (1, TOK), 1).astype(F32)
    q_pos = jnp.concatenate(
        [q_all[a, pl.ds(0, 16), :].astype(F32)[0:1] * TOK + lane for a in range(QG)], axis=1
    )
    rows = lax.broadcasted_iota(jnp.int32, (TOK, QG * TOK), 0).astype(F32)
    parts = []
    for b in range(CHUNK):
        start = kv_all[base + b, pl.ds(384, 16), :].astype(F32)[0:1] * TOK
        start = jnp.concatenate([start] * QG, axis=1)
        parts.append(rows <= (q_pos - start))
    return jnp.concatenate(parts, axis=0)


def head_rows(ref, h, skip=0):
    first = pl.multiple_of(h * HEAD + skip, 16)
    return jnp.concatenate([ref[a, pl.ds(first, HEAD), :] for a in range(QG)], axis=1)


def scores_of(q_all, kv_all, kv_tok, g, base, queries, zeros):
    keys = kv_tok[g, pl.ds(pl.multiple_of(base * TOK, TOK), CHUNK * TOK), :]
    scores = jnp.dot(keys, jnp.concatenate([queries, zeros], axis=0), preferred_element_type=F32)
    return keys, jnp.where(masks_of(q_all, kv_all, base), scores, -1e30)


def turn(rows, heads, cosine, sine, sign):
    parts = rows.reshape(heads, 2, HEAD // 2, TOK)
    one, two = parts[:, 0], parts[:, 1]
    first = one * cosine - sign * two * sine
    second = two * cosine + sign * one * sine
    return jnp.concatenate([first[:, None], second[:, None]], axis=1)


def flipped(rows):
    wide = (rows.shape[1] + 127) // 128 * 128
    if wide != rows.shape[1]:
        rows = jnp.concatenate(
            [rows, jnp.zeros((rows.shape[0], wide - rows.shape[1]), rows.dtype)], axis=1
        )
    return rows.T


def gain_rows(row):
    return jnp.broadcast_to(row, (TOK, WIDE)).T[0:D]


def across(left, right):
    return lax.dot_general(left, right, (((1,), (1,)), ((), ())), preferred_element_type=F32)


def times(left, right):
    return jnp.dot(left, right, preferred_element_type=F32)


GROWS = 128
AROWS = 32 + GROWS
QUARTER = 384
OWN, LATE = pl.ds(0, TOK), pl.ds(TOK, TOK)


def line_peers():
    dp, x_hi, plane, core = place()
    return [
        ((dp + d) % 2, (x_hi + x) % 2, ((dp + d) % 2, ctx_of((x_hi + x) % 2, plane, core)))
        for d, x in ((1, 0), (0, 1), (1, 1))
    ]


def sum_pieces(pieces, count, rows):
    total = pieces[0, rows, :].astype(F32)
    for i in range(1, count):
        total = total + pieces[i, rows, :].astype(F32)
    return total


def starts(copies):
    for c in copies:
        c.start()


def arrive(copies):
    for c in copies:
        c.wait_recv()


def prepare_spread(r):
    row = lax.broadcasted_iota(jnp.int32, (1024, 1), 0)
    chip, inside = row >> 5, row & 31
    plain = jnp.where(inside < 18, chip * 18 + inside, -1)
    column = lax.broadcasted_iota(jnp.int32, (1024, D), 1)
    r.spread_one[...] = jnp.where(column == plain, 1.0, 0.0).astype(BF)
    target = jnp.where(
        inside < 18,
        plain,
        jnp.where(
            inside < 24,
            D + chip * 6 + inside - 18,
            jnp.where(inside < 30, D + 192 + chip * 6 + inside - 24, -1),
        ),
    )
    column = lax.broadcasted_iota(jnp.int32, (1024, 960), 1)
    r.spread[...] = jnp.where(column == target, 1.0, 0.0).astype(BF)


STEPS = ((0,), (1,), (2, 3))


def layer_kernel(*refs):
    r = SimpleNamespace(**dict(zip(NAMES, refs)))
    dp, x_hi, plane, core = place()
    mine, plane, query_peers, key_peers = groups()
    y, z = plane // 4, plane % 4
    slot = dp * 2 + x_hi
    line = line_peers()
    near = line[0][2]
    sibling = (dp, ctx_of(x_hi, plane, 1 - core))
    others = [
        (1 - dp, ctx_of((x_hi + x) % 2, plane, (core + c) % 2)) for x in range(2) for c in range(2)
    ]
    friends = [d for _, d in query_peers] + [d for _, d in key_peers] + others
    greet(friends)
    done = []
    shards = [r.s_key, r.s_value, r.s_query, r.s_out, r.s_gate, r.s_up, r.s_down]
    fulls = [r.w_key, r.w_value, r.w_query, r.w_out, r.w_gate, r.w_up, r.w_down]
    own_w, first_w, second_w = weight_copies(
        shards, fulls, r.w_own, r.w_send, r.w_recv, r.w_core_send, r.w_core_recv
    )
    starts(own_w)
    r.gain_own[...] = jnp.zeros_like(r.gain_own)
    r.gain_own[0:1, 0:288] = r.gain_a[...].astype(F32)
    r.gain_own[1:2, 0:288] = r.gain_f[...].astype(F32)
    placed = r.gain_own[...]
    r.gain_own[...] = jnp.where(dp == 0, placed, pltpu.roll(placed, 288, 1))
    met(friends)
    gain_copy = remote(r.gain_own, r.gain_got, r.gain_send.at[0], r.gain_recv.at[0], near)
    gain_copy.start()
    starts(first_w[:6])
    done += first_w + second_w + [gain_copy]
    state = r.hidden[...].astype(F32)
    scale_one = lax.rsqrt(jnp.mean(state * state, axis=0, keepdims=True) + eps)
    unit_one = state * scale_one
    run = r.positions[0:1, 0:1].astype(F32) * (1.0 / TOK)
    lane = lax.broadcasted_iota(jnp.int32, (HEAD // 2, 64), 1).astype(F32)
    at_run = lane == run
    cos_a = jnp.sum(jnp.where(at_run, r.run_cos[...], 0.0), axis=1, keepdims=True)
    sin_a = jnp.sum(jnp.where(at_run, r.run_sin[...], 0.0), axis=1, keepdims=True)
    cosine = cos_a * r.in_cos[...] - sin_a * r.in_sin[...]
    sine = sin_a * r.in_cos[...] + cos_a * r.in_sin[...]
    r.tables[0] = cosine
    r.tables[1] = sine
    run_rows = jnp.broadcast_to(run, (16, TOK)).astype(BF)
    gain_copy.wait_recv()
    r.gains[...] = r.gain_own[...] + r.gain_got[...]
    normal_one = flipped((unit_one * gain_rows(r.gains[0:1, :])).astype(BF).astype(F32)).astype(BF)
    r.one_all[OWN, D:WIDE] = jnp.zeros((TOK, WIDE - D), BF)
    r.one_all[OWN, 0:D] = normal_one
    for c, d in zip(first_w[:6], second_w[:6]):
        c.wait_recv()
        d.start()
    for c in own_w[:3]:
        c.wait()
    arrive(second_w[:4])
    keys = flipped(times(normal_one, r.w_key[...]))[0:192]
    keys = turn(keys, KV_HEADS, cosine, sine, 1.0).astype(BF).reshape(192, TOK)
    values = flipped(times(normal_one, r.w_value[...]))[0:192].astype(BF)
    for g in range(KV_HEADS):
        r.kv_all[plane, g * 128 : g * 128 + HEAD, :] = keys[g * HEAD : (g + 1) * HEAD]
        r.kv_all[plane, g * 128 + HEAD : (g + 1) * 128, :] = values[g * HEAD : (g + 1) * HEAD]
    r.kv_all[plane, 384:400, :] = run_rows
    q_copies, kv_copies = [], [None]
    own_kv, own_q = r.kv_all.at[plane], r.q_all.at[mine]
    for o in range(1, KG):
        kv_copies.append(
            remote(own_kv, own_kv, r.kv_send.at[o], r.kv_recv.at[o], key_peers[o - 1][1])
        )
    starts(kv_copies[1:])
    arrive(second_w[4:6])
    query = flipped(times(normal_one, r.w_query[...]))[0:D]
    query = turn(query, HEADS, cosine, sine, 1.0).astype(BF).reshape(D, TOK)
    r.q_all[mine, 0:16, :] = run_rows
    r.q_all[mine, 16:QROWS, :] = query * jnp.asarray(0.125, BF)
    for g in range(KV_HEADS):
        rows = pl.ds(16 + 192 * g, 192) if g else pl.ds(0, 208)
        for o in range(1, QG):
            q_copies.append(
                remote(
                    own_q.at[rows], own_q.at[rows], r.q_send.at[o, g], r.q_recv.at[o, g], query_peers[o - 1][1]
                )
            )
    starts(q_copies + first_w[6:])
    one_copy = remote(
        r.one_all.at[OWN], r.one_all.at[LATE], r.sib_send.at[0], r.sib_recv.at[0], sibling
    )
    one_copy.start()
    done += q_copies + kv_copies[1:] + [one_copy]
    prepare_spread(r)
    r.yd_all[:, OWN] = times(r.spread_one[...], r.grad_out[...]).astype(BF)
    yd_copy = remote(
        r.yd_all.at[:, OWN], r.yd_all.at[:, LATE], r.sib_send.at[1], r.sib_recv.at[1], sibling
    )
    yd_copy.start()
    done.append(yd_copy)
    zeros = jnp.zeros((HEAD, QG * TOK), BF)
    o_copies = []

    def o_copy(o, g):
        a, device = query_peers[o - 1]
        rows = pl.ds(pl.multiple_of(g * 192, 64), 192)
        return remote(
            r.o_buf.at[a, rows], r.o_got.at[mine, rows], r.o_send.at[o, g], r.o_recv.at[o, g], device
        )

    for step, rows_of in enumerate(STEPS):
        bases = [((y + 4 - back) % 4) * 4 for back in rows_of]
        for back, base in zip(rows_of, bases):
            arrive([kv_copies[back * 4 + dz] for dz in range(4) if back * 4 + dz])

            def flip(b, unused, base=base):
                flip_keys(r.kv_all, r.kv_tok, base + b)
                return unused

            lax.fori_loop(0, 4, flip, 0)
        last = step == len(STEPS) - 1

        def three(g, unused, step=step, bases=bases, last=last):
            for i in range(3):
                h = g * 3 + i
                first = pl.multiple_of(h * HEAD, HEAD)
                queries = head_rows(r.q_all, h, 16)
                scores = [
                    scores_of(r.q_all, r.kv_all, r.kv_tok, g, base, queries, zeros)[1]
                    for base in bases
                ]
                new_top = jnp.max(scores[0], axis=0, keepdims=True)
                for more in scores[1:]:
                    new_top = jnp.maximum(new_top, jnp.max(more, axis=0, keepdims=True))
                if step:
                    top = r.top_all[pl.ds(h, 1), :]
                    new_top = jnp.maximum(top, new_top)
                value_rows = pl.ds(pl.multiple_of(g * 128 + HEAD, HEAD), HEAD)
                total, accum = None, None
                for base, back, part in zip(bases, rows_of, scores):
                    probs = jnp.exp(part - new_top)
                    values = jnp.concatenate(
                        [r.kv_all[base + b, value_rows, :] for b in range(CHUNK)], axis=1
                    )
                    part_total = jnp.sum(probs, axis=0, keepdims=True)
                    probs = probs.astype(BF)
                    part_accum = times(values, probs)
                    total = part_total if total is None else total + part_total
                    accum = part_accum if accum is None else accum + part_accum
                if step:
                    fade = jnp.exp(top - new_top)
                    total = total + r.total_all[pl.ds(h, 1), :] * fade
                    accum = accum + r.accum_all[pl.ds(first, HEAD), :] * fade
                if not last:
                    r.top_all[pl.ds(h, 1), :] = new_top
                    r.total_all[pl.ds(h, 1), :] = total
                    r.accum_all[pl.ds(first, HEAD), :] = accum
                    continue
                part = (accum / total).astype(BF)
                for a in range(QG):
                    lanes = slice(a * TOK, (a + 1) * TOK)
                    r.o_buf[a, pl.ds(first, HEAD), :] = part[:, lanes]
                    r.ml_buf[a, pl.ds(h, 1), :] = new_top[:, lanes]
                    r.ml_buf[a, pl.ds(h + 16, 1), :] = total[:, lanes]
            return unused

        if step == 0:
            for g in range(KV_HEADS):
                arrive(q_copies[3 * g : 3 * g + 3])
                lax.fori_loop(g, g + 1, three, 0)
            continue
        if not last:
            lax.fori_loop(0, KV_HEADS, three, 0)
            if step == 1:
                for c, d in zip(first_w[6:], second_w[6:]):
                    c.wait_recv()
                    d.start()
            continue

        def three_and_send(g, unused):
            three(g, unused)
            starts([o_copy(o, g) for o in range(1, QG)])
            return unused

        lax.fori_loop(0, KV_HEADS, three_and_send, 0)
    o_copies += [o_copy(o, g) for o in range(1, QG) for g in range(KV_HEADS)]
    for o in range(1, QG):
        a, device = query_peers[o - 1]
        c = remote(r.ml_buf.at[a], r.ml_got.at[mine], r.ml_send.at[o], r.ml_recv.at[o], device)
        c.start()
        o_copies.append(c)
    done += o_copies
    r.o_got[mine] = r.o_buf[mine]
    r.ml_got[mine] = r.ml_buf[mine]
    for c in own_w[3:]:
        c.wait()
    arrive(second_w[6:])
    arrive(o_copies)
    r.st_own[...] = jnp.zeros_like(r.st_own)
    for h in range(HEADS):
        tops = [r.ml_got[a, pl.ds(h, 1), :] for a in range(QG)]
        best = jnp.maximum(jnp.maximum(tops[0], tops[1]), jnp.maximum(tops[2], tops[3]))
        shares = [r.ml_got[a, pl.ds(h + 16, 1), :] * jnp.exp(tops[a] - best) for a in range(QG)]
        whole = shares[0] + shares[1] + shares[2] + shares[3]
        r.st_own[pl.ds(h, 1), :] = best + jnp.log(whole)
        result = jnp.zeros((HEAD, TOK), F32)
        for a in range(QG):
            result = result + r.o_got[a, pl.ds(h * HEAD, HEAD), :].astype(F32) * (shares[a] / whole)
        r.o_rows[pl.ds(h * HEAD, HEAD), :] = result
    def to_sibling(src, dst, at):
        c = remote(src, dst, r.sib_send.at[at], r.sib_recv.at[at], sibling)
        c.start()
        done.append(c)
        return c

    attended = r.o_rows[...].T.astype(BF)
    r.att_all[OWN, D:WIDE] = jnp.zeros((TOK, WIDE - D), BF)
    r.att_all[OWN, 0:D] = attended
    att_copy = to_sibling(r.att_all.at[OWN], r.att_all.at[LATE], 2)
    gain = r.gains[1:2, 0:D]
    grad_low = r.grad_out[...].astype(F32).T.astype(BF)
    middle = r.hidden[...].astype(F32).T + times(attended, r.w_out[...])
    scale = lax.rsqrt(jnp.mean(middle * middle, axis=-1, keepdims=True) + eps)
    unit = middle * scale
    normal = (unit * gain).astype(BF)
    r.nrm_all[OWN, D:WIDE] = jnp.zeros((TOK, WIDE - D), BF)
    r.nrm_all[OWN, 0:D] = normal
    nrm_copy = to_sibling(r.nrm_all.at[OWN], r.nrm_all.at[LATE], 3)
    gate = times(normal, r.w_gate[...])
    upper = times(normal, r.w_up[...])
    sigma = 1.0 / (1.0 + jnp.exp(-gate))
    silu = gate * sigma
    inner = (silu * upper).astype(BF)
    for c in range(2):
        for d in range(2):
            first = 768 * d + QUARTER * c
            r.in_parts[c, :, QUARTER * d : QUARTER * (d + 1)] = inner[:, first : first + QUARTER]
    in_copy = to_sibling(r.in_parts.at[1 - core], r.in_all.at[LATE], 4)
    r.in_all[OWN, :] = r.in_parts[core]
    grad_inner = times(grad_low, r.w_down[...])
    grad_gate = (grad_inner * upper * sigma * (1.0 + gate * (1.0 - sigma))).astype(BF)
    grad_up = (grad_inner * silu).astype(BF)
    gate_flat = grad_gate.astype(F32).T.astype(BF)
    up_flat = grad_up.astype(F32).T.astype(BF)
    for c in range(2):
        r.yg_parts[c, 0:768, :] = gate_flat[768 * c : 768 * (c + 1)]
        r.yg_parts[c, 768:1536, :] = up_flat[768 * c : 768 * (c + 1)]
    yg_copy = to_sibling(r.yg_parts.at[1 - core], r.yg_all.at[:, LATE], 5)
    r.yg_all[:, OWN] = r.yg_parts[core]
    grad_normal = across(grad_gate, r.w_gate[...]) + across(grad_up, r.w_up[...])
    r.gn_own[...] = jnp.zeros_like(r.gn_own)
    r.gn_own[1:2, 0:D] = jnp.sum(grad_normal * unit, axis=0, keepdims=True)
    grad_unit = grad_normal * gain
    back = (
        scale * (grad_unit - unit * jnp.mean(grad_unit * unit, axis=-1, keepdims=True))
        + grad_low.astype(F32)
    )
    branch = back.astype(BF)
    grads_low = across(r.w_out[...], branch).astype(BF)
    r.do_all[mine] = grads_low
    for h in range(HEADS):
        rows = slice(h * HEAD, (h + 1) * HEAD)
        r.st_own[16 + h : 17 + h, :] = jnp.sum(
            grads_low[rows].astype(F32) * r.o_rows[rows, :], axis=0, keepdims=True
        )
    r.st_all[mine] = r.st_own[...]
    st_copies = []
    own_do, own_st = r.do_all.at[mine], r.st_all.at[mine]
    for o in range(1, QG):
        device = query_peers[o - 1][1]
        st_copies.append(remote(own_st, own_st, r.st_send.at[o], r.st_recv.at[o], device))

    def do_copy(o, g):
        rows = own_do.at[pl.ds(pl.multiple_of(g * 192, 64), 192)]
        return remote(rows, rows, r.do_send.at[o, g], r.do_recv.at[o, g], query_peers[o - 1][1])

    starts(st_copies)
    for g in range(KV_HEADS):
        starts([do_copy(o, g) for o in range(1, QG)])
    done += st_copies + [do_copy(o, g) for o in range(1, QG) for g in range(KV_HEADS)]
    o_part = across(r.spread_one[...], branch).astype(BF)
    r.yo_parts[0] = o_part[0:512]
    r.yo_parts[1] = o_part[512:1024]
    yo_copy = to_sibling(r.yo_parts.at[1 - core], r.yo_all.at[:, LATE], 6)
    r.yo_all[:, OWN] = r.yo_parts[core]
    r.back[...] = flipped(back)[0:D]
    arrive([yd_copy, in_copy])
    part = times(r.yd_all[...], r.in_all[...]).astype(BF)
    for x in range(2):
        for d in range(2):
            r.gd[x, d] = part[512 * x : 512 * (x + 1), QUARTER * d : QUARTER * (d + 1)].reshape(
                KG, 32, QUARTER
            )
    d_sends = []
    for i, (d, x, device) in enumerate(line):
        d_sends.append(remote(r.gd.at[x, d], r.rd.at[slot], r.d_send.at[i], r.d_recv.at[i], device))
    starts(d_sends)
    r.rd[slot] = r.gd[x_hi, dp]
    arrive([nrm_copy, yg_copy])
    gate_part = times(r.yg_all[0:768, :], r.nrm_all[...]).astype(BF).reshape(KG, 48, WIDE)
    up_part = times(r.yg_all[768:1536, :], r.nrm_all[...]).astype(BF).reshape(KG, 48, WIDE)
    arrive([att_copy, yo_copy])
    out_part = times(r.yo_all[...], r.att_all[...]).astype(BF).reshape(KG, 32, WIDE)
    for j in range(KG):
        r.g1[j // 4, j % 4, 0:32, :] = out_part[j]
        r.g1[j // 4, j % 4, 32:64, :] = gate_part[j, 0:32]
        r.g2[j % 4, j // 4, 0:16, :] = gate_part[j, 32:48]
        r.g2[j % 4, j // 4, 16:64, :] = up_part[j]
    a_sends, b_sends, p_sends = [], [], []
    for i in range(1, 4):
        y_to, z_to = (y + i) % 4, (z + i) % 4
        along_y = (dp, ctx_of(x_hi, y_to * 4 + z, core))
        along_z = (dp, ctx_of(x_hi, y * 4 + z_to, core))
        a_sends.append(
            remote(r.g1.at[y_to], r.r1.at[y], r.a_send.at[0, i], r.a_recv.at[0, i], along_y)
        )
        a_sends.append(
            remote(r.g2.at[z_to], r.r2.at[z], r.a_send.at[1, i], r.a_recv.at[1, i], along_z)
        )
        b_sends.append(
            remote(r.s1.at[z_to], r.t1.at[z], r.b_send.at[0, i], r.b_recv.at[0, i], along_z)
        )
        b_sends.append(
            remote(r.s2.at[y_to], r.t2.at[y], r.b_send.at[1, i], r.b_recv.at[1, i], along_y)
        )
    starts(a_sends)
    r.r1[y] = r.g1[y]
    r.r2[z] = r.g2[z]
    for o in range(1, KG):
        j, device = key_peers[o - 1]
        p_sends.append(
            remote(r.gp.at[j], r.rp.at[plane], r.p_send.at[o], r.p_recv.at[o], device)
        )
    done += d_sends + a_sends + b_sends + p_sends
    arrive(st_copies)

    def dkv_copy(o, g):
        j, device = key_peers[o - 1]
        rows = pl.ds(pl.multiple_of(g * 128, 128), 128)
        return remote(
            r.dkv_buf.at[j, rows], r.dkv_got.at[plane, rows], r.dkv_send.at[o, g], r.dkv_recv.at[o, g], device
        )

    def dq_copy(o, g):
        a, device = query_peers[o - 1]
        rows = pl.ds(pl.multiple_of(g * 192, 64), 192)
        return remote(
            r.dq_buf.at[a, rows], r.dq_got.at[mine, rows], r.dq_send.at[o, g], r.dq_recv.at[o, g], device
        )

    def key_head(g, unused):
        arrive([do_copy(o, g) for o in range(1, QG)])
        for c in (1, 2, 3, 0):
            base = ((y + c) % 4) * 4
            key_term, value_term = None, None
            for i in range(3):
                h = g * 3 + i
                queries = head_rows(r.q_all, h, 16)
                grads = head_rows(r.do_all, h)
                lse = jnp.concatenate([r.st_all[a, pl.ds(h, 1), :] for a in range(QG)], axis=1)
                delta = jnp.concatenate([r.st_all[a, pl.ds(h + 16, 1), :] for a in range(QG)], axis=1)
                keys, scores = scores_of(r.q_all, r.kv_all, r.kv_tok, g, base, queries, zeros)
                probs = jnp.exp(scores - lse)
                grad_probs = times(keys, jnp.concatenate([zeros, grads], axis=0))
                grad_scores = (probs * (grad_probs - delta)).astype(BF)
                key_rows = pl.ds(pl.multiple_of(g * 128, 128), HEAD)
                flat_keys = jnp.concatenate(
                    [r.kv_all[base + b, key_rows, :] for b in range(CHUNK)], axis=1
                )
                part = times(flat_keys, grad_scores)
                rows = slice(i * HEAD, (i + 1) * HEAD)
                r.dq_acc[rows, :] = part if c == 1 else r.dq_acc[rows, :] + part
                key_part = across(queries, grad_scores)
                value_part = across(grads, probs.astype(BF))
                key_term = key_part if key_term is None else key_term + key_part
                value_term = value_part if value_term is None else value_term + value_part
            first = pl.multiple_of(g * 128, 128)
            for b in range(CHUNK):
                lanes = slice(b * TOK, (b + 1) * TOK)
                r.dkv_buf[base + b, pl.ds(first, HEAD), :] = key_term[:, lanes].astype(BF)
                r.dkv_buf[base + b, pl.ds(pl.multiple_of(first + HEAD, HEAD), HEAD), :] = (
                    value_term[:, lanes].astype(BF)
                )
            starts([dkv_copy(c * 4 + dz, g) for dz in range(4) if c * 4 + dz])
        rows = pl.ds(pl.multiple_of(g * 192, 64), 192)
        for a in range(QG):
            r.dq_buf[a, rows, :] = r.dq_acc[:, a * TOK : (a + 1) * TOK].astype(BF)
        starts([dq_copy(o, g) for o in range(1, QG)])

        @pl.when(g == 1)
        def _():
            arrive(d_sends)
            for j in range(KG):
                total = r.rd[0, j].astype(F32)
                for i in range(1, 4):
                    total = total + r.rd[i, j].astype(F32)
                r.gp[j] = total.astype(BF)
            starts(p_sends)
            arrive(a_sends)
            for i in range(4):
                for pieces, sums in ((r.r1, r.s1), (r.r2, r.s2)):
                    total = pieces[0, i].astype(F32)
                    for j in range(1, 4):
                        total = total + pieces[j, i].astype(F32)
                    sums[i] = total.astype(BF)
            starts(b_sends)

        return unused

    lax.fori_loop(0, KV_HEADS, key_head, 0)
    sends = [dkv_copy(o, g) for o in range(1, KG) for g in range(KV_HEADS)]
    sends += [dq_copy(o, g) for o in range(1, QG) for g in range(KV_HEADS)]
    r.rp[plane] = r.gp[plane]
    r.t1[z] = r.s1[z]
    r.t2[y] = r.s2[y]
    r.dq_got[mine] = r.dq_buf[mine]
    r.dkv_got[plane] = r.dkv_buf[plane]
    arrive(p_sends)
    r.fd[core] = sum_pieces(r.rp, KG, slice(0, 32))
    final = remote(r.fd.at[core], r.fd.at[core], r.f_send.at[0], r.f_recv.at[0], sibling)
    final.start()
    arrive(b_sends)
    r.sa[0:64, :] = sum_pieces(r.t1, 4, slice(0, 64)).astype(BF)
    r.sa[64:128, :] = sum_pieces(r.t2, 4, slice(0, 64)).astype(BF)
    collector = core == x_hi

    def toward(target_dp, src, dst, send, recv):
        device = (target_dp, ctx_of(core, plane, core))
        lanes = pl.ds(pl.multiple_of(target_dp * 256, 128), QUARTER)
        return remote(src.at[:, lanes], dst.at[slot], send.at[target_dp], recv.at[slot], device)

    def pass_on(src, dst, send, recv):
        for target_dp in range(2):
            here = jnp.logical_and(collector, dp == target_dp)

            @pl.when(jnp.logical_not(here))
            def _():
                toward(target_dp, src, dst, send, recv).start()

            @pl.when(here)
            def _():
                dst[slot] = src[:, target_dp * 256 : target_dp * 256 + QUARTER]

    pass_on(r.sa, r.wa, r.wa_send, r.wa_recv)
    arrive(sends)
    done += sends
    cosine, sine = r.tables[0], r.tables[1]
    total = r.dq_got[0].astype(F32)
    for a in range(1, QG):
        total = total + r.dq_got[a].astype(F32)
    dq = turn(total * 0.125, HEADS, cosine, sine, -1.0).astype(BF).reshape(D, TOK)
    total = r.dkv_got[0].astype(F32)
    for j in range(1, KG):
        total = total + r.dkv_got[j].astype(F32)
    total = total.reshape(KV_HEADS, 2, HEAD, TOK)
    dk = turn(total[:, 0], KV_HEADS, cosine, sine, -1.0).astype(BF).reshape(192, TOK)
    dv = total[:, 1].astype(BF).reshape(192, TOK)
    placed = times(r.spread[...], jnp.concatenate([dq, dk, dv], axis=0)).astype(BF)
    r.yq_parts[0] = placed[0:512]
    r.yq_parts[1] = placed[512:1024]
    yq_copy = to_sibling(r.yq_parts.at[1 - core], r.yq_all.at[:, LATE], 7)
    r.yq_all[:, OWN] = r.yq_parts[core]
    first = times(r.w_query[...], dq) + times(r.w_key[...], dk) + times(r.w_value[...], dv)
    state = r.hidden[...].astype(F32)
    scale = lax.rsqrt(jnp.mean(state * state, axis=0, keepdims=True) + eps)
    unit = state * scale
    terms = jnp.concatenate([first * unit, jnp.zeros((WIDE - D, TOK), F32)], axis=0).T
    r.gn_own[0:1, :] = jnp.sum(terms, axis=0, keepdims=True)
    gn_copy = to_sibling(r.gn_own, r.gn_all, 8)
    grad_unit = first * gain_rows(r.gains[0:1, :])
    r.grad[...] = (
        scale * (grad_unit - unit * jnp.mean(grad_unit * unit, axis=0, keepdims=True))
        + r.back[...]
    )
    arrive([one_copy, yq_copy, gn_copy])
    part = times(r.yq_all[...], r.one_all[...]).reshape(KG, 32, WIDE)
    sums = r.gn_own[...] + r.gn_all[...]
    line_of = lax.broadcasted_iota(jnp.int32, (KG, 32, WIDE), 1)
    part = jnp.where(line_of == 30, sums[0:1][None], part)
    part = jnp.where(line_of == 31, sums[1:2][None], part)
    r.gq[...] = part.astype(BF)
    q_sends = []
    for o in range(1, KG):
        j, device = key_peers[o - 1]
        q_sends.append(
            remote(r.gq.at[j], r.rq.at[plane], r.gq_send.at[o], r.gq_recv.at[o], device)
        )
    starts(q_sends)
    done += q_sends
    r.rq[plane] = r.gq[plane]
    r.output[...] = flipped(middle + across(inner, r.w_down[...]))[0:D].astype(BF)
    final.wait_recv()
    done.append(final)

    def collect(src, dst, send, recv, rows, at):
        part = r.fa.at[rows]
        passed = remote(part, part, r.f_send.at[at], r.f_recv.at[at], sibling)

        @pl.when(collector)
        def _():
            for source in range(4):

                @pl.when(slot != source)
                def _():
                    remote(
                        src.at[:, pl.ds(0, QUARTER)], dst.at[source], send.at[0], recv.at[source], sibling
                    ).wait_recv()

            part[...] = sum_pieces(dst, 4, slice(None))
            passed.start()

        return passed

    moves = ((r.sa, r.wa, r.wa_send, r.wa_recv), (r.sq, r.wb, r.wb_send, r.wb_recv))
    early = collect(*moves[0], pl.ds(32, GROWS), 1)
    arrive(q_sends)
    r.sq[...] = sum_pieces(r.rq, KG, slice(0, 32)).astype(BF)
    pass_on(r.sq, r.wb, r.wb_send, r.wb_recv)
    late = collect(*moves[1], pl.ds(0, 32), 2)

    @pl.when(collector)
    def _():
        early.wait_send()
        late.wait_send()

    @pl.when(jnp.logical_not(collector))
    def _():
        early.wait_recv()
        late.wait_recv()

    for target_dp in range(2):

        @pl.when(jnp.logical_not(jnp.logical_and(collector, dp == target_dp)))
        def _():
            for move in moves:
                toward(target_dp, *move).wait_send()

    for c in done:
        c.wait_send()


INPUTS = (
    "hidden",
    "positions",
    "run_cos",
    "run_sin",
    "in_cos",
    "in_sin",
    "gain_a",
    "gain_f",
    "grad_out",
    "s_key",
    "s_value",
    "s_query",
    "s_out",
    "s_gate",
    "s_up",
    "s_down",
)
OUTPUTS = (
    ("output", (D, TOK), BF),
    ("grad", (D, TOK), F32),
    ("fa", (AROWS, QUARTER), F32),
    ("fd", (2, 32, QUARTER), F32),
)
SCRATCH = (
    ("gain_own", (8, WIDE), F32),
    ("gain_got", (8, WIDE), F32),
    ("gains", (8, WIDE), F32),
    ("tables", (2, HEAD // 2, TOK), F32),
    ("w_key", (D, 192), BF),
    ("w_value", (D, 192), BF),
    ("w_query", (D, D), BF),
    ("w_out", (D, D), BF),
    ("w_gate", (D, FF), BF),
    ("w_up", (D, FF), BF),
    ("w_down", (D, FF), BF),
    ("q_all", (QG, QROWS, TOK), BF),
    ("kv_all", (KG, KROWS, TOK), BF),
    ("kv_tok", (KV_HEADS, KG * TOK, 128), BF),
    ("accum_all", (D, QG * TOK), F32),
    ("top_all", (16, QG * TOK), F32),
    ("total_all", (16, QG * TOK), F32),
    ("o_buf", (QG, D, TOK), BF),
    ("o_got", (QG, D, TOK), BF),
    ("ml_buf", (QG, 32, TOK), F32),
    ("ml_got", (QG, 32, TOK), F32),
    ("o_rows", (D, TOK), F32),
    ("st_own", (32, TOK), F32),
    ("st_all", (QG, 32, TOK), F32),
    ("do_all", (QG, D, TOK), BF),
    ("spread_one", (1024, D), BF),
    ("spread", (1024, 960), BF),
    ("one_all", (2 * TOK, WIDE), BF),
    ("att_all", (2 * TOK, WIDE), BF),
    ("nrm_all", (2 * TOK, WIDE), BF),
    ("in_parts", (2, TOK, 2 * QUARTER), BF),
    ("in_all", (2 * TOK, 2 * QUARTER), BF),
    ("yd_all", (1024, 2 * TOK), BF),
    ("yg_parts", (2, 1536, TOK), BF),
    ("yg_all", (1536, 2 * TOK), BF),
    ("yo_parts", (2, 512, TOK), BF),
    ("yo_all", (512, 2 * TOK), BF),
    ("yq_parts", (2, 512, TOK), BF),
    ("yq_all", (512, 2 * TOK), BF),
    ("gn_own", (8, WIDE), F32),
    ("gn_all", (8, WIDE), F32),
    ("back", (D, TOK), F32),
    ("gd", (2, 2, KG, 32, QUARTER), BF),
    ("rd", (4, KG, 32, QUARTER), BF),
    ("gp", (KG, 32, QUARTER), BF),
    ("rp", (KG, 32, QUARTER), BF),
    ("g1", (4, 4, 64, WIDE), BF),
    ("g2", (4, 4, 64, WIDE), BF),
    ("r1", (4, 4, 64, WIDE), BF),
    ("r2", (4, 4, 64, WIDE), BF),
    ("s1", (4, 64, WIDE), BF),
    ("s2", (4, 64, WIDE), BF),
    ("t1", (4, 64, WIDE), BF),
    ("t2", (4, 64, WIDE), BF),
    ("sa", (GROWS, WIDE), BF),
    ("gq", (KG, 32, WIDE), BF),
    ("rq", (KG, 32, WIDE), BF),
    ("sq", (32, WIDE), BF),
    ("wa", (4, GROWS, QUARTER), BF),
    ("wb", (4, 32, QUARTER), BF),
    ("dq_acc", (192, QG * TOK), F32),
    ("dq_buf", (QG, D, TOK), BF),
    ("dq_got", (QG, D, TOK), BF),
    ("dkv_buf", (KG, 384, TOK), BF),
    ("dkv_got", (KG, 384, TOK), BF),
)
SEMAPHORES = (
    ("w_own", (7,)),
    ("w_send", (7, 2)),
    ("w_recv", (7, 2)),
    ("w_core_send", (7, 2)),
    ("w_core_recv", (7, 2)),
    ("gain_send", (1,)),
    ("gain_recv", (1,)),
    ("q_send", (QG, KV_HEADS)),
    ("q_recv", (QG, KV_HEADS)),
    ("kv_send", (KG,)),
    ("kv_recv", (KG,)),
    ("o_send", (QG, KV_HEADS)),
    ("o_recv", (QG, KV_HEADS)),
    ("ml_send", (QG,)),
    ("ml_recv", (QG,)),
    ("sib_send", (9,)),
    ("sib_recv", (9,)),
    ("do_send", (QG, KV_HEADS)),
    ("do_recv", (QG, KV_HEADS)),
    ("st_send", (QG,)),
    ("st_recv", (QG,)),
    ("d_send", (3,)),
    ("d_recv", (3,)),
    ("a_send", (2, 4)),
    ("a_recv", (2, 4)),
    ("b_send", (2, 4)),
    ("b_recv", (2, 4)),
    ("p_send", (KG,)),
    ("p_recv", (KG,)),
    ("dkv_send", (KG, KV_HEADS)),
    ("dkv_recv", (KG, KV_HEADS)),
    ("dq_send", (QG, KV_HEADS)),
    ("dq_recv", (QG, KV_HEADS)),
    ("f_send", (3,)),
    ("f_recv", (3,)),
    ("gq_send", (KG,)),
    ("gq_recv", (KG,)),
    ("wa_send", (2,)),
    ("wa_recv", (4,)),
    ("wb_send", (2,)),
    ("wb_recv", (4,)),
)
NAMES = (
    list(INPUTS)
    + [name for name, _, _ in OUTPUTS]
    + [name for name, _, _ in SCRATCH]
    + [name for name, _ in SEMAPHORES]
)


def layer(hidden, positions, gain_attn, gain_ffn, grad_out, shards):
    freqs = rope_base ** (-(np.arange(HEAD // 2, dtype=np.float64) * 2.0 / HEAD))[:, None]
    runs = freqs * (np.arange(64, dtype=np.float64) * TOK)[None]
    inside = freqs * np.arange(TOK, dtype=np.float64)[None]
    tables = [f(a).astype(np.float32) for a in (runs, inside) for f in (np.cos, np.sin)]
    return pl.pallas_call(
        layer_kernel,
        out_shape=[jax.ShapeDtypeStruct(shape, kind) for _, shape, kind in OUTPUTS],
        in_specs=[VM] * 9 + [ANY] * 7,
        out_specs=[VM] * len(OUTPUTS),
        scratch_shapes=[pltpu.VMEM(shape, kind) for _, shape, kind in SCRATCH]
        + [pltpu.SemaphoreType.DMA(shape) for _, shape in SEMAPHORES],
        compiler_params=params(1),
    )(hidden, positions, *[jnp.asarray(t) for t in tables], gain_attn, gain_ffn, grad_out, *shards)


def finish_kernel(fa, fd, grad, result, *outs):
    core = lax.axis_index("ctx") % 2
    dp = lax.axis_index("dp")
    rows = jnp.where(dp == 0, fa[...], pltpu.roll(fa[...], QUARTER - 32, 1))[:, 0:288]
    down = jnp.concatenate([fd[0], fd[1]], axis=1)
    for out, count, block, at in zip(
        outs[:7], (9, 3, 3, 9, 24, 24, 9), (rows,) * 6 + (down,), (0, 18, 24, 32, 64, 112, 0)
    ):
        part = jnp.where(core == 0, block[at : at + count], block[at + count : at + 2 * count])
        if count == 24:
            out[0] = part
        else:
            for i in range(count):
                out[i] = part[i : i + 1]
    outs[7][...] = rows[30:31]
    outs[8][...] = rows[31:32]
    outs[9][...] = grad[...]
    outs[10][...] = result[...]


def finish(fa, fd, grad, result):
    shape = jax.ShapeDtypeStruct
    return pl.pallas_call(
        finish_kernel,
        out_shape=[
            shape((9, 1, 288), F32),
            shape((3, 1, 288), F32),
            shape((3, 1, 288), F32),
            shape((9, 1, 288), F32),
            shape((1, 24, 288), F32),
            shape((1, 24, 288), F32),
            shape((9, 1, 768), F32),
            shape((1, 288), F32),
            shape((1, 288), F32),
            shape((D, TOK), F32),
            shape((D, TOK), BF),
        ],
        in_specs=[VM] * 4,
        out_specs=[VM] * 11,
    )(fa, fd, grad, result)


def local(
    hidden, positions, w_query, w_key, w_value, w_out, w_gate, w_up, w_down,
    gain_attn, gain_ffn, grad_out,
):
    output, grad_input, fa, fd = layer(
        hidden[0].T,
        positions,
        gain_attn,
        gain_ffn,
        grad_out[0].T,
        [w[0] for w in (w_key, w_value, w_query, w_out, w_gate, w_up)] + [w_down[0].T],
    )
    *grads, gain_one, gain_two, grad_input, output = finish(fa, fd, grad_input, output)
    columns = [
        g.transpose(0, 2, 1) if g.shape[0] == 1 else g.transpose(1, 2, 0) for g in grads
    ]
    return (output.T[None], grad_input.T[None]) + tuple(columns) + (gain_one, gain_two)


def solution(mesh):
    in_specs = (
        P("dp", "ctx", None),
        P("dp", "ctx"),
    ) + (P(None, "dp", None),) * 7 + (
        P(None, "dp"),
        P(None, "dp"),
        P("dp", "ctx", None),
    )
    out_specs = (
        P("dp", "ctx", None),
        P("dp", "ctx", None),
    ) + (P(None, "dp", "ctx"),) * 7 + (
        P(None, "dp"),
        P(None, "dp"),
    )
    return jax.shard_map(local, mesh=mesh, in_specs=in_specs, out_specs=out_specs, check_vma=False)
```

```python
from types import SimpleNamespace

import jax
import jax.numpy as jnp
import numpy as np
from jax import lax
from jax.experimental import pallas as pl
from jax.experimental.pallas import tpu as pltpu
from jax.sharding import PartitionSpec as P

HEADS = 9
KV_HEADS = 3
HEAD = 64
TOK = 128
D = 576
FF = 1536
QG = 4
KG = 16
WIDE = 640
eps = 1e-05
rope_base = 100000.0
MESH = pl.DeviceIdType.MESH
BF = jnp.bfloat16
F32 = jnp.float32
LIMIT = 56 * 1024 * 1024
VM = pl.BlockSpec(memory_space=pltpu.VMEM)
ANY = pl.BlockSpec(memory_space=pl.ANY)


def params(ident):
    return pltpu.CompilerParams(
        collective_id=ident, has_side_effects=True, vmem_limit_bytes=LIMIT
    )


def place():
    dp = lax.axis_index("dp")
    ctx = lax.axis_index("ctx")
    x_hi = ctx // 32
    plane = (ctx // 2) % 16
    core = ctx % 2
    return dp, x_hi, plane, core


def ctx_of(x_hi, plane, core):
    return x_hi * 32 + plane * 2 + core


def remote(src, dst, send, recv, device):
    return pltpu.make_async_remote_copy(
        src_ref=src,
        dst_ref=dst,
        send_sem=send,
        recv_sem=recv,
        device_id=device,
        device_id_type=MESH,
    )


def greet(devices):
    barrier = pltpu.get_barrier_semaphore()
    for device in devices:
        pl.semaphore_signal(barrier, inc=1, device_id=device, device_id_type=MESH)


def met(devices):
    pl.semaphore_wait(pltpu.get_barrier_semaphore(), len(devices))


def plane_peer(plane, offset):
    y, z = plane // 4, plane % 4
    return ((y + offset // 4) % 4) * 4 + (z + offset % 4) % 4


def plane_source(plane, offset):
    y, z = plane // 4, plane % 4
    return ((y + 4 - offset // 4) % 4) * 4 + (z + 4 - offset % 4) % 4


def weight_copies(shards, fulls, own_sem, send, recv, core_send, core_recv):
    dp, x_hi, plane, core = place()
    near = (1 - dp, ctx_of(x_hi, plane, core))
    far = (1 - dp, ctx_of(1 - x_hi, plane, core))
    sibling = (dp, ctx_of(x_hi, plane, 1 - core))
    own, first, second = [], [], []
    for which, (shard, full) in enumerate(zip(shards, fulls)):
        rows = shard.shape[0]
        half = rows // 2
        cut = 80 if rows == 288 else half // 2
        by_rows = full.shape[0] != rows

        def part(dp_of, off, size):
            if by_rows:
                return full.at[pl.ds(pl.multiple_of(dp_of * rows + off, 16), size)]
            width = shard.shape[1]
            return full.at[
                pl.ds(pl.multiple_of(off, 16), size), pl.ds(pl.multiple_of(dp_of * width, 128), width)
            ]

        own.append(pltpu.make_async_copy(shard, part(dp, 0, rows), own_sem.at[which]))
        for role, target in ((0, near), (1, far)):
            off = pl.multiple_of(role * cut + core * half, 16)
            size = half - cut if role else cut
            first.append(
                remote(
                    shard.at[pl.ds(off, size)],
                    part(dp, off, size),
                    send.at[which, role],
                    recv.at[which, role],
                    target,
                )
            )
            got = part(1 - dp, off, size)
            second.append(
                remote(got, got, core_send.at[which, role], core_recv.at[which, role], sibling)
            )
    return own, first, second


QROWS = D + 16
KROWS = 384 + 16
CHUNK = 4


def groups():
    dp, x_hi, plane, core = place()
    mine = x_hi * 2 + core
    query_peers = []
    for o in range(1, QG):
        a = (mine + o) % QG
        query_peers.append((a, (dp, ctx_of(a // 2, plane, a % 2))))
    key_peers = []
    for o in range(1, KG):
        j = plane_peer(plane, o)
        key_peers.append((j, (dp, ctx_of(x_hi, j, core))))
    return mine, plane, query_peers, key_peers


def flip_keys(kv_all, kv_tok, j):
    for g in range(KV_HEADS):
        block = kv_all[j, pl.ds(g * 128, 128), :].astype(F32)
        kv_tok[g, pl.ds(pl.multiple_of(j * TOK, TOK), TOK), :] = block.T.astype(BF)


def masks_of(q_all, kv_all, base):
    lane = lax.broadcasted_iota(jnp.int32, (1, TOK), 1).astype(F32)
    q_pos = jnp.concatenate(
        [q_all[a, pl.ds(0, 16), :].astype(F32)[0:1] * TOK + lane for a in range(QG)], axis=1
    )
    rows = lax.broadcasted_iota(jnp.int32, (TOK, QG * TOK), 0).astype(F32)
    parts = []
    for b in range(CHUNK):
        start = kv_all[base + b, pl.ds(384, 16), :].astype(F32)[0:1] * TOK
        start = jnp.concatenate([start] * QG, axis=1)
        parts.append(rows <= (q_pos - start))
    return jnp.concatenate(parts, axis=0)


def head_rows(ref, h, skip=0):
    first = pl.multiple_of(h * HEAD + skip, 16)
    return jnp.concatenate([ref[a, pl.ds(first, HEAD), :] for a in range(QG)], axis=1)


def scores_of(q_all, kv_all, kv_tok, g, base, queries, zeros):
    keys = kv_tok[g, pl.ds(pl.multiple_of(base * TOK, TOK), CHUNK * TOK), :]
    scores = jnp.dot(keys, jnp.concatenate([queries, zeros], axis=0), preferred_element_type=F32)
    return keys, jnp.where(masks_of(q_all, kv_all, base), scores, -1e30)


def turn(rows, heads, cosine, sine, sign):
    parts = rows.reshape(heads, 2, HEAD // 2, TOK)
    one, two = parts[:, 0], parts[:, 1]
    first = one * cosine - sign * two * sine
    second = two * cosine + sign * one * sine
    return jnp.concatenate([first[:, None], second[:, None]], axis=1)


def flipped(rows):
    wide = (rows.shape[1] + 127) // 128 * 128
    if wide != rows.shape[1]:
        rows = jnp.concatenate(
            [rows, jnp.zeros((rows.shape[0], wide - rows.shape[1]), rows.dtype)], axis=1
        )
    return rows.T


def gain_rows(row):
    return jnp.broadcast_to(row, (TOK, WIDE)).T[0:D]


def across(left, right):
    return lax.dot_general(left, right, (((1,), (1,)), ((), ())), preferred_element_type=F32)


def times(left, right):
    return jnp.dot(left, right, preferred_element_type=F32)


GROWS = 128
AROWS = 32 + GROWS
QUARTER = 384
OWN, LATE = pl.ds(0, TOK), pl.ds(TOK, TOK)


def line_peers():
    dp, x_hi, plane, core = place()
    return [
        ((dp + d) % 2, (x_hi + x) % 2, ((dp + d) % 2, ctx_of((x_hi + x) % 2, plane, core)))
        for d, x in ((1, 0), (0, 1), (1, 1))
    ]


def sum_pieces(pieces, count, rows):
    total = pieces[0, rows, :].astype(F32)
    for i in range(1, count):
        total = total + pieces[i, rows, :].astype(F32)
    return total


def starts(copies):
    for c in copies:
        c.start()


def arrive(copies):
    for c in copies:
        c.wait_recv()


def prepare_spread(r):
    row = lax.broadcasted_iota(jnp.int32, (1024, 1), 0)
    chip, inside = row >> 5, row & 31
    plain = jnp.where(inside < 18, chip * 18 + inside, -1)
    column = lax.broadcasted_iota(jnp.int32, (1024, D), 1)
    r.spread_one[...] = jnp.where(column == plain, 1.0, 0.0).astype(BF)
    target = jnp.where(
        inside < 18,
        plain,
        jnp.where(
            inside < 24,
            D + chip * 6 + inside - 18,
            jnp.where(inside < 30, D + 192 + chip * 6 + inside - 24, -1),
        ),
    )
    column = lax.broadcasted_iota(jnp.int32, (1024, 960), 1)
    r.spread[...] = jnp.where(column == target, 1.0, 0.0).astype(BF)


STEPS = ((0,), (1,), (2, 3))


def layer_kernel(*refs):
    r = SimpleNamespace(**dict(zip(NAMES, refs)))
    dp, x_hi, plane, core = place()
    mine, plane, query_peers, key_peers = groups()
    y, z = plane // 4, plane % 4
    slot = dp * 2 + x_hi
    line = line_peers()
    near = line[0][2]
    sibling = (dp, ctx_of(x_hi, plane, 1 - core))
    others = [
        (1 - dp, ctx_of((x_hi + x) % 2, plane, (core + c) % 2)) for x in range(2) for c in range(2)
    ]
    friends = [d for _, d in query_peers] + [d for _, d in key_peers] + others
    greet(friends)
    done = []
    shards = [r.s_key, r.s_value, r.s_query, r.s_out, r.s_gate, r.s_up, r.s_down]
    fulls = [r.w_key, r.w_value, r.w_query, r.w_out, r.w_gate, r.w_up, r.w_down]
    own_w, first_w, second_w = weight_copies(
        shards, fulls, r.w_own, r.w_send, r.w_recv, r.w_core_send, r.w_core_recv
    )
    starts(own_w)
    r.gain_own[...] = jnp.zeros_like(r.gain_own)
    r.gain_own[0:1, 0:288] = r.gain_a[...].astype(F32)
    r.gain_own[1:2, 0:288] = r.gain_f[...].astype(F32)
    placed = r.gain_own[...]
    r.gain_own[...] = jnp.where(dp == 0, placed, pltpu.roll(placed, 288, 1))
    met(friends)
    gain_copy = remote(r.gain_own, r.gain_got, r.gain_send.at[0], r.gain_recv.at[0], near)
    gain_copy.start()
    starts(first_w[:6])
    done += first_w + second_w + [gain_copy]
    state = r.hidden[...].astype(F32)
    scale_one = lax.rsqrt(jnp.mean(state * state, axis=0, keepdims=True) + eps)
    unit_one = state * scale_one
    run = r.positions[0:1, 0:1].astype(F32) * (1.0 / TOK)
    lane = lax.broadcasted_iota(jnp.int32, (HEAD // 2, 64), 1).astype(F32)
    at_run = lane == run
    cos_a = jnp.sum(jnp.where(at_run, r.run_cos[...], 0.0), axis=1, keepdims=True)
    sin_a = jnp.sum(jnp.where(at_run, r.run_sin[...], 0.0), axis=1, keepdims=True)
    cosine = cos_a * r.in_cos[...] - sin_a * r.in_sin[...]
    sine = sin_a * r.in_cos[...] + cos_a * r.in_sin[...]
    r.tables[0] = cosine
    r.tables[1] = sine
    run_rows = jnp.broadcast_to(run, (16, TOK)).astype(BF)
    gain_copy.wait_recv()
    r.gains[...] = r.gain_own[...] + r.gain_got[...]
    normal_one = flipped((unit_one * gain_rows(r.gains[0:1, :])).astype(BF).astype(F32)).astype(BF)
    r.one_all[OWN, D:WIDE] = jnp.zeros((TOK, WIDE - D), BF)
    r.one_all[OWN, 0:D] = normal_one
    for c, d in zip(first_w[:6], second_w[:6]):
        c.wait_recv()
        d.start()
    for c in own_w[:3]:
        c.wait()
    arrive(second_w[:4])
    keys = flipped(times(normal_one, r.w_key[...]))[0:192]
    keys = turn(keys, KV_HEADS, cosine, sine, 1.0).astype(BF).reshape(192, TOK)
    values = flipped(times(normal_one, r.w_value[...]))[0:192].astype(BF)
    for g in range(KV_HEADS):
        r.kv_all[plane, g * 128 : g * 128 + HEAD, :] = keys[g * HEAD : (g + 1) * HEAD]
        r.kv_all[plane, g * 128 + HEAD : (g + 1) * 128, :] = values[g * HEAD : (g + 1) * HEAD]
    r.kv_all[plane, 384:400, :] = run_rows
    q_copies, kv_copies = [], [None]
    own_kv, own_q = r.kv_all.at[plane], r.q_all.at[mine]
    for o in range(1, KG):
        kv_copies.append(
            remote(own_kv, own_kv, r.kv_send.at[o], r.kv_recv.at[o], key_peers[o - 1][1])
        )
    starts(kv_copies[1:])
    arrive(second_w[4:6])
    query = flipped(times(normal_one, r.w_query[...]))[0:D]
    query = turn(query, HEADS, cosine, sine, 1.0).astype(BF).reshape(D, TOK)
    r.q_all[mine, 0:16, :] = run_rows
    r.q_all[mine, 16:QROWS, :] = query * jnp.asarray(0.125, BF)
    for g in range(KV_HEADS):
        rows = pl.ds(16 + 192 * g, 192) if g else pl.ds(0, 208)
        for o in range(1, QG):
            q_copies.append(
                remote(
                    own_q.at[rows], own_q.at[rows], r.q_send.at[o, g], r.q_recv.at[o, g], query_peers[o - 1][1]
                )
            )
    starts(q_copies + first_w[6:])
    one_copy = remote(
        r.one_all.at[OWN], r.one_all.at[LATE], r.sib_send.at[0], r.sib_recv.at[0], sibling
    )
    one_copy.start()
    done += q_copies + kv_copies[1:] + [one_copy]
    prepare_spread(r)
    r.yd_all[:, OWN] = r.grad_out[...]
    yd_copy = remote(
        r.yd_all.at[:, OWN], r.yd_all.at[:, LATE], r.sib_send.at[1], r.sib_recv.at[1], sibling
    )
    yd_copy.start()
    done.append(yd_copy)
    zeros = jnp.zeros((HEAD, QG * TOK), BF)
    o_copies = []

    def o_copy(o, g):
        a, device = query_peers[o - 1]
        rows = pl.ds(pl.multiple_of(g * 192, 64), 192)
        return remote(
            r.o_buf.at[a, rows], r.o_got.at[mine, rows], r.o_send.at[o, g], r.o_recv.at[o, g], device
        )

    for step, rows_of in enumerate(STEPS):
        bases = [((y + 4 - back) % 4) * 4 for back in rows_of]
        for back, base in zip(rows_of, bases):
            arrive([kv_copies[back * 4 + dz] for dz in range(4) if back * 4 + dz])

            def flip(b, unused, base=base):
                flip_keys(r.kv_all, r.kv_tok, base + b)
                return unused

            lax.fori_loop(0, 4, flip, 0)
        last = step == len(STEPS) - 1

        def three(g, unused, step=step, bases=bases, last=last):
            for i in range(3):
                h = g * 3 + i
                first = pl.multiple_of(h * HEAD, HEAD)
                queries = head_rows(r.q_all, h, 16)
                scores = [
                    scores_of(r.q_all, r.kv_all, r.kv_tok, g, base, queries, zeros)[1]
                    for base in bases
                ]
                new_top = jnp.max(scores[0], axis=0, keepdims=True)
                for more in scores[1:]:
                    new_top = jnp.maximum(new_top, jnp.max(more, axis=0, keepdims=True))
                if step:
                    top = r.top_all[pl.ds(h, 1), :]
                    new_top = jnp.maximum(top, new_top)
                value_rows = pl.ds(pl.multiple_of(g * 128 + HEAD, HEAD), HEAD)
                total, accum = None, None
                for base, back, part in zip(bases, rows_of, scores):
                    probs = jnp.exp(part - new_top)
                    values = jnp.concatenate(
                        [r.kv_all[base + b, value_rows, :] for b in range(CHUNK)], axis=1
                    )
                    part_total = jnp.sum(probs, axis=0, keepdims=True)
                    probs = probs.astype(BF)
                    part_accum = times(values, probs)
                    total = part_total if total is None else total + part_total
                    accum = part_accum if accum is None else accum + part_accum
                if step:
                    fade = jnp.exp(top - new_top)
                    total = total + r.total_all[pl.ds(h, 1), :] * fade
                    accum = accum + r.accum_all[pl.ds(first, HEAD), :] * fade
                if not last:
                    r.top_all[pl.ds(h, 1), :] = new_top
                    r.total_all[pl.ds(h, 1), :] = total
                    r.accum_all[pl.ds(first, HEAD), :] = accum
                    continue
                part = (accum / total).astype(BF)
                for a in range(QG):
                    lanes = slice(a * TOK, (a + 1) * TOK)
                    r.o_buf[a, pl.ds(first, HEAD), :] = part[:, lanes]
                    r.ml_buf[a, pl.ds(h, 1), :] = new_top[:, lanes]
                    r.ml_buf[a, pl.ds(h + 16, 1), :] = total[:, lanes]
            return unused

        if step == 0:
            for g in range(KV_HEADS):
                arrive(q_copies[3 * g : 3 * g + 3])
                lax.fori_loop(g, g + 1, three, 0)
            continue
        if not last:
            lax.fori_loop(0, KV_HEADS, three, 0)
            if step == 1:
                for c, d in zip(first_w[6:], second_w[6:]):
                    c.wait_recv()
                    d.start()
            continue

        def three_and_send(g, unused):
            three(g, unused)
            starts([o_copy(o, g) for o in range(1, QG)])
            return unused

        lax.fori_loop(0, KV_HEADS, three_and_send, 0)
    o_copies += [o_copy(o, g) for o in range(1, QG) for g in range(KV_HEADS)]
    for o in range(1, QG):
        a, device = query_peers[o - 1]
        c = remote(r.ml_buf.at[a], r.ml_got.at[mine], r.ml_send.at[o], r.ml_recv.at[o], device)
        c.start()
        o_copies.append(c)
    done += o_copies
    r.o_got[mine] = r.o_buf[mine]
    r.ml_got[mine] = r.ml_buf[mine]
    for c in own_w[3:]:
        c.wait()
    arrive(second_w[6:])
    arrive(o_copies)
    r.st_own[...] = jnp.zeros_like(r.st_own)
    for h in range(HEADS):
        tops = [r.ml_got[a, pl.ds(h, 1), :] for a in range(QG)]
        best = jnp.maximum(jnp.maximum(tops[0], tops[1]), jnp.maximum(tops[2], tops[3]))
        shares = [r.ml_got[a, pl.ds(h + 16, 1), :] * jnp.exp(tops[a] - best) for a in range(QG)]
        whole = shares[0] + shares[1] + shares[2] + shares[3]
        r.st_own[pl.ds(h, 1), :] = best + jnp.log(whole)
        result = jnp.zeros((HEAD, TOK), F32)
        for a in range(QG):
            result = result + r.o_got[a, pl.ds(h * HEAD, HEAD), :].astype(F32) * (shares[a] / whole)
        r.o_rows[pl.ds(h * HEAD, HEAD), :] = result
    def to_sibling(src, dst, at):
        c = remote(src, dst, r.sib_send.at[at], r.sib_recv.at[at], sibling)
        c.start()
        done.append(c)
        return c

    attended = r.o_rows[...].T.astype(BF)
    r.att_all[OWN, D:WIDE] = jnp.zeros((TOK, WIDE - D), BF)
    r.att_all[OWN, 0:D] = attended
    att_copy = to_sibling(r.att_all.at[OWN], r.att_all.at[LATE], 2)
    gain = r.gains[1:2, 0:D]
    grad_low = r.grad_out[...].astype(F32).T.astype(BF)
    middle = r.hidden[...].astype(F32).T + times(attended, r.w_out[...])
    scale = lax.rsqrt(jnp.mean(middle * middle, axis=-1, keepdims=True) + eps)
    unit = middle * scale
    normal = (unit * gain).astype(BF)
    r.nrm_all[OWN, D:WIDE] = jnp.zeros((TOK, WIDE - D), BF)
    r.nrm_all[OWN, 0:D] = normal
    nrm_copy = to_sibling(r.nrm_all.at[OWN], r.nrm_all.at[LATE], 3)
    gate = times(normal, r.w_gate[...])
    upper = times(normal, r.w_up[...])
    sigma = 1.0 / (1.0 + jnp.exp(-gate))
    silu = gate * sigma
    inner = (silu * upper).astype(BF)
    for c in range(2):
        for d in range(2):
            first = 768 * d + QUARTER * c
            r.in_parts[c, :, QUARTER * d : QUARTER * (d + 1)] = inner[:, first : first + QUARTER]
    in_copy = to_sibling(r.in_parts.at[1 - core], r.in_all.at[LATE], 4)
    r.in_all[OWN, :] = r.in_parts[core]
    grad_inner = times(grad_low, r.w_down[...])
    grad_gate = (grad_inner * upper * sigma * (1.0 + gate * (1.0 - sigma))).astype(BF)
    grad_up = (grad_inner * silu).astype(BF)
    gate_flat = grad_gate.astype(F32).T.astype(BF)
    up_flat = grad_up.astype(F32).T.astype(BF)
    for c in range(2):
        r.yg_parts[c, 0:768, :] = gate_flat[768 * c : 768 * (c + 1)]
        r.yg_parts[c, 768:1536, :] = up_flat[768 * c : 768 * (c + 1)]
    yg_copy = to_sibling(r.yg_parts.at[1 - core], r.yg_all.at[:, LATE], 5)
    r.yg_all[:, OWN] = r.yg_parts[core]
    grad_normal = across(grad_gate, r.w_gate[...]) + across(grad_up, r.w_up[...])
    r.gn_own[...] = jnp.zeros_like(r.gn_own)
    r.gn_own[1:2, 0:D] = jnp.sum(grad_normal * unit, axis=0, keepdims=True)
    grad_unit = grad_normal * gain
    back = (
        scale * (grad_unit - unit * jnp.mean(grad_unit * unit, axis=-1, keepdims=True))
        + grad_low.astype(F32)
    )
    branch = back.astype(BF)
    grads_low = across(r.w_out[...], branch).astype(BF)
    r.do_all[mine] = grads_low
    for h in range(HEADS):
        rows = slice(h * HEAD, (h + 1) * HEAD)
        r.st_own[16 + h : 17 + h, :] = jnp.sum(
            grads_low[rows].astype(F32) * r.o_rows[rows, :], axis=0, keepdims=True
        )
    r.st_all[mine] = r.st_own[...]
    st_copies = []
    own_do, own_st = r.do_all.at[mine], r.st_all.at[mine]
    for o in range(1, QG):
        device = query_peers[o - 1][1]
        st_copies.append(remote(own_st, own_st, r.st_send.at[o], r.st_recv.at[o], device))

    def do_copy(o, g):
        rows = own_do.at[pl.ds(pl.multiple_of(g * 192, 64), 192)]
        return remote(rows, rows, r.do_send.at[o, g], r.do_recv.at[o, g], query_peers[o - 1][1])

    starts(st_copies)
    for g in range(KV_HEADS):
        starts([do_copy(o, g) for o in range(1, QG)])
    done += st_copies + [do_copy(o, g) for o in range(1, QG) for g in range(KV_HEADS)]
    o_part = across(r.spread_one[...], branch).astype(BF)
    r.yo_parts[0] = o_part[0:512]
    r.yo_parts[1] = o_part[512:1024]
    yo_copy = to_sibling(r.yo_parts.at[1 - core], r.yo_all.at[:, LATE], 6)
    r.yo_all[:, OWN] = r.yo_parts[core]
    r.back[...] = flipped(back)[0:D]
    arrive([yd_copy, in_copy])
    part = times(r.yd_all[...], r.in_all[...]).astype(BF)
    for x in range(2):
        for d in range(2):
            r.gd[x, d] = part[288 * x : 288 * (x + 1), QUARTER * d : QUARTER * (d + 1)]
    d_sends = []
    for i, (d, x, device) in enumerate(line):
        d_sends.append(remote(r.gd.at[x, d], r.rd.at[slot], r.d_send.at[i], r.d_recv.at[i], device))
    starts(d_sends)
    r.rd[slot] = r.gd[x_hi, dp]
    arrive([nrm_copy, yg_copy])
    gate_part = times(r.yg_all[0:768, :], r.nrm_all[...]).astype(BF).reshape(KG, 48, WIDE)
    up_part = times(r.yg_all[768:1536, :], r.nrm_all[...]).astype(BF).reshape(KG, 48, WIDE)
    arrive([att_copy, yo_copy])
    out_part = times(r.yo_all[...], r.att_all[...]).astype(BF).reshape(KG, 32, WIDE)
    for j in range(KG):
        r.g1[j // 4, j % 4, 0:32, :] = out_part[j]
        r.g1[j // 4, j % 4, 32:64, :] = gate_part[j, 0:32]
        r.g2[j % 4, j // 4, 0:16, :] = gate_part[j, 32:48]
        r.g2[j % 4, j // 4, 16:64, :] = up_part[j]
    a_sends, b_sends, p_sends = [], [], []
    for i in range(1, 4):
        y_to, z_to = (y + i) % 4, (z + i) % 4
        along_y = (dp, ctx_of(x_hi, y_to * 4 + z, core))
        along_z = (dp, ctx_of(x_hi, y * 4 + z_to, core))
        a_sends.append(
            remote(r.g1.at[y_to], r.r1.at[y], r.a_send.at[0, i], r.a_recv.at[0, i], along_y)
        )
        a_sends.append(
            remote(r.g2.at[z_to], r.r2.at[z], r.a_send.at[1, i], r.a_recv.at[1, i], along_z)
        )
        b_sends.append(
            remote(r.s1.at[z_to], r.t1.at[z], r.b_send.at[0, i], r.b_recv.at[0, i], along_z)
        )
        b_sends.append(
            remote(r.s2.at[y_to], r.t2.at[y], r.b_send.at[1, i], r.b_recv.at[1, i], along_y)
        )
    starts(a_sends)
    r.r1[y] = r.g1[y]
    r.r2[z] = r.g2[z]
    for o in range(1, KG):
        j, device = key_peers[o - 1]
        p_sends.append(
            remote(r.gp.at[j], r.rp.at[plane], r.p_send.at[o], r.p_recv.at[o], device)
        )
    done += d_sends + a_sends + b_sends + p_sends
    arrive(st_copies)

    def dkv_copy(o, g):
        j, device = key_peers[o - 1]
        rows = pl.ds(pl.multiple_of(g * 128, 128), 128)
        return remote(
            r.dkv_buf.at[j, rows], r.dkv_got.at[plane, rows], r.dkv_send.at[o, g], r.dkv_recv.at[o, g], device
        )

    def dq_copy(o, g):
        a, device = query_peers[o - 1]
        rows = pl.ds(pl.multiple_of(g * 192, 64), 192)
        return remote(
            r.dq_buf.at[a, rows], r.dq_got.at[mine, rows], r.dq_send.at[o, g], r.dq_recv.at[o, g], device
        )

    def key_head(g, unused):
        arrive([do_copy(o, g) for o in range(1, QG)])
        for c in (1, 2, 3, 0):
            base = ((y + c) % 4) * 4
            key_term, value_term = None, None
            for i in range(3):
                h = g * 3 + i
                queries = head_rows(r.q_all, h, 16)
                grads = head_rows(r.do_all, h)
                lse = jnp.concatenate([r.st_all[a, pl.ds(h, 1), :] for a in range(QG)], axis=1)
                delta = jnp.concatenate([r.st_all[a, pl.ds(h + 16, 1), :] for a in range(QG)], axis=1)
                keys, scores = scores_of(r.q_all, r.kv_all, r.kv_tok, g, base, queries, zeros)
                probs = jnp.exp(scores - lse)
                grad_probs = times(keys, jnp.concatenate([zeros, grads], axis=0))
                grad_scores = (probs * (grad_probs - delta)).astype(BF)
                key_rows = pl.ds(pl.multiple_of(g * 128, 128), HEAD)
                flat_keys = jnp.concatenate(
                    [r.kv_all[base + b, key_rows, :] for b in range(CHUNK)], axis=1
                )
                part = times(flat_keys, grad_scores)
                rows = slice(i * HEAD, (i + 1) * HEAD)
                r.dq_acc[rows, :] = part if c == 1 else r.dq_acc[rows, :] + part
                key_part = across(queries, grad_scores)
                value_part = across(grads, probs.astype(BF))
                key_term = key_part if key_term is None else key_term + key_part
                value_term = value_part if value_term is None else value_term + value_part
            first = pl.multiple_of(g * 128, 128)
            for b in range(CHUNK):
                lanes = slice(b * TOK, (b + 1) * TOK)
                r.dkv_buf[base + b, pl.ds(first, HEAD), :] = key_term[:, lanes].astype(BF)
                r.dkv_buf[base + b, pl.ds(pl.multiple_of(first + HEAD, HEAD), HEAD), :] = (
                    value_term[:, lanes].astype(BF)
                )
            starts([dkv_copy(c * 4 + dz, g) for dz in range(4) if c * 4 + dz])
        rows = pl.ds(pl.multiple_of(g * 192, 64), 192)
        for a in range(QG):
            r.dq_buf[a, rows, :] = r.dq_acc[:, a * TOK : (a + 1) * TOK].astype(BF)
        starts([dq_copy(o, g) for o in range(1, QG)])

        return unused

    lax.fori_loop(0, KV_HEADS, key_head, 0)
    sends = [dkv_copy(o, g) for o in range(1, KG) for g in range(KV_HEADS)]
    sends += [dq_copy(o, g) for o in range(1, QG) for g in range(KV_HEADS)]
    r.dq_got[mine] = r.dq_buf[mine]
    r.dkv_got[plane] = r.dkv_buf[plane]
    arrive(a_sends)
    for i in range(4):
        for pieces, sums in ((r.r1, r.s1), (r.r2, r.s2)):
            total = pieces[0, i].astype(F32)
            for j in range(1, 4):
                total = total + pieces[j, i].astype(F32)
            sums[i] = total.astype(BF)
    starts(b_sends)
    arrive(d_sends)
    total = sum_pieces(r.rd, 4, slice(None)).astype(BF)
    r.gp[...] = times(r.spread_one[0:512, 0:288], total).astype(BF).reshape(KG, 32, QUARTER)
    r.rp[plane] = r.gp[plane]
    r.t1[z] = r.s1[z]
    r.t2[y] = r.s2[y]
    collector = core == x_hi

    def toward(target_dp, src, dst, send, recv):
        device = (target_dp, ctx_of(core, plane, core))
        lanes = pl.ds(pl.multiple_of(target_dp * 256, 128), QUARTER)
        return remote(src.at[:, lanes], dst.at[slot], send.at[target_dp], recv.at[slot], device)

    def pass_on(src, dst, send, recv):
        for target_dp in range(2):
            here = jnp.logical_and(collector, dp == target_dp)

            @pl.when(jnp.logical_not(here))
            def _():
                toward(target_dp, src, dst, send, recv).start()

            @pl.when(here)
            def _():
                dst[slot] = src[:, target_dp * 256 : target_dp * 256 + QUARTER]

    arrive(sends)
    done += sends
    cosine, sine = r.tables[0], r.tables[1]
    total = r.dq_got[0].astype(F32)
    for a in range(1, QG):
        total = total + r.dq_got[a].astype(F32)
    dq = turn(total * 0.125, HEADS, cosine, sine, -1.0).astype(BF).reshape(D, TOK)
    total = r.dkv_got[0].astype(F32)
    for j in range(1, KG):
        total = total + r.dkv_got[j].astype(F32)
    total = total.reshape(KV_HEADS, 2, HEAD, TOK)
    dk = turn(total[:, 0], KV_HEADS, cosine, sine, -1.0).astype(BF).reshape(192, TOK)
    dv = total[:, 1].astype(BF).reshape(192, TOK)
    placed = times(r.spread[...], jnp.concatenate([dq, dk, dv], axis=0)).astype(BF)
    r.yq_parts[0] = placed[0:512]
    r.yq_parts[1] = placed[512:1024]
    yq_copy = to_sibling(r.yq_parts.at[1 - core], r.yq_all.at[:, LATE], 7)
    r.yq_all[:, OWN] = r.yq_parts[core]
    first = times(r.w_query[...], dq) + times(r.w_key[...], dk) + times(r.w_value[...], dv)
    state = r.hidden[...].astype(F32)
    scale = lax.rsqrt(jnp.mean(state * state, axis=0, keepdims=True) + eps)
    unit = state * scale
    terms = jnp.concatenate([first * unit, jnp.zeros((WIDE - D, TOK), F32)], axis=0).T
    r.gn_own[0:1, :] = jnp.sum(terms, axis=0, keepdims=True)
    gn_copy = to_sibling(r.gn_own, r.gn_all, 8)
    grad_unit = first * gain_rows(r.gains[0:1, :])
    r.grad[...] = (
        scale * (grad_unit - unit * jnp.mean(grad_unit * unit, axis=0, keepdims=True))
        + r.back[...]
    )
    arrive([one_copy, yq_copy, gn_copy])
    part = times(r.yq_all[...], r.one_all[...]).reshape(KG, 32, WIDE)
    sums = r.gn_own[...] + r.gn_all[...]
    line_of = lax.broadcasted_iota(jnp.int32, (KG, 32, WIDE), 1)
    part = jnp.where(line_of == 30, sums[0:1][None], part)
    part = jnp.where(line_of == 31, sums[1:2][None], part)
    r.gq[...] = part.astype(BF)
    q_sends = []
    for o in range(1, KG):
        j, device = key_peers[o - 1]
        q_sends.append(
            remote(r.gq.at[j], r.rq.at[plane], r.gq_send.at[o], r.gq_recv.at[o], device)
        )
    starts(q_sends + p_sends)
    done += q_sends
    r.rq[plane] = r.gq[plane]
    r.output[...] = flipped(middle + across(inner, r.w_down[...]))[0:D].astype(BF)
    arrive(b_sends)
    r.sa[0:64, :] = sum_pieces(r.t1, 4, slice(0, 64)).astype(BF)
    r.sa[64:128, :] = sum_pieces(r.t2, 4, slice(0, 64)).astype(BF)
    pass_on(r.sa, r.wa, r.wa_send, r.wa_recv)

    def collect(src, dst, send, recv, rows, at):
        part = r.fa.at[rows]
        passed = remote(part, part, r.f_send.at[at], r.f_recv.at[at], sibling)

        @pl.when(collector)
        def _():
            for source in range(4):

                @pl.when(slot != source)
                def _():
                    remote(
                        src.at[:, pl.ds(0, QUARTER)], dst.at[source], send.at[0], recv.at[source], sibling
                    ).wait_recv()

            part[...] = sum_pieces(dst, 4, slice(None))
            passed.start()

        return passed

    moves = ((r.sa, r.wa, r.wa_send, r.wa_recv), (r.sq, r.wb, r.wb_send, r.wb_recv))
    arrive(q_sends)
    r.sq[...] = sum_pieces(r.rq, KG, slice(0, 32)).astype(BF)
    pass_on(r.sq, r.wb, r.wb_send, r.wb_recv)
    arrive(p_sends)
    r.fd[core] = sum_pieces(r.rp, KG, slice(0, 32))
    final = remote(r.fd.at[core], r.fd.at[core], r.f_send.at[0], r.f_recv.at[0], sibling)
    final.start()
    early = collect(*moves[0], pl.ds(32, GROWS), 1)
    late = collect(*moves[1], pl.ds(0, 32), 2)
    final.wait_recv()
    done.append(final)

    @pl.when(collector)
    def _():
        early.wait_send()
        late.wait_send()

    @pl.when(jnp.logical_not(collector))
    def _():
        early.wait_recv()
        late.wait_recv()

    for target_dp in range(2):

        @pl.when(jnp.logical_not(jnp.logical_and(collector, dp == target_dp)))
        def _():
            for move in moves:
                toward(target_dp, *move).wait_send()

    for c in done:
        c.wait_send()


INPUTS = (
    "hidden",
    "positions",
    "run_cos",
    "run_sin",
    "in_cos",
    "in_sin",
    "gain_a",
    "gain_f",
    "grad_out",
    "s_key",
    "s_value",
    "s_query",
    "s_out",
    "s_gate",
    "s_up",
    "s_down",
)
OUTPUTS = (
    ("output", (D, TOK), BF),
    ("grad", (D, TOK), F32),
    ("fa", (AROWS, QUARTER), F32),
    ("fd", (2, 32, QUARTER), F32),
)
SCRATCH = (
    ("gain_own", (8, WIDE), F32),
    ("gain_got", (8, WIDE), F32),
    ("gains", (8, WIDE), F32),
    ("tables", (2, HEAD // 2, TOK), F32),
    ("w_key", (D, 192), BF),
    ("w_value", (D, 192), BF),
    ("w_query", (D, D), BF),
    ("w_out", (D, D), BF),
    ("w_gate", (D, FF), BF),
    ("w_up", (D, FF), BF),
    ("w_down", (D, FF), BF),
    ("q_all", (QG, QROWS, TOK), BF),
    ("kv_all", (KG, KROWS, TOK), BF),
    ("kv_tok", (KV_HEADS, KG * TOK, 128), BF),
    ("accum_all", (D, QG * TOK), F32),
    ("top_all", (16, QG * TOK), F32),
    ("total_all", (16, QG * TOK), F32),
    ("o_buf", (QG, D, TOK), BF),
    ("o_got", (QG, D, TOK), BF),
    ("ml_buf", (QG, 32, TOK), F32),
    ("ml_got", (QG, 32, TOK), F32),
    ("o_rows", (D, TOK), F32),
    ("st_own", (32, TOK), F32),
    ("st_all", (QG, 32, TOK), F32),
    ("do_all", (QG, D, TOK), BF),
    ("spread_one", (1024, D), BF),
    ("spread", (1024, 960), BF),
    ("one_all", (2 * TOK, WIDE), BF),
    ("att_all", (2 * TOK, WIDE), BF),
    ("nrm_all", (2 * TOK, WIDE), BF),
    ("in_parts", (2, TOK, 2 * QUARTER), BF),
    ("in_all", (2 * TOK, 2 * QUARTER), BF),
    ("yd_all", (D, 2 * TOK), BF),
    ("yg_parts", (2, 1536, TOK), BF),
    ("yg_all", (1536, 2 * TOK), BF),
    ("yo_parts", (2, 512, TOK), BF),
    ("yo_all", (512, 2 * TOK), BF),
    ("yq_parts", (2, 512, TOK), BF),
    ("yq_all", (512, 2 * TOK), BF),
    ("gn_own", (8, WIDE), F32),
    ("gn_all", (8, WIDE), F32),
    ("back", (D, TOK), F32),
    ("gd", (2, 2, 288, QUARTER), BF),
    ("rd", (4, 288, QUARTER), BF),
    ("gp", (KG, 32, QUARTER), BF),
    ("rp", (KG, 32, QUARTER), BF),
    ("g1", (4, 4, 64, WIDE), BF),
    ("g2", (4, 4, 64, WIDE), BF),
    ("r1", (4, 4, 64, WIDE), BF),
    ("r2", (4, 4, 64, WIDE), BF),
    ("s1", (4, 64, WIDE), BF),
    ("s2", (4, 64, WIDE), BF),
    ("t1", (4, 64, WIDE), BF),
    ("t2", (4, 64, WIDE), BF),
    ("sa", (GROWS, WIDE), BF),
    ("gq", (KG, 32, WIDE), BF),
    ("rq", (KG, 32, WIDE), BF),
    ("sq", (32, WIDE), BF),
    ("wa", (4, GROWS, QUARTER), BF),
    ("wb", (4, 32, QUARTER), BF),
    ("dq_acc", (192, QG * TOK), F32),
    ("dq_buf", (QG, D, TOK), BF),
    ("dq_got", (QG, D, TOK), BF),
    ("dkv_buf", (KG, 384, TOK), BF),
    ("dkv_got", (KG, 384, TOK), BF),
)
SEMAPHORES = (
    ("w_own", (7,)),
    ("w_send", (7, 2)),
    ("w_recv", (7, 2)),
    ("w_core_send", (7, 2)),
    ("w_core_recv", (7, 2)),
    ("gain_send", (1,)),
    ("gain_recv", (1,)),
    ("q_send", (QG, KV_HEADS)),
    ("q_recv", (QG, KV_HEADS)),
    ("kv_send", (KG,)),
    ("kv_recv", (KG,)),
    ("o_send", (QG, KV_HEADS)),
    ("o_recv", (QG, KV_HEADS)),
    ("ml_send", (QG,)),
    ("ml_recv", (QG,)),
    ("sib_send", (9,)),
    ("sib_recv", (9,)),
    ("do_send", (QG, KV_HEADS)),
    ("do_recv", (QG, KV_HEADS)),
    ("st_send", (QG,)),
    ("st_recv", (QG,)),
    ("d_send", (3,)),
    ("d_recv", (3,)),
    ("a_send", (2, 4)),
    ("a_recv", (2, 4)),
    ("b_send", (2, 4)),
    ("b_recv", (2, 4)),
    ("p_send", (KG,)),
    ("p_recv", (KG,)),
    ("dkv_send", (KG, KV_HEADS)),
    ("dkv_recv", (KG, KV_HEADS)),
    ("dq_send", (QG, KV_HEADS)),
    ("dq_recv", (QG, KV_HEADS)),
    ("f_send", (3,)),
    ("f_recv", (3,)),
    ("gq_send", (KG,)),
    ("gq_recv", (KG,)),
    ("wa_send", (2,)),
    ("wa_recv", (4,)),
    ("wb_send", (2,)),
    ("wb_recv", (4,)),
)
NAMES = (
    list(INPUTS)
    + [name for name, _, _ in OUTPUTS]
    + [name for name, _, _ in SCRATCH]
    + [name for name, _ in SEMAPHORES]
)


def layer(hidden, positions, gain_attn, gain_ffn, grad_out, shards):
    freqs = rope_base ** (-(np.arange(HEAD // 2, dtype=np.float64) * 2.0 / HEAD))[:, None]
    runs = freqs * (np.arange(64, dtype=np.float64) * TOK)[None]
    inside = freqs * np.arange(TOK, dtype=np.float64)[None]
    tables = [f(a).astype(np.float32) for a in (runs, inside) for f in (np.cos, np.sin)]
    return pl.pallas_call(
        layer_kernel,
        out_shape=[jax.ShapeDtypeStruct(shape, kind) for _, shape, kind in OUTPUTS],
        in_specs=[VM] * 9 + [ANY] * 7,
        out_specs=[VM] * len(OUTPUTS),
        scratch_shapes=[pltpu.VMEM(shape, kind) for _, shape, kind in SCRATCH]
        + [pltpu.SemaphoreType.DMA(shape) for _, shape in SEMAPHORES],
        compiler_params=params(1),
    )(hidden, positions, *[jnp.asarray(t) for t in tables], gain_attn, gain_ffn, grad_out, *shards)


def finish_kernel(fa, fd, grad, result, *outs):
    core = lax.axis_index("ctx") % 2
    dp = lax.axis_index("dp")
    rows = jnp.where(dp == 0, fa[...], pltpu.roll(fa[...], QUARTER - 32, 1))[:, 0:288]
    down = jnp.concatenate([fd[0], fd[1]], axis=1)
    for out, count, block, at in zip(
        outs[:7], (9, 3, 3, 9, 24, 24, 9), (rows,) * 6 + (down,), (0, 18, 24, 32, 64, 112, 0)
    ):
        part = jnp.where(core == 0, block[at : at + count], block[at + count : at + 2 * count])
        if count == 24:
            out[0] = part
        else:
            for i in range(count):
                out[i] = part[i : i + 1]
    outs[7][...] = rows[30:31]
    outs[8][...] = rows[31:32]
    outs[9][...] = grad[...]
    outs[10][...] = result[...]


def finish(fa, fd, grad, result):
    shape = jax.ShapeDtypeStruct
    return pl.pallas_call(
        finish_kernel,
        out_shape=[
            shape((9, 1, 288), F32),
            shape((3, 1, 288), F32),
            shape((3, 1, 288), F32),
            shape((9, 1, 288), F32),
            shape((1, 24, 288), F32),
            shape((1, 24, 288), F32),
            shape((9, 1, 768), F32),
            shape((1, 288), F32),
            shape((1, 288), F32),
            shape((D, TOK), F32),
            shape((D, TOK), BF),
        ],
        in_specs=[VM] * 4,
        out_specs=[VM] * 11,
    )(fa, fd, grad, result)


def local(
    hidden, positions, w_query, w_key, w_value, w_out, w_gate, w_up, w_down,
    gain_attn, gain_ffn, grad_out,
):
    output, grad_input, fa, fd = layer(
        hidden[0].T,
        positions,
        gain_attn,
        gain_ffn,
        grad_out[0].T,
        [w[0] for w in (w_key, w_value, w_query, w_out, w_gate, w_up)] + [w_down[0].T],
    )
    *grads, gain_one, gain_two, grad_input, output = finish(fa, fd, grad_input, output)
    columns = [
        g.transpose(0, 2, 1) if g.shape[0] == 1 else g.transpose(1, 2, 0) for g in grads
    ]
    return (output.T[None], grad_input.T[None]) + tuple(columns) + (gain_one, gain_two)


def solution(mesh):
    in_specs = (
        P("dp", "ctx", None),
        P("dp", "ctx"),
    ) + (P(None, "dp", None),) * 7 + (
        P(None, "dp"),
        P(None, "dp"),
        P("dp", "ctx", None),
    )
    out_specs = (
        P("dp", "ctx", None),
        P("dp", "ctx", None),
    ) + (P(None, "dp", "ctx"),) * 7 + (
        P(None, "dp"),
        P(None, "dp"),
    )
    return jax.shard_map(local, mesh=mesh, in_specs=in_specs, out_specs=out_specs, check_vma=False)
```

```python
from types import SimpleNamespace

import jax
import jax.numpy as jnp
import numpy as np
from jax import lax
from jax.experimental import pallas as pl
from jax.experimental.pallas import tpu as pltpu
from jax.sharding import PartitionSpec as P

HEADS = 9
KV_HEADS = 3
HEAD = 64
TOK = 128
D = 576
FF = 1536
QG = 4
KG = 16
WIDE = 640
eps = 1e-05
rope_base = 100000.0
MESH = pl.DeviceIdType.MESH
BF = jnp.bfloat16
F32 = jnp.float32
LIMIT = 56 * 1024 * 1024
VM = pl.BlockSpec(memory_space=pltpu.VMEM)
ANY = pl.BlockSpec(memory_space=pl.ANY)


def params(ident):
    return pltpu.CompilerParams(
        collective_id=ident, has_side_effects=True, vmem_limit_bytes=LIMIT
    )


def place():
    dp = lax.axis_index("dp")
    ctx = lax.axis_index("ctx")
    x_hi = ctx // 32
    plane = (ctx // 2) % 16
    core = ctx % 2
    return dp, x_hi, plane, core


def ctx_of(x_hi, plane, core):
    return x_hi * 32 + plane * 2 + core


def remote(src, dst, send, recv, device):
    return pltpu.make_async_remote_copy(
        src_ref=src,
        dst_ref=dst,
        send_sem=send,
        recv_sem=recv,
        device_id=device,
        device_id_type=MESH,
    )


def greet(devices):
    barrier = pltpu.get_barrier_semaphore()
    for device in devices:
        pl.semaphore_signal(barrier, inc=1, device_id=device, device_id_type=MESH)


def met(devices):
    pl.semaphore_wait(pltpu.get_barrier_semaphore(), len(devices))


def plane_peer(plane, offset):
    y, z = plane // 4, plane % 4
    return ((y + offset // 4) % 4) * 4 + (z + offset % 4) % 4


def plane_source(plane, offset):
    y, z = plane // 4, plane % 4
    return ((y + 4 - offset // 4) % 4) * 4 + (z + 4 - offset % 4) % 4


def weight_copies(shards, fulls, own_sem, send, recv, core_send, core_recv):
    dp, x_hi, plane, core = place()
    near = (1 - dp, ctx_of(x_hi, plane, core))
    far = (1 - dp, ctx_of(1 - x_hi, plane, core))
    sibling = (dp, ctx_of(x_hi, plane, 1 - core))
    own, first, second = [], [], []
    for which, (shard, full) in enumerate(zip(shards, fulls)):
        rows = shard.shape[0]
        half = rows // 2
        cut = 80 if rows == 288 else half // 2
        by_rows = full.shape[0] != rows

        def part(dp_of, off, size):
            if by_rows:
                return full.at[pl.ds(pl.multiple_of(dp_of * rows + off, 16), size)]
            width = shard.shape[1]
            return full.at[
                pl.ds(pl.multiple_of(off, 16), size), pl.ds(pl.multiple_of(dp_of * width, 128), width)
            ]

        own.append(pltpu.make_async_copy(shard, part(dp, 0, rows), own_sem.at[which]))
        for role, target in ((0, near), (1, far)):
            off = pl.multiple_of(role * cut + core * half, 16)
            size = half - cut if role else cut
            first.append(
                remote(
                    shard.at[pl.ds(off, size)],
                    part(dp, off, size),
                    send.at[which, role],
                    recv.at[which, role],
                    target,
                )
            )
            got = part(1 - dp, off, size)
            second.append(
                remote(got, got, core_send.at[which, role], core_recv.at[which, role], sibling)
            )
    return own, first, second


QROWS = D + 16
KROWS = 384 + 16
CHUNK = 4


def groups():
    dp, x_hi, plane, core = place()
    mine = x_hi * 2 + core
    query_peers = []
    for o in range(1, QG):
        a = (mine + o) % QG
        query_peers.append((a, (dp, ctx_of(a // 2, plane, a % 2))))
    key_peers = []
    for o in range(1, KG):
        j = plane_peer(plane, o)
        key_peers.append((j, (dp, ctx_of(x_hi, j, core))))
    return mine, plane, query_peers, key_peers


def flip_keys(kv_all, kv_tok, j):
    for g in range(KV_HEADS):
        block = kv_all[j, pl.ds(g * 128, 128), :].astype(F32)
        kv_tok[g, pl.ds(pl.multiple_of(j * TOK, TOK), TOK), :] = block.T.astype(BF)


def masks_of(q_all, kv_all, base):
    lane = lax.broadcasted_iota(jnp.int32, (1, TOK), 1).astype(F32)
    q_pos = jnp.concatenate(
        [q_all[a, pl.ds(0, 16), :].astype(F32)[0:1] * TOK + lane for a in range(QG)], axis=1
    )
    rows = lax.broadcasted_iota(jnp.int32, (TOK, QG * TOK), 0).astype(F32)
    parts = []
    for b in range(CHUNK):
        start = kv_all[base + b, pl.ds(384, 16), :].astype(F32)[0:1] * TOK
        start = jnp.concatenate([start] * QG, axis=1)
        parts.append(rows <= (q_pos - start))
    return jnp.concatenate(parts, axis=0)


def head_rows(ref, h, skip=0):
    first = pl.multiple_of(h * HEAD + skip, 16)
    return jnp.concatenate([ref[a, pl.ds(first, HEAD), :] for a in range(QG)], axis=1)


def scores_of(q_all, kv_all, kv_tok, g, base, queries, zeros):
    keys = kv_tok[g, pl.ds(pl.multiple_of(base * TOK, TOK), CHUNK * TOK), :]
    scores = jnp.dot(keys, jnp.concatenate([queries, zeros], axis=0), preferred_element_type=F32)
    return keys, jnp.where(masks_of(q_all, kv_all, base), scores, -1e30)


def turn(rows, heads, cosine, sine, sign):
    parts = rows.reshape(heads, 2, HEAD // 2, TOK)
    one, two = parts[:, 0], parts[:, 1]
    first = one * cosine - sign * two * sine
    second = two * cosine + sign * one * sine
    return jnp.concatenate([first[:, None], second[:, None]], axis=1)


def flipped(rows):
    wide = (rows.shape[1] + 127) // 128 * 128
    if wide != rows.shape[1]:
        rows = jnp.concatenate(
            [rows, jnp.zeros((rows.shape[0], wide - rows.shape[1]), rows.dtype)], axis=1
        )
    return rows.T


def gain_rows(row):
    return jnp.broadcast_to(row, (TOK, WIDE)).T[0:D]


def across(left, right):
    return lax.dot_general(left, right, (((1,), (1,)), ((), ())), preferred_element_type=F32)


def times(left, right):
    return jnp.dot(left, right, preferred_element_type=F32)


GROWS = 128
AROWS = 32 + GROWS
QUARTER = 384
OWN, LATE = pl.ds(0, TOK), pl.ds(TOK, TOK)


def line_peers():
    dp, x_hi, plane, core = place()
    return [
        ((dp + d) % 2, (x_hi + x) % 2, ((dp + d) % 2, ctx_of((x_hi + x) % 2, plane, core)))
        for d, x in ((1, 0), (0, 1), (1, 1))
    ]


def sum_pieces(pieces, count, rows):
    total = pieces[0, rows, :].astype(F32)
    for i in range(1, count):
        total = total + pieces[i, rows, :].astype(F32)
    return total


def starts(copies):
    for c in copies:
        c.start()


def arrive(copies):
    for c in copies:
        c.wait_recv()


def prepare_spread(r):
    row = lax.broadcasted_iota(jnp.int32, (1024, 1), 0)
    chip, inside = row >> 5, row & 31
    plain = jnp.where(inside < 18, chip * 18 + inside, -1)
    column = lax.broadcasted_iota(jnp.int32, (1024, D), 1)
    r.spread_one[...] = jnp.where(column == plain, 1.0, 0.0).astype(BF)
    target = jnp.where(
        inside < 18,
        plain,
        jnp.where(
            inside < 24,
            D + chip * 6 + inside - 18,
            jnp.where(inside < 30, D + 192 + chip * 6 + inside - 24, -1),
        ),
    )
    column = lax.broadcasted_iota(jnp.int32, (1024, 960), 1)
    r.spread[...] = jnp.where(column == target, 1.0, 0.0).astype(BF)


STEPS = ((0,), (1,), (2, 3))


def layer_kernel(*refs):
    r = SimpleNamespace(**dict(zip(NAMES, refs)))
    dp, x_hi, plane, core = place()
    mine, plane, query_peers, key_peers = groups()
    y, z = plane // 4, plane % 4
    slot = dp * 2 + x_hi
    line = line_peers()
    near = line[0][2]
    sibling = (dp, ctx_of(x_hi, plane, 1 - core))
    others = [
        (1 - dp, ctx_of((x_hi + x) % 2, plane, (core + c) % 2)) for x in range(2) for c in range(2)
    ]
    friends = [d for _, d in query_peers] + [d for _, d in key_peers] + others
    greet(friends)
    done = []
    shards = [r.s_key, r.s_value, r.s_query, r.s_out, r.s_gate, r.s_up, r.s_down]
    fulls = [r.w_key, r.w_value, r.w_query, r.w_out, r.w_gate, r.w_up, r.w_down]
    own_w, first_w, second_w = weight_copies(
        shards, fulls, r.w_own, r.w_send, r.w_recv, r.w_core_send, r.w_core_recv
    )
    starts(own_w)
    r.gain_own[...] = jnp.zeros_like(r.gain_own)
    r.gain_own[0:1, 0:288] = r.gain_a[...].astype(F32)
    r.gain_own[1:2, 0:288] = r.gain_f[...].astype(F32)
    placed = r.gain_own[...]
    r.gain_own[...] = jnp.where(dp == 0, placed, pltpu.roll(placed, 288, 1))
    met(friends)
    gain_copy = remote(r.gain_own, r.gain_got, r.gain_send.at[0], r.gain_recv.at[0], near)
    gain_copy.start()
    starts(first_w[:6])
    done += first_w + second_w + [gain_copy]
    state = r.hidden[...].astype(F32)
    scale_one = lax.rsqrt(jnp.mean(state * state, axis=0, keepdims=True) + eps)
    unit_one = state * scale_one
    run = r.positions[0:1, 0:1].astype(F32) * (1.0 / TOK)
    lane = lax.broadcasted_iota(jnp.int32, (HEAD // 2, 64), 1).astype(F32)
    at_run = lane == run
    cos_a = jnp.sum(jnp.where(at_run, r.run_cos[...], 0.0), axis=1, keepdims=True)
    sin_a = jnp.sum(jnp.where(at_run, r.run_sin[...], 0.0), axis=1, keepdims=True)
    cosine = cos_a * r.in_cos[...] - sin_a * r.in_sin[...]
    sine = sin_a * r.in_cos[...] + cos_a * r.in_sin[...]
    r.tables[0] = cosine
    r.tables[1] = sine
    run_rows = jnp.broadcast_to(run, (16, TOK)).astype(BF)
    gain_copy.wait_recv()
    r.gains[...] = r.gain_own[...] + r.gain_got[...]
    normal_one = flipped((unit_one * gain_rows(r.gains[0:1, :])).astype(BF).astype(F32)).astype(BF)
    r.one_all[OWN, D:WIDE] = jnp.zeros((TOK, WIDE - D), BF)
    r.one_all[OWN, 0:D] = normal_one
    for c, d in zip(first_w[:6], second_w[:6]):
        c.wait_recv()
        d.start()
    for c in own_w[:3]:
        c.wait()
    arrive(second_w[:4])
    keys = flipped(times(normal_one, r.w_key[...]))[0:192]
    keys = turn(keys, KV_HEADS, cosine, sine, 1.0).astype(BF).reshape(192, TOK)
    values = flipped(times(normal_one, r.w_value[...]))[0:192].astype(BF)
    for g in range(KV_HEADS):
        r.kv_all[plane, g * 128 : g * 128 + HEAD, :] = keys[g * HEAD : (g + 1) * HEAD]
        r.kv_all[plane, g * 128 + HEAD : (g + 1) * 128, :] = values[g * HEAD : (g + 1) * HEAD]
    r.kv_all[plane, 384:400, :] = run_rows
    q_copies, kv_copies = [], [None]
    own_kv, own_q = r.kv_all.at[plane], r.q_all.at[mine]
    for o in range(1, KG):
        kv_copies.append(
            remote(own_kv, own_kv, r.kv_send.at[o], r.kv_recv.at[o], key_peers[o - 1][1])
        )
    starts(kv_copies[1:])
    arrive(second_w[4:6])
    query = flipped(times(normal_one, r.w_query[...]))[0:D]
    query = turn(query, HEADS, cosine, sine, 1.0).astype(BF).reshape(D, TOK)
    r.q_all[mine, 0:16, :] = run_rows
    r.q_all[mine, 16:QROWS, :] = query * jnp.asarray(0.125, BF)
    for g in range(KV_HEADS):
        rows = pl.ds(16 + 192 * g, 192) if g else pl.ds(0, 208)
        for o in range(1, QG):
            q_copies.append(
                remote(
                    own_q.at[rows], own_q.at[rows], r.q_send.at[o, g], r.q_recv.at[o, g], query_peers[o - 1][1]
                )
            )
    starts(q_copies + first_w[6:])
    one_copy = remote(
        r.one_all.at[OWN], r.one_all.at[LATE], r.sib_send.at[0], r.sib_recv.at[0], sibling
    )
    one_copy.start()
    done += q_copies + kv_copies[1:] + [one_copy]
    prepare_spread(r)
    r.yd_all[:, OWN] = r.grad_out[...]
    yd_copy = remote(
        r.yd_all.at[:, OWN], r.yd_all.at[:, LATE], r.sib_send.at[1], r.sib_recv.at[1], sibling
    )
    yd_copy.start()
    done.append(yd_copy)
    zeros = jnp.zeros((HEAD, QG * TOK), BF)
    o_copies = []

    def o_copy(o, g):
        a, device = query_peers[o - 1]
        rows = pl.ds(pl.multiple_of(g * 192, 64), 192)
        return remote(
            r.o_buf.at[a, rows], r.o_got.at[mine, rows], r.o_send.at[o, g], r.o_recv.at[o, g], device
        )

    for step, rows_of in enumerate(STEPS):
        bases = [((y + 4 - back) % 4) * 4 for back in rows_of]
        for back, base in zip(rows_of, bases):
            arrive([kv_copies[back * 4 + dz] for dz in range(4) if back * 4 + dz])

            def flip(b, unused, base=base):
                flip_keys(r.kv_all, r.kv_tok, base + b)
                return unused

            lax.fori_loop(0, 4, flip, 0)
        last = step == len(STEPS) - 1

        def three(g, unused, step=step, bases=bases, last=last):
            for i in range(3):
                h = g * 3 + i
                first = pl.multiple_of(h * HEAD, HEAD)
                queries = head_rows(r.q_all, h, 16)
                scores = [
                    scores_of(r.q_all, r.kv_all, r.kv_tok, g, base, queries, zeros)[1]
                    for base in bases
                ]
                new_top = jnp.max(scores[0], axis=0, keepdims=True)
                for more in scores[1:]:
                    new_top = jnp.maximum(new_top, jnp.max(more, axis=0, keepdims=True))
                if step:
                    top = r.top_all[pl.ds(h, 1), :]
                    new_top = jnp.maximum(top, new_top)
                value_rows = pl.ds(pl.multiple_of(g * 128 + HEAD, HEAD), HEAD)
                total, accum = None, None
                for base, back, part in zip(bases, rows_of, scores):
                    probs = jnp.exp(part - new_top)
                    values = jnp.concatenate(
                        [r.kv_all[base + b, value_rows, :] for b in range(CHUNK)], axis=1
                    )
                    part_total = jnp.sum(probs, axis=0, keepdims=True)
                    probs = probs.astype(BF)
                    part_accum = times(values, probs)
                    total = part_total if total is None else total + part_total
                    accum = part_accum if accum is None else accum + part_accum
                if step:
                    fade = jnp.exp(top - new_top)
                    total = total + r.total_all[pl.ds(h, 1), :] * fade
                    accum = accum + r.accum_all[pl.ds(first, HEAD), :] * fade
                if not last:
                    r.top_all[pl.ds(h, 1), :] = new_top
                    r.total_all[pl.ds(h, 1), :] = total
                    r.accum_all[pl.ds(first, HEAD), :] = accum
                    continue
                part = (accum / total).astype(BF)
                for a in range(QG):
                    lanes = slice(a * TOK, (a + 1) * TOK)
                    r.o_buf[a, pl.ds(first, HEAD), :] = part[:, lanes]
                    r.ml_buf[a, pl.ds(h, 1), :] = new_top[:, lanes]
                    r.ml_buf[a, pl.ds(h + 16, 1), :] = total[:, lanes]
            return unused

        if step == 0:
            for g in range(KV_HEADS):
                arrive(q_copies[3 * g : 3 * g + 3])
                lax.fori_loop(g, g + 1, three, 0)
            continue
        if not last:
            lax.fori_loop(0, KV_HEADS, three, 0)
            if step == 1:
                for c, d in zip(first_w[6:], second_w[6:]):
                    c.wait_recv()
                    d.start()
            continue

        def three_and_send(g, unused):
            three(g, unused)
            starts([o_copy(o, g) for o in range(1, QG)])
            return unused

        lax.fori_loop(0, KV_HEADS, three_and_send, 0)
    o_copies += [o_copy(o, g) for o in range(1, QG) for g in range(KV_HEADS)]
    for o in range(1, QG):
        a, device = query_peers[o - 1]
        c = remote(r.ml_buf.at[a], r.ml_got.at[mine], r.ml_send.at[o], r.ml_recv.at[o], device)
        c.start()
        o_copies.append(c)
    done += o_copies
    r.o_got[mine] = r.o_buf[mine]
    r.ml_got[mine] = r.ml_buf[mine]
    for c in own_w[3:]:
        c.wait()
    arrive(second_w[6:])
    arrive(o_copies)
    r.st_own[...] = jnp.zeros_like(r.st_own)
    for h in range(HEADS):
        tops = [r.ml_got[a, pl.ds(h, 1), :] for a in range(QG)]
        best = jnp.maximum(jnp.maximum(tops[0], tops[1]), jnp.maximum(tops[2], tops[3]))
        shares = [r.ml_got[a, pl.ds(h + 16, 1), :] * jnp.exp(tops[a] - best) for a in range(QG)]
        whole = shares[0] + shares[1] + shares[2] + shares[3]
        r.st_own[pl.ds(h, 1), :] = best + jnp.log(whole)
        result = jnp.zeros((HEAD, TOK), F32)
        for a in range(QG):
            result = result + r.o_got[a, pl.ds(h * HEAD, HEAD), :].astype(F32) * (shares[a] / whole)
        r.o_rows[pl.ds(h * HEAD, HEAD), :] = result
    def to_sibling(src, dst, at):
        c = remote(src, dst, r.sib_send.at[at], r.sib_recv.at[at], sibling)
        c.start()
        done.append(c)
        return c

    attended = r.o_rows[...].T.astype(BF)
    r.att_all[OWN, D:WIDE] = jnp.zeros((TOK, WIDE - D), BF)
    r.att_all[OWN, 0:D] = attended
    att_copy = to_sibling(r.att_all.at[OWN], r.att_all.at[LATE], 2)
    gain = r.gains[1:2, 0:D]
    grad_low = r.grad_out[...].astype(F32).T.astype(BF)
    middle = r.hidden[...].astype(F32).T + times(attended, r.w_out[...])
    scale = lax.rsqrt(jnp.mean(middle * middle, axis=-1, keepdims=True) + eps)
    unit = middle * scale
    normal = (unit * gain).astype(BF)
    r.nrm_all[OWN, D:WIDE] = jnp.zeros((TOK, WIDE - D), BF)
    r.nrm_all[OWN, 0:D] = normal
    nrm_copy = to_sibling(r.nrm_all.at[OWN], r.nrm_all.at[LATE], 3)
    gate = times(normal, r.w_gate[...])
    upper = times(normal, r.w_up[...])
    sigma = 1.0 / (1.0 + jnp.exp(-gate))
    silu = gate * sigma
    inner = (silu * upper).astype(BF)
    for c in range(2):
        for d in range(2):
            first = 768 * d + QUARTER * c
            r.in_parts[c, :, QUARTER * d : QUARTER * (d + 1)] = inner[:, first : first + QUARTER]
    in_copy = to_sibling(r.in_parts.at[1 - core], r.in_all.at[LATE], 4)
    r.in_all[OWN, :] = r.in_parts[core]
    grad_inner = times(grad_low, r.w_down[...])
    grad_gate = (grad_inner * upper * sigma * (1.0 + gate * (1.0 - sigma))).astype(BF)
    grad_up = (grad_inner * silu).astype(BF)
    gate_flat = grad_gate.astype(F32).T.astype(BF)
    up_flat = grad_up.astype(F32).T.astype(BF)
    for c in range(2):
        r.yg_parts[c, 0:768, :] = gate_flat[768 * c : 768 * (c + 1)]
        r.yg_parts[c, 768:1536, :] = up_flat[768 * c : 768 * (c + 1)]
    yg_copy = to_sibling(r.yg_parts.at[1 - core], r.yg_all.at[:, LATE], 5)
    r.yg_all[:, OWN] = r.yg_parts[core]
    grad_normal = across(grad_gate, r.w_gate[...]) + across(grad_up, r.w_up[...])
    r.gn_own[...] = jnp.zeros_like(r.gn_own)
    r.gn_own[1:2, 0:D] = jnp.sum(grad_normal * unit, axis=0, keepdims=True)
    grad_unit = grad_normal * gain
    back = (
        scale * (grad_unit - unit * jnp.mean(grad_unit * unit, axis=-1, keepdims=True))
        + grad_low.astype(F32)
    )
    branch = back.astype(BF)
    grads_low = across(r.w_out[...], branch).astype(BF)
    r.do_all[mine] = grads_low
    for h in range(HEADS):
        rows = slice(h * HEAD, (h + 1) * HEAD)
        r.st_own[16 + h : 17 + h, :] = jnp.sum(
            grads_low[rows].astype(F32) * r.o_rows[rows, :], axis=0, keepdims=True
        )
    r.st_all[mine] = r.st_own[...]
    st_copies = []
    own_do, own_st = r.do_all.at[mine], r.st_all.at[mine]
    for o in range(1, QG):
        device = query_peers[o - 1][1]
        st_copies.append(remote(own_st, own_st, r.st_send.at[o], r.st_recv.at[o], device))

    def do_copy(o, g):
        rows = own_do.at[pl.ds(pl.multiple_of(g * 192, 64), 192)]
        return remote(rows, rows, r.do_send.at[o, g], r.do_recv.at[o, g], query_peers[o - 1][1])

    starts(st_copies)
    for g in range(KV_HEADS):
        starts([do_copy(o, g) for o in range(1, QG)])
    done += st_copies + [do_copy(o, g) for o in range(1, QG) for g in range(KV_HEADS)]
    o_part = across(r.spread_one[...], branch).astype(BF)
    r.yo_parts[0] = o_part[0:512]
    r.yo_parts[1] = o_part[512:1024]
    yo_copy = to_sibling(r.yo_parts.at[1 - core], r.yo_all.at[:, LATE], 6)
    r.yo_all[:, OWN] = r.yo_parts[core]
    r.back[...] = flipped(back)[0:D]
    arrive([nrm_copy, yg_copy])
    gate_part = times(r.yg_all[0:768, :], r.nrm_all[...]).astype(BF).reshape(KG, 48, WIDE)
    up_part = times(r.yg_all[768:1536, :], r.nrm_all[...]).astype(BF).reshape(KG, 48, WIDE)
    for j in range(KG):
        r.g1[j // 4, j % 4, 32:64, :] = gate_part[j, 0:32]
        r.g2[j % 4, j // 4, 0:16, :] = gate_part[j, 32:48]
        r.g2[j % 4, j // 4, 16:64, :] = up_part[j]
    a_sends, b_sends, p_sends = [], [], []
    for i in range(1, 4):
        y_to, z_to = (y + i) % 4, (z + i) % 4
        along_y = (dp, ctx_of(x_hi, y_to * 4 + z, core))
        along_z = (dp, ctx_of(x_hi, y * 4 + z_to, core))
        a_sends.append(
            remote(r.g1.at[y_to], r.r1.at[y], r.a_send.at[0, i], r.a_recv.at[0, i], along_y)
        )
        a_sends.append(
            remote(r.g2.at[z_to], r.r2.at[z], r.a_send.at[1, i], r.a_recv.at[1, i], along_z)
        )
        b_sends.append(
            remote(r.s1.at[z_to], r.t1.at[z], r.b_send.at[0, i], r.b_recv.at[0, i], along_z)
        )
        b_sends.append(
            remote(r.s2.at[y_to], r.t2.at[y], r.b_send.at[1, i], r.b_recv.at[1, i], along_y)
        )
    starts(a_sends[1::2])
    arrive([att_copy, yo_copy])
    out_part = times(r.yo_all[...], r.att_all[...]).astype(BF).reshape(KG, 32, WIDE)
    for j in range(KG):
        r.g1[j // 4, j % 4, 0:32, :] = out_part[j]
    starts(a_sends[0::2])
    arrive([yd_copy, in_copy])
    part = times(r.yd_all[...], r.in_all[...]).astype(BF)
    for x in range(2):
        for d in range(2):
            r.gd[x, d] = part[288 * x : 288 * (x + 1), QUARTER * d : QUARTER * (d + 1)]
    d_sends = []
    for i, (d, x, device) in enumerate(line):
        d_sends.append(remote(r.gd.at[x, d], r.rd.at[slot], r.d_send.at[i], r.d_recv.at[i], device))
    starts(d_sends)
    r.rd[slot] = r.gd[x_hi, dp]
    r.r1[y] = r.g1[y]
    r.r2[z] = r.g2[z]
    for o in range(1, KG):
        j, device = key_peers[o - 1]
        p_sends.append(
            remote(r.gp.at[j], r.rp.at[plane], r.p_send.at[o], r.p_recv.at[o], device)
        )
    done += d_sends + a_sends + b_sends + p_sends
    arrive(st_copies)

    def dkv_copy(o, g):
        j, device = key_peers[o - 1]
        rows = pl.ds(pl.multiple_of(g * 128, 128), 128)
        return remote(
            r.dkv_buf.at[j, rows], r.dkv_got.at[plane, rows], r.dkv_send.at[o, g], r.dkv_recv.at[o, g], device
        )

    def dq_copy(o, g):
        a, device = query_peers[o - 1]
        rows = pl.ds(pl.multiple_of(g * 192, 64), 192)
        return remote(
            r.dq_buf.at[a, rows], r.dq_got.at[mine, rows], r.dq_send.at[o, g], r.dq_recv.at[o, g], device
        )

    def key_head(g, unused):
        arrive([do_copy(o, g) for o in range(1, QG)])
        for c in (1, 2, 3, 0):
            base = ((y + c) % 4) * 4
            key_term, value_term = None, None
            for i in range(3):
                h = g * 3 + i
                queries = head_rows(r.q_all, h, 16)
                grads = head_rows(r.do_all, h)
                lse = jnp.concatenate([r.st_all[a, pl.ds(h, 1), :] for a in range(QG)], axis=1)
                delta = jnp.concatenate([r.st_all[a, pl.ds(h + 16, 1), :] for a in range(QG)], axis=1)
                keys, scores = scores_of(r.q_all, r.kv_all, r.kv_tok, g, base, queries, zeros)
                probs = jnp.exp(scores - lse)
                grad_probs = times(keys, jnp.concatenate([zeros, grads], axis=0))
                grad_scores = (probs * (grad_probs - delta)).astype(BF)
                key_rows = pl.ds(pl.multiple_of(g * 128, 128), HEAD)
                flat_keys = jnp.concatenate(
                    [r.kv_all[base + b, key_rows, :] for b in range(CHUNK)], axis=1
                )
                part = times(flat_keys, grad_scores)
                rows = slice(i * HEAD, (i + 1) * HEAD)
                r.dq_acc[rows, :] = part if c == 1 else r.dq_acc[rows, :] + part
                key_part = across(queries, grad_scores)
                value_part = across(grads, probs.astype(BF))
                key_term = key_part if key_term is None else key_term + key_part
                value_term = value_part if value_term is None else value_term + value_part
            first = pl.multiple_of(g * 128, 128)
            for b in range(CHUNK):
                lanes = slice(b * TOK, (b + 1) * TOK)
                r.dkv_buf[base + b, pl.ds(first, HEAD), :] = key_term[:, lanes].astype(BF)
                r.dkv_buf[base + b, pl.ds(pl.multiple_of(first + HEAD, HEAD), HEAD), :] = (
                    value_term[:, lanes].astype(BF)
                )
            starts([dkv_copy(c * 4 + dz, g) for dz in range(4) if c * 4 + dz])
        rows = pl.ds(pl.multiple_of(g * 192, 64), 192)
        for a in range(QG):
            r.dq_buf[a, rows, :] = r.dq_acc[:, a * TOK : (a + 1) * TOK].astype(BF)
        starts([dq_copy(o, g) for o in range(1, QG)])

        return unused

    lax.fori_loop(0, KV_HEADS, key_head, 0)
    sends = [dkv_copy(o, g) for o in range(1, KG) for g in range(KV_HEADS)]
    sends += [dq_copy(o, g) for o in range(1, QG) for g in range(KV_HEADS)]
    r.dq_got[mine] = r.dq_buf[mine]
    r.dkv_got[plane] = r.dkv_buf[plane]
    arrive(a_sends)
    for i in range(4):
        for pieces, sums in ((r.r1, r.s1), (r.r2, r.s2)):
            total = pieces[0, i].astype(F32)
            for j in range(1, 4):
                total = total + pieces[j, i].astype(F32)
            sums[i] = total.astype(BF)
    starts(b_sends)
    arrive(d_sends)
    total = sum_pieces(r.rd, 4, slice(None)).astype(BF)
    r.gp[...] = times(r.spread_one[0:512, 0:288], total).astype(BF).reshape(KG, 32, QUARTER)
    r.rp[plane] = r.gp[plane]
    r.t1[z] = r.s1[z]
    r.t2[y] = r.s2[y]
    collector = core == x_hi

    def toward(target_dp, src, dst, send, recv):
        device = (target_dp, ctx_of(core, plane, core))
        lanes = pl.ds(pl.multiple_of(target_dp * 256, 128), QUARTER)
        return remote(src.at[:, lanes], dst.at[slot], send.at[target_dp], recv.at[slot], device)

    def pass_on(src, dst, send, recv):
        for target_dp in range(2):
            here = jnp.logical_and(collector, dp == target_dp)

            @pl.when(jnp.logical_not(here))
            def _():
                toward(target_dp, src, dst, send, recv).start()

            @pl.when(here)
            def _():
                dst[slot] = src[:, target_dp * 256 : target_dp * 256 + QUARTER]

    arrive(sends)
    done += sends
    cosine, sine = r.tables[0], r.tables[1]
    total = r.dq_got[0].astype(F32)
    for a in range(1, QG):
        total = total + r.dq_got[a].astype(F32)
    dq = turn(total * 0.125, HEADS, cosine, sine, -1.0).astype(BF).reshape(D, TOK)
    total = r.dkv_got[0].astype(F32)
    for j in range(1, KG):
        total = total + r.dkv_got[j].astype(F32)
    total = total.reshape(KV_HEADS, 2, HEAD, TOK)
    dk = turn(total[:, 0], KV_HEADS, cosine, sine, -1.0).astype(BF).reshape(192, TOK)
    dv = total[:, 1].astype(BF).reshape(192, TOK)
    placed = times(r.spread[...], jnp.concatenate([dq, dk, dv], axis=0)).astype(BF)
    r.yq_parts[0] = placed[0:512]
    r.yq_parts[1] = placed[512:1024]
    yq_copy = to_sibling(r.yq_parts.at[1 - core], r.yq_all.at[:, LATE], 7)
    r.yq_all[:, OWN] = r.yq_parts[core]
    first = times(r.w_query[...], dq) + times(r.w_key[...], dk) + times(r.w_value[...], dv)
    state = r.hidden[...].astype(F32)
    scale = lax.rsqrt(jnp.mean(state * state, axis=0, keepdims=True) + eps)
    unit = state * scale
    terms = jnp.concatenate([first * unit, jnp.zeros((WIDE - D, TOK), F32)], axis=0).T
    r.gn_own[0:1, :] = jnp.sum(terms, axis=0, keepdims=True)
    gn_copy = to_sibling(r.gn_own, r.gn_all, 8)
    grad_unit = first * gain_rows(r.gains[0:1, :])
    r.grad[...] = (
        scale * (grad_unit - unit * jnp.mean(grad_unit * unit, axis=0, keepdims=True))
        + r.back[...]
    )
    arrive([one_copy, yq_copy, gn_copy])
    part = times(r.yq_all[...], r.one_all[...]).reshape(KG, 32, WIDE)
    sums = r.gn_own[...] + r.gn_all[...]
    line_of = lax.broadcasted_iota(jnp.int32, (KG, 32, WIDE), 1)
    part = jnp.where(line_of == 30, sums[0:1][None], part)
    part = jnp.where(line_of == 31, sums[1:2][None], part)
    r.gq[...] = part.astype(BF)
    q_sends = []
    for o in range(1, KG):
        j, device = key_peers[o - 1]
        q_sends.append(
            remote(r.gq.at[j], r.rq.at[plane], r.gq_send.at[o], r.gq_recv.at[o], device)
        )
    starts(q_sends + p_sends)
    done += q_sends
    r.rq[plane] = r.gq[plane]
    r.output[...] = flipped(middle + across(inner, r.w_down[...]))[0:D].astype(BF)
    arrive(b_sends)
    r.sa[0:64, :] = sum_pieces(r.t1, 4, slice(0, 64)).astype(BF)
    r.sa[64:128, :] = sum_pieces(r.t2, 4, slice(0, 64)).astype(BF)
    pass_on(r.sa, r.wa, r.wa_send, r.wa_recv)

    def collect(src, dst, send, recv, rows, at):
        part = r.fa.at[rows]
        passed = remote(part, part, r.f_send.at[at], r.f_recv.at[at], sibling)

        @pl.when(collector)
        def _():
            for source in range(4):

                @pl.when(slot != source)
                def _():
                    remote(
                        src.at[:, pl.ds(0, QUARTER)], dst.at[source], send.at[0], recv.at[source], sibling
                    ).wait_recv()

            part[...] = sum_pieces(dst, 4, slice(None))
            passed.start()

        return passed

    moves = ((r.sa, r.wa, r.wa_send, r.wa_recv), (r.sq, r.wb, r.wb_send, r.wb_recv))
    arrive(q_sends)
    r.sq[...] = sum_pieces(r.rq, KG, slice(0, 32)).astype(BF)
    pass_on(r.sq, r.wb, r.wb_send, r.wb_recv)
    arrive(p_sends)
    r.fd[core] = sum_pieces(r.rp, KG, slice(0, 32))
    final = remote(r.fd.at[core], r.fd.at[core], r.f_send.at[0], r.f_recv.at[0], sibling)
    final.start()
    early = collect(*moves[0], pl.ds(32, GROWS), 1)
    late = collect(*moves[1], pl.ds(0, 32), 2)
    final.wait_recv()
    done.append(final)

    @pl.when(collector)
    def _():
        early.wait_send()
        late.wait_send()

    @pl.when(jnp.logical_not(collector))
    def _():
        early.wait_recv()
        late.wait_recv()

    for target_dp in range(2):

        @pl.when(jnp.logical_not(jnp.logical_and(collector, dp == target_dp)))
        def _():
            for move in moves:
                toward(target_dp, *move).wait_send()

    for c in done:
        c.wait_send()


INPUTS = (
    "hidden",
    "positions",
    "run_cos",
    "run_sin",
    "in_cos",
    "in_sin",
    "gain_a",
    "gain_f",
    "grad_out",
    "s_key",
    "s_value",
    "s_query",
    "s_out",
    "s_gate",
    "s_up",
    "s_down",
)
OUTPUTS = (
    ("output", (D, TOK), BF),
    ("grad", (D, TOK), F32),
    ("fa", (AROWS, QUARTER), F32),
    ("fd", (2, 32, QUARTER), F32),
)
SCRATCH = (
    ("gain_own", (8, WIDE), F32),
    ("gain_got", (8, WIDE), F32),
    ("gains", (8, WIDE), F32),
    ("tables", (2, HEAD // 2, TOK), F32),
    ("w_key", (D, 192), BF),
    ("w_value", (D, 192), BF),
    ("w_query", (D, D), BF),
    ("w_out", (D, D), BF),
    ("w_gate", (D, FF), BF),
    ("w_up", (D, FF), BF),
    ("w_down", (D, FF), BF),
    ("q_all", (QG, QROWS, TOK), BF),
    ("kv_all", (KG, KROWS, TOK), BF),
    ("kv_tok", (KV_HEADS, KG * TOK, 128), BF),
    ("accum_all", (D, QG * TOK), F32),
    ("top_all", (16, QG * TOK), F32),
    ("total_all", (16, QG * TOK), F32),
    ("o_buf", (QG, D, TOK), BF),
    ("o_got", (QG, D, TOK), BF),
    ("ml_buf", (QG, 32, TOK), F32),
    ("ml_got", (QG, 32, TOK), F32),
    ("o_rows", (D, TOK), F32),
    ("st_own", (32, TOK), F32),
    ("st_all", (QG, 32, TOK), F32),
    ("do_all", (QG, D, TOK), BF),
    ("spread_one", (1024, D), BF),
    ("spread", (1024, 960), BF),
    ("one_all", (2 * TOK, WIDE), BF),
    ("att_all", (2 * TOK, WIDE), BF),
    ("nrm_all", (2 * TOK, WIDE), BF),
    ("in_parts", (2, TOK, 2 * QUARTER), BF),
    ("in_all", (2 * TOK, 2 * QUARTER), BF),
    ("yd_all", (D, 2 * TOK), BF),
    ("yg_parts", (2, 1536, TOK), BF),
    ("yg_all", (1536, 2 * TOK), BF),
    ("yo_parts", (2, 512, TOK), BF),
    ("yo_all", (512, 2 * TOK), BF),
    ("yq_parts", (2, 512, TOK), BF),
    ("yq_all", (512, 2 * TOK), BF),
    ("gn_own", (8, WIDE), F32),
    ("gn_all", (8, WIDE), F32),
    ("back", (D, TOK), F32),
    ("gd", (2, 2, 288, QUARTER), BF),
    ("rd", (4, 288, QUARTER), BF),
    ("gp", (KG, 32, QUARTER), BF),
    ("rp", (KG, 32, QUARTER), BF),
    ("g1", (4, 4, 64, WIDE), BF),
    ("g2", (4, 4, 64, WIDE), BF),
    ("r1", (4, 4, 64, WIDE), BF),
    ("r2", (4, 4, 64, WIDE), BF),
    ("s1", (4, 64, WIDE), BF),
    ("s2", (4, 64, WIDE), BF),
    ("t1", (4, 64, WIDE), BF),
    ("t2", (4, 64, WIDE), BF),
    ("sa", (GROWS, WIDE), BF),
    ("gq", (KG, 32, WIDE), BF),
    ("rq", (KG, 32, WIDE), BF),
    ("sq", (32, WIDE), BF),
    ("wa", (4, GROWS, QUARTER), BF),
    ("wb", (4, 32, QUARTER), BF),
    ("dq_acc", (192, QG * TOK), F32),
    ("dq_buf", (QG, D, TOK), BF),
    ("dq_got", (QG, D, TOK), BF),
    ("dkv_buf", (KG, 384, TOK), BF),
    ("dkv_got", (KG, 384, TOK), BF),
)
SEMAPHORES = (
    ("w_own", (7,)),
    ("w_send", (7, 2)),
    ("w_recv", (7, 2)),
    ("w_core_send", (7, 2)),
    ("w_core_recv", (7, 2)),
    ("gain_send", (1,)),
    ("gain_recv", (1,)),
    ("q_send", (QG, KV_HEADS)),
    ("q_recv", (QG, KV_HEADS)),
    ("kv_send", (KG,)),
    ("kv_recv", (KG,)),
    ("o_send", (QG, KV_HEADS)),
    ("o_recv", (QG, KV_HEADS)),
    ("ml_send", (QG,)),
    ("ml_recv", (QG,)),
    ("sib_send", (9,)),
    ("sib_recv", (9,)),
    ("do_send", (QG, KV_HEADS)),
    ("do_recv", (QG, KV_HEADS)),
    ("st_send", (QG,)),
    ("st_recv", (QG,)),
    ("d_send", (3,)),
    ("d_recv", (3,)),
    ("a_send", (2, 4)),
    ("a_recv", (2, 4)),
    ("b_send", (2, 4)),
    ("b_recv", (2, 4)),
    ("p_send", (KG,)),
    ("p_recv", (KG,)),
    ("dkv_send", (KG, KV_HEADS)),
    ("dkv_recv", (KG, KV_HEADS)),
    ("dq_send", (QG, KV_HEADS)),
    ("dq_recv", (QG, KV_HEADS)),
    ("f_send", (3,)),
    ("f_recv", (3,)),
    ("gq_send", (KG,)),
    ("gq_recv", (KG,)),
    ("wa_send", (2,)),
    ("wa_recv", (4,)),
    ("wb_send", (2,)),
    ("wb_recv", (4,)),
)
NAMES = (
    list(INPUTS)
    + [name for name, _, _ in OUTPUTS]
    + [name for name, _, _ in SCRATCH]
    + [name for name, _ in SEMAPHORES]
)


def layer(hidden, positions, gain_attn, gain_ffn, grad_out, shards):
    freqs = rope_base ** (-(np.arange(HEAD // 2, dtype=np.float64) * 2.0 / HEAD))[:, None]
    runs = freqs * (np.arange(64, dtype=np.float64) * TOK)[None]
    inside = freqs * np.arange(TOK, dtype=np.float64)[None]
    tables = [f(a).astype(np.float32) for a in (runs, inside) for f in (np.cos, np.sin)]
    return pl.pallas_call(
        layer_kernel,
        out_shape=[jax.ShapeDtypeStruct(shape, kind) for _, shape, kind in OUTPUTS],
        in_specs=[VM] * 9 + [ANY] * 7,
        out_specs=[VM] * len(OUTPUTS),
        scratch_shapes=[pltpu.VMEM(shape, kind) for _, shape, kind in SCRATCH]
        + [pltpu.SemaphoreType.DMA(shape) for _, shape in SEMAPHORES],
        compiler_params=params(1),
    )(hidden, positions, *[jnp.asarray(t) for t in tables], gain_attn, gain_ffn, grad_out, *shards)


def finish_kernel(fa, fd, grad, result, *outs):
    core = lax.axis_index("ctx") % 2
    dp = lax.axis_index("dp")
    rows = jnp.where(dp == 0, fa[...], pltpu.roll(fa[...], QUARTER - 32, 1))[:, 0:288]
    down = jnp.concatenate([fd[0], fd[1]], axis=1)
    for out, count, block, at in zip(
        outs[:7], (9, 3, 3, 9, 24, 24, 9), (rows,) * 6 + (down,), (0, 18, 24, 32, 64, 112, 0)
    ):
        part = jnp.where(core == 0, block[at : at + count], block[at + count : at + 2 * count])
        if count == 24:
            out[0] = part
        else:
            for i in range(count):
                out[i] = part[i : i + 1]
    outs[7][...] = rows[30:31]
    outs[8][...] = rows[31:32]
    outs[9][...] = grad[...]
    outs[10][...] = result[...]


def finish(fa, fd, grad, result):
    shape = jax.ShapeDtypeStruct
    return pl.pallas_call(
        finish_kernel,
        out_shape=[
            shape((9, 1, 288), F32),
            shape((3, 1, 288), F32),
            shape((3, 1, 288), F32),
            shape((9, 1, 288), F32),
            shape((1, 24, 288), F32),
            shape((1, 24, 288), F32),
            shape((9, 1, 768), F32),
            shape((1, 288), F32),
            shape((1, 288), F32),
            shape((D, TOK), F32),
            shape((D, TOK), BF),
        ],
        in_specs=[VM] * 4,
        out_specs=[VM] * 11,
    )(fa, fd, grad, result)


def local(
    hidden, positions, w_query, w_key, w_value, w_out, w_gate, w_up, w_down,
    gain_attn, gain_ffn, grad_out,
):
    output, grad_input, fa, fd = layer(
        hidden[0].T,
        positions,
        gain_attn,
        gain_ffn,
        grad_out[0].T,
        [w[0] for w in (w_key, w_value, w_query, w_out, w_gate, w_up)] + [w_down[0].T],
    )
    *grads, gain_one, gain_two, grad_input, output = finish(fa, fd, grad_input, output)
    columns = [
        g.transpose(0, 2, 1) if g.shape[0] == 1 else g.transpose(1, 2, 0) for g in grads
    ]
    return (output.T[None], grad_input.T[None]) + tuple(columns) + (gain_one, gain_two)


def solution(mesh):
    in_specs = (
        P("dp", "ctx", None),
        P("dp", "ctx"),
    ) + (P(None, "dp", None),) * 7 + (
        P(None, "dp"),
        P(None, "dp"),
        P("dp", "ctx", None),
    )
    out_specs = (
        P("dp", "ctx", None),
        P("dp", "ctx", None),
    ) + (P(None, "dp", "ctx"),) * 7 + (
        P(None, "dp"),
        P(None, "dp"),
    )
    return jax.shard_map(local, mesh=mesh, in_specs=in_specs, out_specs=out_specs, check_vma=False)
```
